32 devices in a mesh: seq: 16 (over z, x, core), bkt: 2 (over y).
Axes of the slice: x: 2, y: 2, z: 4, core: 2. Of those that a mesh axis runs over, the one named last changes fastest.
Arguments:
- tokens: bfloat16 [2, 4, 1024, 768], P('bkt', None, 'seq'), may hold values from -6 to 6
- first_values: bfloat16 [2, 4, 1024, 384], P('bkt', None, 'seq'), may hold values from -6 to 6
- lengths: int32 [2, 4], P('bkt'), may hold values from 512 to 1024, as said below
- cotangent: bfloat16 [2, 4, 1024, 768], P('bkt', None, 'seq'), may hold values from -6 to 6
- first_gain: bfloat16 [768], P('seq'), may hold values from 0.5 to 1.5
- first_shift: bfloat16 [768], P('seq'), may hold values from -2 to 2
- query_weight: bfloat16 [768, 768], P('seq', 'bkt'), may hold values from -0.21875 to 0.21875
- query_bias: bfloat16 [768], P('seq'), may hold values from -2 to 2
- key_weight: bfloat16 [768, 768], P('seq', 'bkt'), may hold values from -0.21875 to 0.21875
- value_weight: bfloat16 [768, 384], P('seq', 'bkt'), may hold values from -0.21875 to 0.21875
- value_bias: bfloat16 [384], P('seq'), may hold values from -2 to 2
- output_weight: bfloat16 [768, 768], P('seq', 'bkt'), may hold values from -3.5 to 3.5
- output_bias: bfloat16 [768], P('seq'), may hold values from -2 to 2
- second_gain: bfloat16 [768], P('seq'), may hold values from 0.5 to 1.5
- second_shift: bfloat16 [768], P('seq'), may hold values from -2 to 2
- expand_weight: bfloat16 [768, 3072], P('seq', 'bkt'), may hold values from -0.21875 to 0.21875
- expand_bias: bfloat16 [3072], P('seq'), may hold values from -2 to 2
- reduce_weight: bfloat16 [3072, 768], P('seq', 'bkt'), may hold values from -0.109375 to 0.109375
- reduce_bias: bfloat16 [768], P('seq'), may hold values from -2 to 2
Outputs:
- mixed: bfloat16 [2, 4, 1024, 768], P('bkt', None, 'seq')
- grad_tokens: bfloat16 [2, 4, 1024, 768], P('bkt', None, 'seq')
- grad_first: bfloat16 [2, 4, 1024, 384], P('bkt', None, 'seq')
- first_gain_grad: float32 [768], P('seq')
- first_shift_grad: float32 [768], P('seq')
- query_weight_grad: float32 [768, 768], P('seq', 'bkt')
- query_bias_grad: float32 [768], P('seq')
- key_weight_grad: float32 [768, 768], P('seq', 'bkt')
- value_weight_grad: float32 [768, 384], P('seq', 'bkt')
- value_bias_grad: float32 [384], P('seq')
- output_weight_grad: float32 [768, 768], P('seq', 'bkt')
- output_bias_grad: float32 [768], P('seq')
- second_gain_grad: float32 [768], P('seq')
- second_shift_grad: float32 [768], P('seq')
- expand_weight_grad: float32 [768, 3072], P('seq', 'bkt')
- expand_bias_grad: float32 [3072], P('seq')
- reduce_weight_grad: float32 [3072, 768], P('seq', 'bkt')
- reduce_bias_grad: float32 [768], P('seq')
The draws below stay inside these ranges and needn't reach their ends.
Inputs may be any that keep to these rules, and one draw needn't show every extreme that they name: `lengths`: each bucket holds one sequence of exactly 1024 tokens, which one drawn from the seed.
All inputs are finite; a program needn't handle non-finite values.
Results may differ from the reference program's by a relative error of at most 0.025.
Values may be sent and summed in bfloat16 or wider, within the bound.
No kernel may reach another device: no remote copies, remote signals or barrier semaphores. Data moves between devices by JAX's collectives and lax.ppermute only.
A program may use at most 128 MiB of HBM per device.

```python
import jax
import jax.numpy as jnp
from jax import lax

D = 768
H = 12
HD = 64
FF = 3072
SEQS = 4
DV = 384
LPAD = 1024
BUCKETS = 2


def draw_lengths(key, part):
    key = jax.random.fold_in(key, 11)
    keys = jax.random.split(key, 4)
    half = LPAD // 2
    shape = (BUCKETS, SEQS)
    shorter = jnp.minimum(jax.random.randint(keys[0], shape, 0, half + 1), jax.random.randint(keys[1], shape, 0, half + 1))
    shorter = jnp.minimum(shorter, jax.random.randint(keys[2], shape, 0, half + 1))
    longest = jax.random.randint(keys[3], (BUCKETS, 1), 0, SEQS)
    column = lax.broadcasted_iota(jnp.int32, shape, 1)
    return jnp.where(column == longest, LPAD, half + shorter).astype(jnp.int32)


def block_levels(stream_key, dims, pieces, smallest, top_value):
    def one(dim, blocks):
        heights = jax.random.uniform(jax.random.fold_in(jax.random.fold_in(stream_key, 6), dim), (blocks,), jnp.float32, smallest / len(pieces), top_value / len(pieces))
        return jnp.repeat(jnp.exp(heights), dims[dim] // blocks).reshape((-1,) + (1,) * (len(dims) - dim - 1))

    loudness = one(*pieces[0])
    for cut in pieces[1:]:
        loudness = loudness * one(*cut)
    return loudness


def gaussian(key, dims, scale, reach, pieces=(), kind=jnp.bfloat16):
    values = jax.random.normal(key, dims, jnp.float32) * scale
    if len(pieces) > 0:
        values = block_levels(key, dims, pieces, -0.22, 0.18) * values
    return jnp.clip(values, min=-reach, max=reach).astype(kind)


def setup_inputs(seed: int = 0) -> dict:
    arg_keys = jax.random.split(jax.random.key(seed), 20)
    return {
        "tokens": gaussian(arg_keys[0], (BUCKETS, SEQS, LPAD, D), 1.0, 6.0, ((0, 2), (2, 16))),
        "first_values": gaussian(arg_keys[1], (BUCKETS, SEQS, LPAD, DV), 1.0, 6.0, ((0, 2), (2, 16))),
        "lengths": draw_lengths(jax.random.fold_in(arg_keys[19], 71), 0),
        "cotangent": gaussian(arg_keys[3], (BUCKETS, SEQS, LPAD, D), 1.0, 6.0, ((0, 2), (2, 16))),
        "first_gain": jnp.clip(1.0 + 0.1 * jax.random.normal(arg_keys[4], (D,), jnp.float32), 0.5, 1.5).astype(jnp.bfloat16),
        "first_shift": gaussian(arg_keys[5], (D,), 0.3, 2.0, ((0, 16),)),
        "query_weight": gaussian(arg_keys[6], (D, D), D ** -0.5, 0.21875, ((0, 16), (1, 2))),
        "query_bias": gaussian(arg_keys[7], (D,), 0.3, 2.0, ((0, 16),)),
        "key_weight": gaussian(arg_keys[8], (D, D), D ** -0.5, 0.21875, ((0, 16), (1, 2))),
        "value_weight": gaussian(arg_keys[9], (D, DV), D ** -0.5, 0.21875, ((0, 16), (1, 2))),
        "value_bias": gaussian(arg_keys[10], (DV,), 0.3, 2.0, ((0, 16),)),
        "output_weight": gaussian(arg_keys[11], (D, D), (max(1, 4 * D // LPAD)) ** -0.5, 3.5, ((0, 16), (1, 2))),
        "output_bias": gaussian(arg_keys[12], (D,), 0.3, 2.0, ((0, 16),)),
        "second_gain": jnp.clip(1.0 + 0.1 * jax.random.normal(arg_keys[13], (D,), jnp.float32), 0.5, 1.5).astype(jnp.bfloat16),
        "second_shift": gaussian(arg_keys[14], (D,), 0.3, 2.0, ((0, 16),)),
        "expand_weight": gaussian(arg_keys[15], (D, FF), D ** -0.5, 0.21875, ((0, 16), (1, 2))),
        "expand_bias": gaussian(arg_keys[16], (FF,), 0.3, 2.0, ((0, 16),)),
        "reduce_weight": gaussian(arg_keys[17], (FF, D), FF ** -0.5, 0.109375, ((0, 16), (1, 2))),
        "reduce_bias": gaussian(arg_keys[18], (D,), 0.3, 2.0, ((0, 16),)),
    }


@jax.custom_vjp
def low(v):
    return lax.optimization_barrier(v.astype(jnp.bfloat16)).astype(jnp.float32)

@jax.custom_vjp
def low_back(v):
    return v

def low_keep(v):
    return (low(v), None)

def low_pass(kept, grad):
    return (grad,)

def back_keep(v):
    return (v, None)

def back_low(kept, grad):
    return (low(grad),)
low.defvjp(low_keep, low_pass)
low_back.defvjp(back_keep, back_low)

def norm_rows(values, gain, shift):
    centre = values - lax.optimization_barrier(jnp.mean(values, -1, keepdims=True))
    spread = lax.optimization_barrier(jnp.mean(centre * centre, -1, keepdims=True))
    return centre * lax.rsqrt(spread + 1e-05) * gain + shift

def product(left, right):
    return jnp.dot(left, right, precision=lax.Precision.HIGHEST, preferred_element_type=jnp.float32)

def one_sequence(rows_in, first_rows, length, params):
    first_gain, first_shift, query_weight, query_bias, key_weight, value_weight, value_bias, output_weight, output_bias, second_gain, second_shift, expand_weight, expand_bias, reduce_weight, reduce_bias = params
    count = rows_in.shape[0]
    normed = low(norm_rows(rows_in, first_gain, first_shift))
    query = low(low_back(product(normed, query_weight) + query_bias)).reshape(count, H, HD)
    keys = low(low_back(product(normed, key_weight))).reshape(count, H, HD)
    fresh = low(low_back(product(normed, value_weight) + value_bias)).reshape(count, H // 2, HD)
    values = jnp.concatenate([fresh, first_rows.reshape(count, H // 2, HD)], 1)
    scores = jnp.einsum('qhd,khd->hqk', query, keys, precision=lax.Precision.HIGHEST, preferred_element_type=jnp.float32) * HD ** (-0.5)
    scores = low_back(scores)
    position = lax.iota(jnp.int32, count)
    allowed = (position[None, :] <= position[:, None]) & (position[None, :] < length)
    probs = low(jax.nn.softmax(jnp.where(allowed[None], scores, -1e+30), axis=-1))
    attended = jnp.einsum('hqk,khd->qhd', probs, values, precision=lax.Precision.HIGHEST, preferred_element_type=jnp.float32).reshape(count, D)
    attended = low(low_back(attended))
    branch = low_back(product(attended, output_weight) + output_bias)
    middle = rows_in + branch
    second = low(norm_rows(middle, second_gain, second_shift))
    hidden = low_back(product(second, expand_weight) + expand_bias)
    active = low(jax.nn.gelu(hidden, approximate=True))
    return middle + product(active, reduce_weight) + reduce_bias

def reference(tokens, first_values, lengths, cotangent, first_gain, first_shift, query_weight, query_bias, key_weight, value_weight, value_bias, output_weight, output_bias, second_gain, second_shift, expand_weight, expand_bias, reduce_weight, reduce_bias):
    params = (first_gain.astype(jnp.float32), first_shift.astype(jnp.float32), query_weight.astype(jnp.float32), query_bias.astype(jnp.float32), key_weight.astype(jnp.float32), value_weight.astype(jnp.float32), value_bias.astype(jnp.float32), output_weight.astype(jnp.float32), output_bias.astype(jnp.float32), second_gain.astype(jnp.float32), second_shift.astype(jnp.float32), expand_weight.astype(jnp.float32), expand_bias.astype(jnp.float32), reduce_weight.astype(jnp.float32), reduce_bias.astype(jnp.float32))
    flat_tokens = tokens.astype(jnp.float32).reshape(BUCKETS * SEQS, LPAD, D)
    flat_first = first_values.astype(jnp.float32).reshape(BUCKETS * SEQS, LPAD, DV)
    flat_length = lengths.reshape(BUCKETS * SEQS).astype(jnp.int32)

    def forward(all_tokens, all_first, weights):

        def per_sequence(item):
            return one_sequence(item[0], item[1], item[2], weights)
        return lax.map(jax.checkpoint(per_sequence), (all_tokens, all_first, flat_length))
    result, pullback = jax.vjp(forward, flat_tokens, flat_first, params)
    valid = lax.iota(jnp.int32, LPAD)[None, :] < flat_length[:, None]
    upstream = jnp.where(valid[:, :, None], cotangent.astype(jnp.float32).reshape(BUCKETS * SEQS, LPAD, D), 0.0)
    tokens_grad, first_grad, grads = pullback(upstream)
    return (result.astype(jnp.bfloat16).reshape(BUCKETS, SEQS, LPAD, D), tokens_grad.astype(jnp.bfloat16).reshape(BUCKETS, SEQS, LPAD, D), first_grad.astype(jnp.bfloat16).reshape(BUCKETS, SEQS, LPAD, DV), grads[0], grads[1], grads[2], grads[3], grads[4], grads[5], grads[6], grads[7], grads[8], grads[9], grads[10], grads[11], grads[12], grads[13], grads[14])
```

```python
import jax
import jax.numpy as jnp
from jax import lax
from jax.sharding import Mesh, PartitionSpec as P

D = 768
H = 12
HD = 64
FF = 3072
DV = 384
GROUP = 4
HG = D // GROUP

EPS = 1e-05
NEG = -1e30
BF = jnp.bfloat16
F32 = jnp.float32


def gray(k):
    return k ^ (k >> 1)


def swap(value, axis, mask):
    return lax.ppermute(value, axis, [(i, i ^ mask) for i in range(lax.axis_size(axis))])


def relative(blocks, axis):
    n = lax.axis_size(axis)
    if n == 1:
        return blocks
    me = lax.axis_index(axis)
    return jnp.concatenate(
        [lax.dynamic_index_in_dim(blocks, gray(r) ^ me, 0, keepdims=True) for r in range(n)], 0
    )


def absolute(rel, axis):
    n = lax.axis_size(axis)
    if n == 1:
        return rel
    me = lax.axis_index(axis)
    return jnp.concatenate(
        [lax.dynamic_index_in_dim(rel, gray(a ^ me), 0, keepdims=True) for a in range(n)], 0
    )


def gather_relative(value, axis):
    buf = value[None]
    while buf.shape[0] < lax.axis_size(axis):
        buf = jnp.concatenate([buf, swap(buf, axis, gray(buf.shape[0]))], 0)
    return buf


def gather(value, axis):
    return absolute(gather_relative(value, axis), axis)


def scatter_sum(blocks, axis):
    rel = relative(blocks, axis)
    while rel.shape[0] > 1:
        half = rel.shape[0] // 2
        got = swap(rel[half:].astype(BF), axis, gray(half))
        rel = rel[:half].astype(F32) + got.astype(F32)
    return rel[0]


def exchange(blocks, axis):
    n = lax.axis_size(axis)
    rel = relative(blocks, axis)
    bit = 1
    while bit < n:
        shape = rel.shape
        pairs = rel.reshape((n // (2 * bit), 2, bit) + shape[1:])
        got = swap(pairs[:, 1], axis, gray(bit))
        rel = jnp.stack([pairs[:, 0], got], 1).reshape(shape)
        bit *= 2
    return absolute(rel, axis)


def whole_sum(value, axis):
    n = lax.axis_size(axis)
    bit = 1
    while bit < n:
        value = value + swap(value, axis, gray(bit))
        bit *= 2
    return value


def norm_parts(values):
    centre = values - jnp.mean(values, -1, keepdims=True)
    spread = lax.rsqrt(jnp.mean(centre * centre, -1, keepdims=True) + EPS)
    return centre * spread, spread


def norm_back(d_out, gain, xhat, spread):
    e = d_out * gain
    return spread * (
        e - jnp.mean(e, -1, keepdims=True) - xhat * jnp.mean(e * xhat, -1, keepdims=True)
    )


def dot(a, b):
    return jnp.dot(a, b, preferred_element_type=F32)


def dot_nt(a, b):
    return lax.dot_general(a, b, (((1,), (1,)), ((), ())), preferred_element_type=F32)


def dot_tn(a, b):
    return lax.dot_general(a, b, (((0,), (0,)), ((), ())), preferred_element_type=F32)


def on_device(
    tokens,
    first_values,
    lengths,
    cotangent,
    first_gain,
    first_shift,
    query_weight,
    query_bias,
    key_weight,
    value_weight,
    value_bias,
    output_weight,
    output_bias,
    second_gain,
    second_shift,
    expand_weight,
    expand_bias,
    reduce_weight,
    reduce_bias,
):
    count = tokens.shape[1]
    block = tokens.shape[2]
    part_q = lax.axis_size("q")
    nb = lax.axis_size("y")
    cycle = count * part_q * GROUP
    own_rows = count * block
    si, qi, xi, ci, yi = (lax.axis_index(a) for a in ("s", "q", "x", "c", "y"))
    group = 2 * ci + xi
    length = lax.dynamic_index_in_dim(lengths[0], si, 0, keepdims=False)

    def gather_group(value):
        by_x = gather(value, "x")
        return jnp.swapaxes(gather(by_x, "c"), 0, 1)

    def gather_parts(value):
        flat = gather(gather(value, "q"), "s")
        return flat

    sizes = [D // cycle] * 2 + [D // cycle, DV // cycle] + [D // cycle] * 4 + [FF // cycle]
    packed = jnp.concatenate(
        [
            first_gain,
            first_shift,
            query_bias,
            value_bias,
            output_bias,
            second_gain,
            second_shift,
            reduce_bias,
            expand_bias,
        ]
    )
    spread_out = gather_parts(gather_group(packed)).reshape(cycle, -1).astype(F32)
    vectors = []
    at = 0
    for size in sizes:
        vectors.append(spread_out[:, at : at + size].reshape(-1))
        at += size
    gain_one, shift_one, q_bias, v_bias, o_bias, gain_two, shift_two, r_bias, e_bias = vectors

    def all_columns(weight):
        full = gather(weight, "y")
        return jnp.swapaxes(full, 0, 1).reshape(weight.shape[0], -1)

    rows_w = D // cycle
    q_cols = all_columns(query_weight).reshape(rows_w, 2, 2, HG)
    k_cols = all_columns(key_weight).reshape(rows_w, 2, 2, HG)
    v_cols = all_columns(value_weight).reshape(rows_w, 1, 2, HG)
    v_cols = jnp.concatenate([v_cols, v_cols], 1)
    mine = jnp.stack([q_cols, k_cols, v_cols], 1)
    by_x = exchange(jnp.moveaxis(mine, 3, 0), "x")
    by_c = exchange(jnp.moveaxis(by_x, 3, 0), "c")
    by_group = jnp.swapaxes(by_c, 0, 1)
    qkv_weight = gather_parts(by_group)
    qkv_weight = qkv_weight.reshape(D, 3, HG)
    q_w, k_w, v_w = (qkv_weight[:, j] for j in range(3))

    o_w = gather(gather_parts(gather(output_weight, "x")), "y")
    o_w = gather(o_w, "c")
    o_w = jnp.transpose(o_w, (2, 3, 4, 0, 5, 1, 6))
    o_w = o_w.reshape(D, D)

    unit = FF // cycle
    blocks_y = cycle // nb // GROUP
    e_cols = expand_weight.reshape(rows_w, blocks_y, 2, 2, unit)
    by_x = exchange(jnp.moveaxis(e_cols, 2, 0), "x")
    by_c = exchange(jnp.moveaxis(by_x, 3, 0), "c")
    e_w = gather(gather_parts(jnp.swapaxes(by_c, 0, 1)), "y")
    e_w = jnp.moveaxis(e_w, 0, 5).reshape(D, FF // GROUP)
    r_w = gather(gather_parts(reduce_weight), "y")
    r_w = jnp.moveaxis(r_w, 0, 3).reshape(FF // GROUP, D)
    my_ebias = e_bias.reshape(cycle // GROUP, GROUP, unit)
    my_ebias = lax.dynamic_index_in_dim(my_ebias, 2 * xi + ci, 1, keepdims=False).reshape(-1)
    my_qbias = lax.dynamic_index_in_dim(q_bias.reshape(GROUP, HG), group, 0, keepdims=False)
    my_vbias = lax.dynamic_index_in_dim(v_bias.reshape(2, HG), xi, 0, keepdims=False)

    own_tokens = exchange(tokens[0], "s").reshape(own_rows, D)
    own_first = exchange(first_values[0], "s").reshape(own_rows, 2, HG)
    own_cot = exchange(cotangent[0], "s").reshape(own_rows, D)

    def in_order(value):
        wide = value.shape[-1]
        parts = value.reshape(2, 2, count, block, wide)
        return jnp.transpose(parts, (2, 0, 1, 3, 4)).reshape(count * GROUP * block, wide)

    def by_device(value):
        wide = value.shape[-1]
        parts = value.reshape(count, 2, 2, block, wide)
        return jnp.transpose(parts, (1, 2, 0, 3, 4)).reshape(2, 2, own_rows, wide)

    all_tokens = in_order(gather_group(own_tokens))
    first_x = exchange(jnp.moveaxis(own_first, 1, 0), "x")
    first_mine = in_order(jnp.swapaxes(gather(first_x, "c"), 0, 1))

    seq_rows = all_tokens.shape[0]
    xhat_all, unused = norm_parts(all_tokens.astype(F32))
    normed = (xhat_all * gain_one + shift_one).astype(BF)
    query = (dot(normed, q_w) + my_qbias).astype(BF)
    keys = dot(normed, k_w).astype(BF)
    fresh = (dot(normed, v_w) + my_vbias).astype(BF)
    values = jnp.where(ci == 0, fresh, first_mine)

    chunk = GROUP * block

    def whole_keys(value):
        full = gather(value.reshape(count, chunk, HG), "q")
        return jnp.swapaxes(full, 0, 1).reshape(count * part_q * chunk, HG)

    heads = HG // HD
    keys_h = whole_keys(keys).reshape(-1, heads, HD)
    values_h = whole_keys(values).reshape(-1, heads, HD)
    query_h = query.reshape(-1, heads, HD)
    row = lax.iota(jnp.int32, seq_rows)
    row_pos = ((row // chunk) * part_q + qi) * chunk + row % chunk
    key_pos = lax.iota(jnp.int32, count * part_q * chunk)
    allowed = ((key_pos[None, :] <= row_pos[:, None]) & (key_pos[None, :] < length))[None]
    scale = HD**-0.5
    scores = jnp.einsum("qhd,khd->hqk", query_h, keys_h, preferred_element_type=F32) * scale
    scores = jnp.where(allowed, scores, NEG)
    peak = jnp.max(scores, -1, keepdims=True)
    weights = jnp.exp(scores - peak)
    probs = weights / jnp.sum(weights, -1, keepdims=True)
    probs_low = probs.astype(BF)
    attended = jnp.einsum("hqk,khd->qhd", probs_low, values_h, preferred_element_type=F32)
    attended_low = attended.reshape(seq_rows, HG).astype(BF)

    def to_rows(value):
        got = exchange(exchange(by_device(value), "x").swapaxes(0, 1), "c")
        return jnp.transpose(got, (2, 0, 1, 3)).reshape(own_rows, -1)

    def to_heads(value):
        parts = jnp.transpose(value.reshape(own_rows, 2, 2, HG), (2, 1, 0, 3))
        got = exchange(exchange(parts, "x").swapaxes(0, 1), "c").swapaxes(0, 1)
        return in_order(got)

    att_rows = to_rows(attended_low)
    resid = own_tokens.astype(F32)
    middle = resid + dot(att_rows, o_w) + o_bias
    xhat_two, spread_two = norm_parts(middle)
    second = (xhat_two * gain_two + shift_two).astype(BF)

    own_pos = ((lax.iota(jnp.int32, own_rows) // block * part_q + qi) * GROUP + 2 * xi + ci) * block
    own_pos = own_pos + lax.iota(jnp.int32, own_rows) % block
    upstream_low = jnp.where((own_pos < length)[:, None], own_cot, jnp.zeros_like(own_cot))
    upstream = upstream_low.astype(F32)

    second_all = gather_group(second).reshape(-1, D)
    upstream_all = gather_group(upstream_low).reshape(-1, D)
    hidden = dot(second_all, e_w) + my_ebias
    k0 = 0.7978845608028654
    inner = k0 * (hidden + 0.044715 * hidden * hidden * hidden)
    tanh = jnp.tanh(inner)
    active = (0.5 * hidden * (1.0 + tanh)).astype(BF)
    slope = 0.5 * (1.0 + tanh) + 0.5 * hidden * (1.0 - tanh * tanh) * k0 * (
        1.0 + 3 * 0.044715 * hidden * hidden
    )

    def sum_group(value):
        parts = value.reshape(2, 2, own_rows, D)
        return scatter_sum(scatter_sum(parts.swapaxes(0, 1), "c"), "x")

    mixed = middle + sum_group(dot(active, r_w)) + r_bias
    reduce_grad = dot_tn(active, upstream_all)
    d_hidden = (dot_nt(upstream_all, r_w) * slope).astype(BF)
    expand_grad = dot_tn(second_all, d_hidden)
    expand_bias_grad = jnp.sum(d_hidden.astype(F32), 0)
    d_second = sum_group(dot_nt(d_hidden, e_w))
    gain_two_grad = jnp.sum(d_second * xhat_two, 0)
    shift_two_grad = jnp.sum(d_second, 0)
    d_middle = upstream + norm_back(d_second, gain_two, xhat_two, spread_two)
    d_branch = d_middle.astype(BF)
    output_grad = dot_tn(att_rows, d_branch)
    output_bias_grad = jnp.sum(d_branch.astype(F32), 0)
    d_att_rows = dot_nt(d_branch, o_w).astype(BF)
    d_att = to_heads(d_att_rows)

    d_out_h = d_att.reshape(-1, heads, HD)
    d_probs = jnp.einsum("qhd,khd->hqk", d_out_h, values_h, preferred_element_type=F32)
    delta = jnp.sum(probs * d_probs, -1, keepdims=True)
    d_scores = (probs * (d_probs - delta)).astype(BF)
    d_query = jnp.einsum("hqk,khd->qhd", d_scores, keys_h, preferred_element_type=F32) * scale
    d_keys = jnp.einsum("hqk,qhd->khd", d_scores, query_h, preferred_element_type=F32) * scale
    d_values = jnp.einsum("hqk,qhd->khd", probs_low, d_out_h, preferred_element_type=F32)

    def own_keys(value):
        if part_q == 1:
            return value.reshape(seq_rows, HG)
        parts = value.reshape(count, part_q, chunk, HG).swapaxes(0, 1)
        return scatter_sum(parts, "q").reshape(seq_rows, HG)

    d_query_low = d_query.reshape(seq_rows, HG).astype(BF)
    d_keys_low = own_keys(d_keys).astype(BF)
    d_values_low = own_keys(d_values).astype(BF)
    d_fresh_low = jnp.where(ci == 0, d_values_low, jnp.zeros_like(d_values_low))

    first_back = exchange(by_device(d_values_low), "x").swapaxes(0, 1)
    first_back = gather(first_back, "c")[1]
    first_back = lax.dynamic_index_in_dim(first_back, ci, 0, keepdims=False)
    first_back = jnp.moveaxis(first_back, 0, 1).reshape(count, block, DV)
    grad_first = exchange(first_back, "s")[None]

    qkv_grad = jnp.stack(
        [dot_tn(normed, d_query_low), dot_tn(normed, d_keys_low), dot_tn(normed, d_fresh_low)], 1
    )
    d_normed = dot_nt(d_query_low, q_w) + dot_nt(d_keys_low, k_w) + dot_nt(d_fresh_low, v_w)
    d_normed = sum_group(by_device(d_normed))
    xhat_one, spread_one = norm_parts(resid)
    gain_one_grad = jnp.sum(d_normed * xhat_one, 0)
    shift_one_grad = jnp.sum(d_normed, 0)
    grad_rows = d_middle + norm_back(d_normed, gain_one, xhat_one, spread_one)

    grad_tokens = exchange(grad_rows.astype(BF).reshape(count, block, D), "s")[None]
    mixed_out = exchange(mixed.astype(BF).reshape(count, block, D), "s")[None]

    def sum_parts(value):
        return scatter_sum(scatter_sum(value, "s"), "q")

    qkv_part = sum_parts(qkv_grad.reshape(count, part_q, 2, 2, rows_w, 3, HG))
    by_c = exchange(jnp.swapaxes(qkv_part, 0, 1).astype(BF), "c")
    by_x = exchange(jnp.moveaxis(by_c, 1, 0), "x")
    q_all = by_x[:, :, :, 0]
    k_all = by_x[:, :, :, 1]
    v_all = by_x[:, 0, :, 2]

    def columns_home(value):
        return scatter_sum(jnp.moveaxis(value.reshape(rows_w, nb, -1), 1, 0), "y")

    q_home = columns_home(jnp.transpose(q_all, (2, 1, 0, 3)))
    k_home = columns_home(jnp.transpose(k_all, (2, 1, 0, 3)))
    v_home = columns_home(jnp.transpose(v_all, (1, 0, 2)))

    o_part = output_grad.reshape(count, part_q, 2, 2, rows_w, nb, D // nb)
    o_part = scatter_sum(jnp.moveaxis(o_part, 3, 0), "c")
    o_part = scatter_sum(jnp.moveaxis(o_part, 4, 0), "y")
    o_home = scatter_sum(sum_parts(o_part), "x")

    e_part = expand_grad.reshape(D, nb, blocks_y * unit)
    e_part = scatter_sum(jnp.moveaxis(e_part, 1, 0), "y")
    e_part = sum_parts(e_part.reshape(count, part_q, 2, 2, rows_w, blocks_y, unit))
    by_c = exchange(jnp.swapaxes(e_part, 0, 1).astype(BF), "c")
    by_x = exchange(jnp.moveaxis(by_c, 1, 0), "x")
    e_home = jnp.transpose(by_x, (2, 3, 0, 1, 4)).reshape(rows_w, FF // nb).astype(F32)

    r_part = reduce_grad.reshape(FF // GROUP, nb, D // nb)
    r_part = scatter_sum(jnp.moveaxis(r_part, 1, 0), "y")
    r_home = sum_parts(r_part.reshape(count, part_q, unit, D // nb))

    def placed(value, index, parts):
        zero = jnp.zeros((parts,) + value.shape, F32)
        return lax.dynamic_update_index_in_dim(zero, value, index, 0).reshape(-1)

    ebias_full = jnp.zeros((cycle // GROUP, GROUP, unit), F32)
    ebias_full = lax.dynamic_update_index_in_dim(
        ebias_full, expand_bias_grad.reshape(cycle // GROUP, unit), 2 * xi + ci, 1
    ).reshape(-1)
    qb = jnp.sum(d_query_low.astype(F32), 0)
    vb = jnp.sum(d_fresh_low.astype(F32), 0)
    vec = [
        gain_one_grad,
        shift_one_grad,
        placed(qb, group, GROUP),
        placed(vb, xi, 2),
        output_bias_grad,
        gain_two_grad,
        shift_two_grad,
        jnp.sum(upstream, 0),
        ebias_full,
    ]
    vec = jnp.concatenate([v.reshape(cycle, -1) for v in vec], 1)
    vec = vec.reshape(count, part_q, 2, 2, -1)
    for axis in ("c", "x", "y", "q", "s"):
        vec = whole_sum(vec, axis)
    vec = lax.dynamic_index_in_dim(vec.reshape(cycle, -1), ((si * part_q + qi) * 2 + xi) * 2 + ci, 0, keepdims=False)
    home = []
    at = 0
    for size in sizes:
        home.append(vec[at : at + size])
        at += size
    return (
        mixed_out,
        grad_tokens,
        grad_first,
        home[0],
        home[1],
        q_home,
        home[2],
        k_home,
        v_home,
        home[3],
        o_home,
        home[4],
        home[5],
        home[6],
        e_home,
        home[8],
        r_home,
        home[7],
    )


def solution(mesh):
    cycle, nb = mesh.devices.shape
    sequences = 4
    fine = Mesh(
        mesh.devices.reshape(sequences, cycle // (sequences * GROUP), 2, 2, nb),
        ("s", "q", "x", "c", "y"),
    )
    seq = ("s", "q", "x", "c")
    rows = P("y", None, seq, None)
    matrix = P(seq, "y")
    vector = P(seq)
    in_specs = (
        rows,
        rows,
        P("y", None),
        rows,
        vector,
        vector,
        matrix,
        vector,
        matrix,
        matrix,
        vector,
        matrix,
        vector,
        vector,
        vector,
        matrix,
        vector,
        matrix,
        vector,
    )
    out_specs = (
        rows,
        rows,
        rows,
        vector,
        vector,
        matrix,
        vector,
        matrix,
        matrix,
        vector,
        matrix,
        vector,
        vector,
        vector,
        matrix,
        vector,
        matrix,
        vector,
    )
    return jax.shard_map(
        on_device, mesh=fine, in_specs=in_specs, out_specs=out_specs, check_vma=False
    )
```

```python
import functools

import jax
import jax.numpy as jnp
from jax import lax
from jax.experimental import pallas as pl
from jax.experimental.pallas import tpu as pltpu
from jax.sharding import Mesh, PartitionSpec as P

D = 768
H = 12
HD = 64
FF = 3072
DV = 384
GROUP = 4
HG = D // GROUP
HEADS = HG // HD
UG = FF // GROUP

EPS = 1e-05
NEG = -1e30
SCALE = HD**-0.5
BF = jnp.bfloat16
F32 = jnp.float32
VMEM = pl.BlockSpec(memory_space=pltpu.VMEM)
SMEM = pl.BlockSpec(memory_space=pltpu.SMEM)


def gray(k):
    return k ^ (k >> 1)


def swap(value, axis, mask):
    return lax.ppermute(value, axis, [(i, i ^ mask) for i in range(lax.axis_size(axis))])


def pick(blocks, index):
    return lax.dynamic_index_in_dim(blocks, index, 0, keepdims=False)


def after(value, *others):
    return lax.optimization_barrier((value, *others))[0]


def relative(blocks, axis):
    n = lax.axis_size(axis)
    if n == 1:
        return blocks
    me = lax.axis_index(axis)
    return jnp.stack([pick(blocks, gray(r) ^ me) for r in range(n)], 0)


def absolute(rel, axis):
    n = lax.axis_size(axis)
    if n == 1:
        return rel
    me = lax.axis_index(axis)
    return jnp.stack([pick(rel, gray(a ^ me)) for a in range(n)], 0)


def gather_list(value, axis):
    pieces = [(value[None], [0])]
    size = 1
    while size < lax.axis_size(axis):
        held = pieces[0][0] if size == 1 else jnp.concatenate([p for p, unused in pieces], 0)
        pieces.append((swap(held, axis, gray(size)), list(range(size, 2 * size))))
        size *= 2
    return pieces


def gather(value, axis):
    return absolute(jnp.concatenate([p for p, unused in gather_list(value, axis)], 0), axis)


def direct(parts, axis):
    return [parts[0]] + [swap(parts[k], axis, k) for k in range(1, len(parts))]


def in_place(parts, axis):
    held = jnp.stack(parts)
    me = lax.axis_index(axis)
    return jnp.stack([pick(held, a ^ me) for a in range(len(parts))])


def direct_sum(rel, axis):
    got = direct([rel[0].astype(F32)] + [rel[k].astype(BF) for k in range(1, rel.shape[0])], axis)
    return sum(part.astype(F32) for part in got)


def scatter_slots(low, high, axis, got=None):
    while True:
        half = low.shape[0]
        if got is None:
            got = swap(high.astype(BF), axis, gray(half))
        total = low.astype(F32) + got.astype(F32)
        got = None
        if half == 1:
            return total[0]
        low, high = total[: half // 2], total[half // 2 :]


def scatter_sum(rel, axis):
    half = rel.shape[0] // 2
    return rel[0] if half == 0 else scatter_slots(rel[:half], rel[half:], axis)


def exchange(blocks, axis):
    n = lax.axis_size(axis)
    rel = relative(blocks, axis)
    bit = 1
    while bit < n:
        shape = rel.shape
        pairs = rel.reshape((n // (2 * bit), 2, bit) + shape[1:])
        got = swap(pairs[:, 1], axis, gray(bit))
        rel = jnp.stack([pairs[:, 0], got], 1).reshape(shape)
        bit *= 2
    return absolute(rel, axis)


def whole_sum(value, axis):
    n = lax.axis_size(axis)
    bit = 1
    while bit < n:
        value = value + swap(value, axis, bit)
        bit *= 2
    return value


def norm_parts(values):
    centre = values - jnp.mean(values, -1, keepdims=True)
    spread = lax.rsqrt(jnp.mean(centre * centre, -1, keepdims=True) + EPS)
    return centre * spread, spread


def norm_back(d_out, gain, xhat, spread):
    e = d_out * gain
    return spread * (
        e - jnp.mean(e, -1, keepdims=True) - xhat * jnp.mean(e * xhat, -1, keepdims=True)
    )


def dot(a, b):
    return jnp.dot(a, b, preferred_element_type=F32)


def dot_nt(a, b):
    return lax.dot_general(a, b, (((1,), (1,)), ((), ())), preferred_element_type=F32)


def dot_tn(a, b):
    return lax.dot_general(a, b, (((0,), (0,)), ((), ())), preferred_element_type=F32)


def places():
    return tuple(lax.axis_index(a) for a in ("s", "q", "x", "c", "y"))


def merged(blocks):
    n, rows, cols = blocks.shape
    if rows % 16 == 0:
        return blocks.reshape(n * rows, cols)
    return blocks.astype(F32).reshape(n * rows, cols).astype(BF)


def split_rows(rows, n):
    size = rows.shape[0] // n
    if size % 16 == 0:
        return [rows[i * size : (i + 1) * size] for i in range(n)]
    wide = rows.astype(F32)
    return [wide[i * size : (i + 1) * size].astype(BF) for i in range(n)]


def shape(dims, kind=BF):
    return jax.ShapeDtypeStruct(tuple(dims), kind)


def call(body, outs, scratch, flops, *operands, smem=0, mib=24):
    arrays = operands[smem:]
    n, n_out = len(arrays), len(outs)
    def copied(*refs):
        scalars, sources = refs[:smem], refs[smem : smem + n]
        results = refs[smem + n : smem + n + n_out]
        own = refs[smem + n + n_out : len(refs) - n - 1]
        held, sems = refs[len(refs) - n - 1 : -1], refs[-1]
        copies = [
            pltpu.make_async_copy(sources[i], held[i], sems.at[i]) for i in range(n)
        ]
        for copy in copies:
            copy.start()
        for copy in copies:
            copy.wait()
        body(*scalars, *held, *results, *own)

    return pl.pallas_call(
        copied,
        out_shape=tuple(outs),
        in_specs=[SMEM] * smem + [pl.BlockSpec(memory_space=pl.ANY)] * n,
        out_specs=tuple(VMEM for unused in outs),
        scratch_shapes=[*scratch]
        + [pltpu.VMEM(v.shape, v.dtype) for v in arrays]
        + [pltpu.SemaphoreType.DMA((n,))],
        cost_estimate=pl.CostEstimate(flops=1, bytes_accessed=1, transcendentals=0),
        compiler_params=pltpu.CompilerParams(vmem_limit_bytes=mib * 1024 * 1024),
    )(*operands)


def pack_rows_body(nb, query, keys, values, output, *refs):
    vectors = refs[:9]
    out, rows = refs[9:]
    cw, vw = D // nb, DV // nb
    out[:, :cw] = query[...]
    out[:, cw : 2 * cw] = keys[...]
    out[:, 2 * cw : 3 * cw] = output[...]
    out[:, 3 * cw : 3 * cw + vw] = values[...]
    rows[...] = jnp.zeros_like(rows)
    for j, vector in enumerate(vectors):
        size = vector.shape[0]
        rows[j : j + 1, :size] = vector[...].astype(F32).reshape(1, size)
    out[:, 3 * cw + vw :] = rows[...].astype(BF)


def pack_columns_body(nb, rw, n_own, y_slots, *refs):
    owns = refs[:n_own]
    pieces = refs[n_own : n_own + len(y_slots)]
    keep, send, out, scr, rows = refs[n_own + len(y_slots) :]
    si, qi, xi, ci, yi = places()
    cw, vw = D // nb, DV // nb
    per = owns[0].shape[0]
    n2 = n_own * per
    width = 3 * cw + vw
    rows[...] = jnp.zeros_like(rows)
    for j in range(n_own):
        scr[yi, j * per : (j + 1) * per] = owns[j][:, :, :width]
        out[0, j * per : (j + 1) * per] = owns[j][:, :, 2 * cw : 3 * cw]
        for q in range(per):
            held = owns[j][q, :, width:].astype(F32)
            for v in range(9):
                at = 3 * (j * per + q) + v // 3
                rows[at : at + 1, (v % 3) * HG : (v % 3 + 1) * HG] = held[v : v + 1]
    for ref, slots in zip(pieces, y_slots):
        for at, ry in enumerate(slots):
            scr[yi ^ gray(ry)] = ref[at]
            out[ry] = ref[at, :, :, 2 * cw : 3 * cw]
    both = ([], [])
    for n in range(n2):
        full = [
            jnp.concatenate([scr[y, n][:, a : a + w].astype(F32) for y in range(nb)], 1)
            for a, w in ((0, cw), (cw, cw), (3 * cw, vw))
        ]

        def part(x, c):
            cols = [v[:, (2 * c + x) * HG : (2 * c + x + 1) * HG] for v in full[:2]]
            return jnp.concatenate(cols + [full[2][:, x * HG : (x + 1) * HG]], 1)

        for c in range(2):
            one, two = part(0, c), part(1, c)
            both[c].append((jnp.where(xi == 0, one, two), jnp.where(xi == 0, two, one)))
    for which, ref in ((0, keep), (1, send)):
        parts = [pair[which] for c in range(2) for pair in both[c]] + [rows[...]]
        ref[...] = jnp.concatenate(parts, 0).astype(BF)


def pack_cores_body(mine, from_x, keep, send):
    si, qi, xi, ci, yi = places()
    half = (mine.shape[0] - 16) // 2
    parts = [], []
    for ref in (mine, from_x):
        a, b = ref[:half].astype(F32), ref[half : 2 * half].astype(F32)
        parts[0].append(jnp.where(ci == 0, a, b))
        parts[1].append(jnp.where(ci == 0, b, a))
    vectors = [ref[2 * half :].astype(F32) for ref in (mine, from_x)]
    keep[...] = jnp.concatenate(parts[0] + vectors, 0).astype(BF)
    send[...] = jnp.concatenate(parts[1] + vectors, 0).astype(BF)


def vectors_body(slots, part_q, rw, cycle, *refs):
    pieces = refs[: 2 * len(slots)]
    gain_one, shift_one, q_bias, v_bias, o_bias, gain_two, shift_two, r_bias, e_bias, scr = refs[
        2 * len(slots) :
    ]
    si, qi, xi, ci, yi = places()
    for stage, marks in enumerate(slots):
        for rc in range(2):
            for rx in range(2):
                ref = pieces[2 * stage + rc]
                at = ref.shape[0] - 32 + 16 * rx
                rows = ref[at : at + 16].astype(F32)
                for at, (rs, rq) in enumerate(marks):
                    place = ((si ^ rs) * part_q + (qi ^ gray(rq))) * GROUP
                    place = place + 2 * (xi ^ rx) + (ci ^ rc)
                    scr[pl.ds(place, 1), 0:3] = rows[3 * at : 3 * at + 3][None]

    def whole(j, size):
        held = scr[:, j // 3, (j % 3) * HG : (j % 3) * HG + size]
        wide = cycle * size
        lane = lax.broadcasted_iota(jnp.int32, (size, wide), 1)
        row = lax.broadcasted_iota(jnp.int32, (size, wide), 0)
        spread = jnp.where(lane % size == row, 1.0, 0.0).astype(BF)
        out = dot(held.astype(BF), spread)
        mark = lax.broadcasted_iota(jnp.int32, (cycle, wide), 1) // size
        row = lax.broadcasted_iota(jnp.int32, (cycle, wide), 0)
        return jnp.sum(jnp.where(mark == row, out, 0.0), 0, keepdims=True)

    for j, ref in ((0, gain_one), (1, shift_one), (4, o_bias), (5, gain_two), (6, shift_two), (7, r_bias)):
        ref[...] = whole(j, rw)
    query = whole(2, rw)
    group = 2 * ci + xi
    total = jnp.zeros((1, HG), F32)
    for g in range(GROUP):
        total = total + jnp.where(group == g, query[:, g * HG : (g + 1) * HG], 0.0)
    q_bias[...] = total
    value = whole(3, DV // cycle)
    v_bias[...] = jnp.where(xi == 0, value[:, :HG], value[:, HG:])
    unit = FF // cycle
    parts = []
    for j in range(cycle // GROUP):
        held = scr[j * GROUP + 2 * xi + ci]
        parts.append(held[2:3, 2 * HG : 2 * HG + unit])
    e_bias[...] = jnp.concatenate(parts, 1)


def pack_units_body(nb, blocks_y, expand, keep, send):
    si, qi, xi, ci, yi = places()
    unit = FF // (blocks_y * GROUP * nb)

    def part(x, c):
        cols = [expand[:, (GROUP * b + 2 * x + c) * unit : (GROUP * b + 2 * x + c + 1) * unit] for b in range(blocks_y)]
        return jnp.concatenate([v.astype(F32) for v in cols], 1)

    for c in range(2):
        one, two = part(0, c), part(1, c)
        keep[c] = jnp.where(xi == 0, one, two).astype(BF)
        send[c] = jnp.where(xi == 0, two, one).astype(BF)


def units_home_body(blocks_y, mine, other, out):
    si, qi, xi, ci, yi = places()
    unit = mine.shape[2] // blocks_y
    for b in range(blocks_y):
        for g in range(GROUP):
            total = jnp.zeros((mine.shape[1], unit), F32)
            for rx, ref in ((0, mine), (1, other)):
                for rc in range(2):
                    here = 2 * (xi ^ rx) + (ci ^ rc) == g
                    part = ref[rc, :, b * unit : (b + 1) * unit].astype(F32)
                    total = total + jnp.where(here, part, 0.0)
            at = (GROUP * b + g) * unit
            out[:, at : at + unit] = total


def columns_home_body(nb, n, keep, from_c, x_keep, x_from_c, low, high, scr):
    si, qi, xi, ci, yi = places()
    cw, vw = D // nb, DV // nb
    sources = ((0, 0, keep), (0, 1, from_c), (1, 0, x_keep), (1, 1, x_from_c))
    for s in range(n):
        full = []
        for kind in range(3):
            groups = []
            for g in range(GROUP if kind < 2 else 2):
                total = jnp.zeros((keep.shape[1], HG), F32)
                for rx, rc, ref in sources:
                    here = 2 * (ci ^ rc) + (xi ^ rx) == g
                    part = ref[s, :, kind * HG : (kind + 1) * HG].astype(F32)
                    total = total + jnp.where(here, part, 0.0)
                groups.append(total)
            full.append(jnp.concatenate(groups, 1))
        for y in range(nb):
            scr[y] = jnp.concatenate(
                [
                    full[0][:, y * cw : (y + 1) * cw],
                    full[1][:, y * cw : (y + 1) * cw],
                    full[2][:, y * vw : (y + 1) * vw],
                ],
                1,
            )
        for ry in range(nb):
            to = low if ry < nb // 2 else high
            to[ry % (nb // 2), s] = scr[yi ^ gray(ry)].astype(to.dtype)


def project_body(slots, count, part_q, block, rw, *refs):
    n_pieces = 2 * len(slots)
    sources = refs[:8]
    pieces = refs[8 : 8 + n_pieces]
    gain, shift, q_bias, v_bias = refs[8 + n_pieces : 12 + n_pieces]
    query, keys, values, normed, weight, scr_w, scr_f = refs[12 + n_pieces :]
    si, qi, xi, ci, unused = places()
    for stage, marks in enumerate(slots):
        for at, (rs, rq) in enumerate(marks):
            base = ((si ^ rs) * part_q + (qi ^ gray(rq))) * GROUP
            for rc in range(2):
                ref = pieces[2 * stage + rc]
                n2 = len(marks)
                held = split_rows(ref[: 2 * n2 * rw], 2 * n2)
                for rx in range(2):
                    place = base + 2 * (xi ^ rx) + (ci ^ rc)
                    scr_w[pl.ds(place, 1)] = held[rx * n2 + at][None]
    weight[...] = merged(scr_w[...])
    for pair in range(4):
        rx, rc = pair % 2, pair // 2
        for r in range(count):
            here = sources[2 * pair + r // 2][r % 2]
            at = (((si ^ r) * 2 + (xi ^ rx)) * 2 + (ci ^ rc)) * block
            at = pl.multiple_of(at, block)
            xhat, unused = norm_parts(here[:, :D].astype(F32))
            normed[pl.ds(at, block), :] = (xhat * gain[...] + shift[...]).astype(BF)
            scr_f[pl.ds(at, block), :] = jnp.where(
                xi == 0, here[:, D : D + HG], here[:, D + HG : D + 2 * HG]
            )
    rows = GROUP * block
    for i in range(count):
        span = slice(i * rows, (i + 1) * rows)
        out = dot(normed[span, :], weight[...])
        q_low = (out[:, :HG] + q_bias[...]).astype(BF) * SCALE
        k_low = out[:, HG : 2 * HG].astype(BF)
        v_low = (out[:, 2 * HG :] + v_bias[...]).astype(BF)
        v_low = jnp.where(ci == 0, v_low, scr_f[span, :])
        for h in range(HEADS):
            cols = slice(h * HD, (h + 1) * HD)
            query[h, span, :] = q_low[:, cols].astype(BF)
            keys[h, span, :] = k_low[:, cols]
            values[h, span, :] = v_low[:, cols]


def allowed_at(i, rows, width, part_q, length):
    unused, qi, *unused = places()
    row_pos = (i * part_q + qi) * rows + lax.broadcasted_iota(jnp.int32, (1, rows), 1)
    last = jnp.minimum(row_pos, length - 1)
    return lax.broadcasted_iota(jnp.int32, (width, rows), 0) <= last


def attend_body(count, part_q, block, lengths, query, keys, values, att, lse, keep, send, scr):
    si, qi, xi, ci, unused = places()
    length = lengths[0, si]
    rows = GROUP * block
    for i in range(count):
        span = slice(i * rows, (i + 1) * rows)
        width = (i + 1) * part_q * rows
        allowed = allowed_at(i, rows, width, part_q, length)
        outs = []
        for h in range(HEADS):
            scores = dot_nt(keys[h, :width, :], query[h, span, :])
            scores = jnp.where(allowed, scores, NEG)
            peak = jnp.max(scores, 0, keepdims=True)
            weights = jnp.exp(scores - peak)
            total = jnp.sum(weights, 0, keepdims=True)
            out = dot_tn(values[h, :width, :], weights.astype(BF)) * (1.0 / total)
            att[h, :, span] = out
            lse[i * HEADS + h : i * HEADS + h + 1, :] = peak + jnp.log(total)
            outs.append(out)
        scr[span, :] = jnp.concatenate(outs, 0).T.astype(BF)
    for rx, to in ((0, keep), (1, send)):
        for rc in range(2):
            for r in range(count):
                at = (((si ^ r) * 2 + (xi ^ rx)) * 2 + (ci ^ rc)) * block
                to[r * block : (r + 1) * block, rc * HG : (rc + 1) * HG] = scr[
                    pl.ds(pl.multiple_of(at, block), block), :
                ]


def output_body(
    slots, count, part_q, block, nb, rw, tok_a, tok_b, keep, from_x, from_ck, from_cx, *refs
):
    n_pieces = 4 * len(slots)
    pieces = refs[:n_pieces]
    bias, gain, shift, middle, second, weight, scr = refs[n_pieces:]
    si, qi, xi, ci, yi = places()
    for stage, marks in enumerate(slots):
        for rc in range(2):
            for rx in range(2):
                ref = pieces[4 * stage + 2 * rc + rx]
                for at, (rs, rq) in enumerate(marks):
                    place = ((si ^ rs) * part_q + (qi ^ gray(rq))) * GROUP
                    place = place + 2 * (xi ^ rx) + (ci ^ rc)
                    for ry in range(nb):
                        scr[yi ^ gray(ry), pl.ds(place, 1)] = ref[ry, at][None]
    for y in range(nb):
        cw = D // nb
        weight[:, y * cw : (y + 1) * cw] = merged(scr[y])
    tokens = [ref[j][:, :D].astype(F32) for ref in (tok_a, tok_b) for j in range(2)]
    total = jnp.concatenate(tokens, 0) + bias[...]
    for ref, lanes, rx, rc in ((keep, 0, 0, 0), (from_x, 0, 1, 0), (from_ck, 1, 0, 1), (from_cx, 1, 1, 1)):
        group = 2 * (ci ^ rc) + (xi ^ rx)
        rows = weight[pl.ds(pl.multiple_of(group * HG, HG), HG), :]
        total = total + dot(ref[:, lanes * HG : (lanes + 1) * HG], rows)
    middle[...] = total
    xhat, unused = norm_parts(total)
    second[...] = (xhat * gain[...] + shift[...]).astype(BF)


def feed_body(slots, part_q, nb, rw, *refs):
    rows_in = refs[:8]
    pieces = refs[8 : 8 + len(slots)]
    bias, mx_keep, mx_send, ds_keep, ds_send, xs, us, acts, dhs, eb, scr_e, scr_r, e_w, r_w = refs[
        8 + len(slots) :
    ]
    eb[...] = jnp.zeros_like(eb)
    si, qi, xi, ci, yi = places()
    for ref, marks in zip(pieces, slots):
        for at, (ry, rs, rq) in enumerate(marks):
            base = ((si ^ rs) * part_q + (qi ^ gray(rq))) * GROUP
            y = yi ^ gray(ry)
            for inner in range(GROUP):
                place = base + 2 * (xi ^ (inner % 2)) + (ci ^ (inner // 2))
                scr_e[y, pl.ds(place, 1)] = ref[at, inner][None]
            scr_r[y, pl.ds(base, GROUP)] = ref[at, GROUP : 2 * GROUP]
    cw = D // nb
    for y in range(nb):
        e_w[:, y * cw : (y + 1) * cw] = merged(scr_e[y])
        r_w[:, y * cw : (y + 1) * cw] = merged(scr_r[y])
    rows = rows_in[0].shape[0]
    for b in range(4):
        xs[b * rows : (b + 1) * rows, :] = rows_in[b][...]
        us[b * rows : (b + 1) * rows, :] = rows_in[4 + b][...]

    def step(b, unused):
        span = pl.ds(pl.multiple_of(b * rows, rows), rows)
        here = xs[span, :]
        up = us[span, :]
        hidden = dot(here, e_w[...]) + bias[...]
        k0 = 0.7978845608028654
        square = hidden * hidden
        tanh = jnp.tanh(k0 * hidden * (1.0 + 0.044715 * square))
        half = 0.5 * (1.0 + tanh)
        active = (hidden * half).astype(BF)
        slope = half + 0.5 * k0 * hidden * (1.0 - tanh * tanh) * (1.0 + 3 * 0.044715 * square)
        acts[span, :] = active
        mixed = dot(active, r_w[...])
        d_hidden = (dot_nt(up, r_w[...]) * slope).astype(BF)
        dhs[span, :] = d_hidden
        eb[...] += jnp.sum(d_hidden.astype(F32), 0, keepdims=True)
        d_second = dot_nt(d_hidden, e_w[...])

        @pl.when(b % 2 == 0)
        def _():
            mx_keep[b // 2] = mixed
            ds_keep[b // 2] = d_second

        @pl.when(b % 2 == 1)
        def _():
            mx_send[b // 2] = mixed.astype(BF)
            ds_send[b // 2] = d_second.astype(BF)

        return unused

    lax.fori_loop(0, 4, step, 0)


def feed_grad_body(count, part_q, nb, rw, left, right, low, high, scr):
    si, qi, xi, ci, yi = places()
    cw = D // nb
    for y in range(nb):
        scr[y] = dot_tn(left[...], right[:, y * cw : (y + 1) * cw])
    for ry in range(nb):
        to = low if ry < nb // 2 else high
        for rs in range(count):
            for rq in range(part_q):
                at = ((si ^ rs) * part_q + (qi ^ gray(rq))) * GROUP * rw
                part = scr[yi ^ gray(ry), pl.ds(pl.multiple_of(at, GROUP * rw), GROUP * rw), :]
                to[ry % (nb // 2), rs, rq] = part.reshape(GROUP, rw, cw).astype(BF)


def middle_back_body(
    cycle, ds_keep, from_c, from_x, upstream, middle, gain, weight, eb, d_middle, d_branch, keep, send, sums
):
    si, qi, xi, ci, yi = places()
    unit = FF // cycle
    parts = []
    for j in range(cycle // GROUP):
        part = eb[:, j * unit : (j + 1) * unit]
        for g in range(GROUP):
            parts.append(jnp.where(2 * xi + ci == g, part, jnp.zeros_like(part)))
    for j in range(FF // D):
        per = len(parts) * D // FF
        sums[4 + j : 5 + j, :] = jnp.concatenate(parts[j * per : (j + 1) * per], 1)
    d_second = ds_keep[0] + from_c[0].astype(F32) + from_x[...].astype(F32)
    xhat, spread = norm_parts(middle[...])
    up = upstream[...].astype(F32)
    total = up + norm_back(d_second, gain[...], xhat, spread)
    d_middle[...] = total
    low = total.astype(BF)
    d_branch[...] = low
    sums[0:1, :] = jnp.sum(low.astype(F32), 0, keepdims=True)
    sums[1:2, :] = jnp.sum(d_second * xhat, 0, keepdims=True)
    sums[2:3, :] = jnp.sum(d_second, 0, keepdims=True)
    sums[3:4, :] = jnp.sum(up, 0, keepdims=True)
    for rx, to in ((0, keep), (1, send)):
        for rc in range(2):
            group = 2 * (ci ^ rc) + (xi ^ rx)
            rows = weight[pl.ds(pl.multiple_of(group * HG, HG), HG), :]
            to[:, rc * HG : (rc + 1) * HG] = dot_nt(low, rows).astype(BF)


def output_grad_body(count, part_q, nb, rw, keep, from_x, from_ck, from_cx, d_branch, low, high, scr):
    si, qi, xi, ci, yi = places()
    cw = D // nb
    for ref, lanes, rx, rc in ((keep, 0, 0, 0), (from_x, 0, 1, 0), (from_ck, 1, 0, 1), (from_cx, 1, 1, 1)):
        group = 2 * (ci ^ rc) + (xi ^ rx)
        grad = dot_tn(ref[:, lanes * HG : (lanes + 1) * HG], d_branch[...])
        for y in range(nb):
            part = grad[:, y * cw : (y + 1) * cw].reshape(HG // rw, rw, cw)
            scr[y, pl.ds(group * (HG // rw), HG // rw)] = part
    for rc, to in ((0, low), (1, high)):
        for ry in range(nb):
            for rs in range(count):
                for rq in range(part_q):
                    base = ((si ^ rs) * part_q + (qi ^ gray(rq))) * GROUP
                    for rx in range(2):
                        place = base + 2 * (xi ^ rx) + (ci ^ rc)
                        to[ry, rs, rq, rx] = scr[yi ^ gray(ry), place].astype(BF)


def attend_back_body(
    count, part_q, block, lengths, keep, from_x, from_ck, from_cx, query, keys, values, att, lse,
    d_query, d_pair, scr_o, acc_k, acc_v,
):
    si, qi, xi, ci, unused = places()
    length = lengths[0, si]
    rows = GROUP * block
    for ref, lanes, rx, rc in ((keep, 0, 0, 0), (from_x, 0, 1, 0), (from_ck, 1, 0, 1), (from_cx, 1, 1, 1)):
        for r in range(count):
            at = (((si ^ r) * 2 + (xi ^ rx)) * 2 + (ci ^ rc)) * block
            at = pl.multiple_of(at, block)
            scr_o[pl.ds(at, block), :] = ref[
                r * block : (r + 1) * block, lanes * HG : (lanes + 1) * HG
            ]
    acc_k[...] = jnp.zeros_like(acc_k)
    acc_v[...] = jnp.zeros_like(acc_v)
    for i in range(count):
        span = slice(i * rows, (i + 1) * rows)
        width = (i + 1) * part_q * rows
        allowed = allowed_at(i, rows, width, part_q, length)
        d_out_all = scr_o[span, :]
        d_out_t = d_out_all.astype(F32).T
        d_queries = []
        for h in range(HEADS):
            q_here = query[h, span, :]
            k_here = keys[h, :width, :]
            d_out = d_out_all[:, h * HD : (h + 1) * HD]
            scores = dot_nt(k_here, q_here)
            logs = lse[i * HEADS + h : i * HEADS + h + 1, :]
            probs = jnp.where(allowed, jnp.exp(scores - logs), 0.0)
            d_probs = dot_nt(values[h, :width, :], d_out)
            delta = jnp.sum(
                d_out_t[h * HD : (h + 1) * HD, :] * att[h, :, span], 0, keepdims=True
            )
            d_scores = (probs * (d_probs - delta)).astype(BF)
            acc_v[h, :width, :] += dot(probs.astype(BF), d_out)
            acc_k[h, :width, :] += dot(d_scores, q_here)
            d_queries.append(dot_tn(k_here, d_scores) * SCALE)
        d_query[span, :] = jnp.concatenate(d_queries, 0).T.astype(BF)
    kind = d_pair.dtype
    for h in range(HEADS):
        d_pair[:, h * HD : (h + 1) * HD] = acc_k[h].astype(kind)
        d_pair[:, HG + h * HD : HG + (h + 1) * HD] = acc_v[h].astype(kind)


def normed_back_body(count, block, d_query, d_pair, weight, keep, dn_send, first_keep, first_send, scr):
    si, qi, xi, ci, yi = places()
    scr[:, :HG] = d_query[...]
    scr[:, HG : 2 * HG] = d_pair[:, :HG]
    scr[:, 2 * HG :] = jnp.where(ci == 0, d_pair[:, HG:], jnp.zeros_like(d_pair[:, HG:]))
    for rc in (1, 0):
        for rx in (1, 0):
            starts = [
                pl.multiple_of((((si ^ r) * 2 + (xi ^ rx)) * 2 + (ci ^ rc)) * block, block)
                for r in range(count)
            ]
            here = jnp.concatenate([scr[pl.ds(at, block), :] for at in starts], 0)
            out = dot_nt(here, weight[...])
            if rc == 1:
                dn_send[rx] = out.astype(BF)
            else:
                keep[rx] = out
            to = first_send if rx == 1 else first_keep
            for r, at in enumerate(starts):
                to[r * block : (r + 1) * block, rc * HG : (rc + 1) * HG] = d_pair[
                    pl.ds(at, block), HG : 2 * HG
                ]


def project_grad_body(count, part_q, rw, normed, d_query, d_pair, keep, send, sums, scr, scr_d):
    si, qi, xi, ci, yi = places()
    scr_d[:, :HG] = d_query[...]
    scr_d[:, HG : 2 * HG] = d_pair[:, :HG]
    scr_d[:, 2 * HG :] = jnp.where(ci == 0, d_pair[:, HG:], jnp.zeros_like(d_pair[:, HG:]))
    scr[...] = dot_tn(normed[...], scr_d[...])
    total = jnp.sum(scr_d[...].astype(F32), 0, keepdims=True)
    group = 2 * ci + xi
    q_sum = total[:, :HG]
    v_sum = total[:, 2 * HG :]
    zero = jnp.zeros_like(q_sum)
    sums[0:1, :] = jnp.concatenate([jnp.where(group == g, q_sum, zero) for g in range(GROUP)], 1)
    sums[1:2, :] = jnp.concatenate(
        [jnp.where(group == g, v_sum, zero) for g in range(2)] + [zero, zero], 1
    )
    for rc, to in ((0, keep), (1, send)):
        for rx in range(2):
            for rs in range(count):
                for rq in range(part_q):
                    at = ((si ^ rs) * part_q + (qi ^ gray(rq))) * GROUP + 2 * (xi ^ rx) + (ci ^ rc)
                    at = pl.multiple_of(at * rw, rw)
                    to[rx, rs, rq] = scr[pl.ds(at, rw), :].astype(BF)


def tokens_back_body(keep, from_c, from_x, tok_a, tok_b, gain, d_middle, *refs):
    outs, sums = refs[:4], refs[4]
    block = tok_a.shape[1]
    g_sum = jnp.zeros((1, D), F32)
    s_sum = jnp.zeros((1, D), F32)
    for r in range(4):
        span = slice(r * block, (r + 1) * block)
        xhat, spread = norm_parts((tok_a if r < 2 else tok_b)[r % 2][:, :D].astype(F32))
        d_normed = keep[0, span, :] + from_c[0, span, :].astype(F32) + from_x[span, :].astype(F32)
        g_sum = g_sum + jnp.sum(d_normed * xhat, 0, keepdims=True)
        s_sum = s_sum + jnp.sum(d_normed, 0, keepdims=True)
        out = d_middle[span, :] + norm_back(d_normed, gain[...], xhat, spread)
        outs[r][...] = out.astype(BF)
    sums[0:1, :] = g_sum
    sums[1:2, :] = s_sum


def on_device(
    tokens,
    first_values,
    lengths,
    cotangent,
    first_gain,
    first_shift,
    query_weight,
    query_bias,
    key_weight,
    value_weight,
    value_bias,
    output_weight,
    output_bias,
    second_gain,
    second_shift,
    expand_weight,
    expand_bias,
    reduce_weight,
    reduce_bias,
):
    count = tokens.shape[1]
    block = tokens.shape[2]
    part_q = lax.axis_size("q")
    nb = lax.axis_size("y")
    cycle = count * part_q * GROUP
    own_rows = count * block
    seq_rows = GROUP * own_rows
    rw = D // cycle
    cw = D // nb
    si, qi, xi, ci, yi = places()
    length = pick(lengths[0], si)

    vectors = [
        first_gain,
        first_shift,
        query_bias,
        value_bias,
        output_bias,
        second_gain,
        second_shift,
        reduce_bias,
        expand_bias,
    ]
    width = 3 * cw + DV // nb
    payload = call(
        functools.partial(pack_rows_body, nb),
        [shape((rw, width + HG))],
        [pltpu.VMEM((rw, HG), F32)],
        0,
        query_weight,
        key_weight,
        value_weight,
        output_weight,
        *vectors,
        mib=60,
    )[0]
    by_q = jnp.concatenate([p for p, unused in gather_list(payload, "q")], 0)
    by_s = direct([by_q] * count, "s")

    both = after(jnp.concatenate([tokens[0], first_values[0]], -1), *by_s[2:])
    got = direct([pick(both, si ^ k) for k in range(count)], "s")

    qkv_pieces, qkv_slots, o_parts = [], [], []
    for first in (0, 2):
        owns = by_s[first : first + 2]
        if first > 0:
            owns = after(owns, by_y[0][0])
        marks = [(rs, rq) for rs in (first, first + 1) for rq in range(part_q)]
        n2 = len(marks)
        held = jnp.concatenate(owns, 0)[:, :, :width]
        by_y = gather_list(held, "y")[1:]
        if first > 0:
            by_y = [(after(part, *got[2:]), slots) for part, slots in by_y]
        pack_shape = shape((2 * n2 * rw + 16, 3 * HG))
        core_shape = shape((2 * n2 * rw + 32, 3 * HG))
        keep, send, o_part = call(
            functools.partial(pack_columns_body, nb, rw, 2, [slots for unused, slots in by_y]),
            [pack_shape, pack_shape, shape((nb, n2, rw, cw))],
            [pltpu.VMEM((nb, n2, rw, width), BF), pltpu.VMEM((16, 3 * HG), F32)],
            0,
            *owns,
            *[part for part, unused in by_y],
        )
        x_got = swap(send, "x", 1)
        if first == 0:
            got = list(after(tuple(got), x_got))
            tok_a, tok_b = jnp.stack(got[:2]), jnp.stack(got[2:])
        keep, send = call(
            pack_cores_body,
            [core_shape, core_shape],
            [],
            0,
            keep,
            x_got,
        )
        qkv_pieces += [keep, swap(send, "c", 1)]
        qkv_slots.append(marks)
        o_parts.append(o_part)
    xa, xb = swap(tok_a, "x", 1), swap(tok_b, "x", 1)
    sources = [tok_a, tok_b, xa, xb]
    sources = sources + [swap(v, "c", 1) for v in sources]
    row = shape((1, D), F32)
    gain_one, shift_one, my_qbias, my_vbias, o_bias, gain_two, shift_two, r_bias, my_ebias = call(
        functools.partial(vectors_body, qkv_slots, part_q, rw, cycle),
        [row, row, shape((1, HG), F32), shape((1, HG), F32), row, row, row, row, shape((1, UG), F32)],
        [pltpu.VMEM((cycle, 8, 3 * HG), F32)],
        0,
        *qkv_pieces,
    )

    o_both = jnp.concatenate(o_parts, 1)
    o_x = swap(o_both, "x", 1)
    o_pieces = [o_both, o_x, swap(o_both, "c", 1), swap(o_x, "c", 1)]
    o_slots = [qkv_slots[0] + qkv_slots[1]]
    blocks_y = cycle // nb // GROUP
    keep, send = call(
        functools.partial(pack_units_body, nb, blocks_y),
        [shape((2, rw, cw)), shape((2, rw, cw))],
        [],
        0,
        expand_weight,
        mib=60,
    )
    from_x = swap(send, "x", 1)
    from_c = swap(jnp.stack([pick(keep, ci ^ 1), pick(from_x, ci ^ 1)]), "c", 1)
    f_piece = jnp.concatenate(
        [jnp.stack([pick(keep, ci), pick(from_x, ci)]), from_c, reduce_weight.reshape(GROUP, rw, cw)], 0
    )
    f_by_q = jnp.concatenate([p for p, unused in gather_list(f_piece, "q")], 0)
    f_by_q = f_by_q.reshape((part_q,) + f_piece.shape)

    f_two = swap(after(f_by_q, tok_b), "s", 2)

    heads = [shape((HEADS, seq_rows, HD))] * 3
    query, keys, values, normed, qkv_w = call(
        functools.partial(
            project_body, qkv_slots, count, part_q, block, rw
        ),
        heads + [shape((seq_rows, D)), shape((D, 3 * HG))],
        [pltpu.VMEM((cycle, rw, 3 * HG), BF), pltpu.VMEM((seq_rows, HG), BF)],
        2 * seq_rows * D * 3 * HG,
        *sources,
        *qkv_pieces,
        gain_one,
        shift_one,
        my_qbias,
        my_vbias,
    )

    def whole_keys(value):
        if part_q == 1:
            return value
        parts = gather(value.reshape(HEADS, count, GROUP * block, HD), "q")
        return jnp.moveaxis(parts, 0, 2).reshape(HEADS, part_q * seq_rows, HD)

    got = after(cotangent[0], query)
    got = direct([pick(got, si ^ k) for k in range(count)], "s")
    query = after(query, o_x)
    keys, values = whole_keys(keys), whole_keys(values)
    key_rows = keys.shape[1]
    att_flops = 2 * HEADS * seq_rows * key_rows * HD
    pair_shape = shape((own_rows, 2 * HG))
    att, lse, att_keep, att_send = call(
        functools.partial(attend_body, count, part_q, block),
        [
            shape((HEADS, HD, seq_rows), F32),
            shape((count * HEADS, GROUP * block), F32),
            pair_shape,
            pair_shape,
        ],
        [pltpu.VMEM((seq_rows, HG), BF)],
        8 * att_flops,
        lengths,
        query,
        keys,
        values,
        smem=1,
    )
    att_x = swap(att_send, "x", 1)
    f_last = after(f_by_q, att_x)
    f_last = jnp.concatenate([swap(f_last, "s", 3), swap(f_last, "s", 1)], 0)
    pieces, piece_slots = [], []
    for held, steps in ((f_by_q, (0,)), (after(f_two, att_send), (2,)), (f_last, (3, 1))):
        for part, ys in gather_list(held, "y"):
            pieces.append(part.reshape((-1,) + f_piece.shape))
            piece_slots.append([(ry, rs, rq) for ry in ys for rs in steps for rq in range(part_q)])
    upstream = jnp.stack(got)
    slot_of = jnp.stack([si ^ k for k in range(count)])
    position = ((slot_of * part_q + qi) * GROUP + 2 * xi + ci) * block
    position = position[:, None] + lax.iota(jnp.int32, block)[None]
    upstream = jnp.where((position < length)[..., None], upstream, jnp.zeros_like(upstream))
    upstream = upstream.reshape(own_rows, D)
    up_x = swap(upstream, "x", 1)
    ups = [upstream, swap(upstream, "c", 1), up_x, swap(up_x, "c", 1)]

    o_bias = after(o_bias, f_two)
    att_rows = [att_keep, att_x, swap(att_keep, "c", 1), swap(att_x, "c", 1)]
    middle, second, o_w = call(
        functools.partial(output_body, o_slots, count, part_q, block, nb, rw),
        [shape((own_rows, D), F32), shape((own_rows, D)), shape((D, D))],
        [pltpu.VMEM((nb, cycle, rw, cw), BF)],
        2 * own_rows * D * D,
        tok_a,
        tok_b,
        *att_rows,
        *o_pieces,
        o_bias,
        gain_two,
        shift_two,
    )

    second_x = swap(after(second, up_x), "x", 1)
    seconds = [second, swap(second, "c", 1), second_x, swap(second_x, "c", 1)]
    half_keep, half_send = shape((2, own_rows, D), F32), shape((2, own_rows, D))
    mx_keep, mx_send, ds_keep, ds_send, xs, us, acts, dhs, eb_sum = call(
        functools.partial(feed_body, piece_slots, part_q, nb, rw),
        [half_keep, half_send, half_keep, half_send] + [shape((seq_rows, D))] * 4 + [shape((1, UG), F32)],
        [pltpu.VMEM((nb, cycle, rw, cw), BF)] * 2 + [pltpu.VMEM((D, UG), BF), pltpu.VMEM((UG, D), BF)],
        8 * seq_rows * D * UG,
        *seconds,
        *ups,
        *pieces,
        my_ebias,
    )
    ds_c = swap(ds_send, "c", 1)
    ds_x = swap((ds_keep[1] + ds_c[1].astype(F32)).astype(BF), "x", 1)
    grad_shape = shape((nb // 2, count, part_q, GROUP, rw, cw))

    def feed_grad(left, right):
        return call(
            functools.partial(feed_grad_body, count, part_q, nb, rw),
            [grad_shape, grad_shape],
            [pltpu.VMEM((nb, D, cw), F32)],
            2 * seq_rows * D * UG,
            left,
            right,
        )

    xs, acts = after((xs, acts), ds_c)
    e_low, e_high = feed_grad(xs, dhs)
    e_got = swap(e_high, "y", gray(nb // 2))
    r_low, r_high = feed_grad(after(acts, e_low), us)
    mx_c = swap(after(mx_send, ds_c), "c", 1)
    d_middle, d_branch, d_keep, d_send, sums_two = call(
        functools.partial(middle_back_body, cycle),
        [shape((own_rows, D), F32), shape((own_rows, D)), pair_shape, pair_shape, shape((8, D), F32)],
        [],
        2 * own_rows * D * D,
        ds_keep,
        ds_c,
        ds_x,
        upstream,
        middle,
        after(gain_two, r_low, mx_c),
        o_w,
        eb_sum,
    )
    d_x = swap(d_send, "x", 1)
    d_rows = [d_keep, d_x, swap(d_keep, "c", 1), swap(d_x, "c", 1)]
    o_shape = shape((nb, count, part_q, 2, rw, cw))
    o_low, o_high = call(
        functools.partial(output_grad_body, count, part_q, nb, rw),
        [o_shape, o_shape],
        [pltpu.VMEM((nb, cycle, rw, cw), F32)],
        2 * own_rows * D * D,
        *att_rows,
        d_branch,
    )

    o_part = scatter_slots(o_low[None], o_high[None], "c")
    r_got = swap(after(r_high, e_got), "y", gray(nb // 2))
    mx_x = swap(after((mx_keep[1] + mx_c[1].astype(F32)).astype(BF), d_x), "x", 1)
    att = after(att, o_part, e_got)
    e_part = scatter_slots(e_low, None, "y", e_got)
    e_got = direct([e_part[0]] + [e_part[k].astype(BF) for k in range(1, count)], "s")

    d_query, d_pair = call(
        functools.partial(attend_back_body, count, part_q, block),
        [shape((seq_rows, HG)), shape((key_rows, 2 * HG), BF if part_q == 1 else F32)],
        [pltpu.VMEM((seq_rows, HG), BF)] + [pltpu.VMEM((HEADS, key_rows, HD), F32)] * 2,
        20 * att_flops,
        lengths,
        *d_rows,
        query,
        keys,
        values,
        att,
        lse,
        smem=1,
    )
    qkv_w, normed = after(qkv_w, mx_x, *e_got[1:]), after(normed, r_got)
    o_part = scatter_sum(after(o_part, r_got), "y")
    if part_q > 1:
        parts = d_pair.reshape(count, part_q, GROUP * block, 2 * HG).swapaxes(0, 1)
        d_pair = scatter_sum(relative(parts, "q"), "q").reshape(seq_rows, 2 * HG).astype(BF)
    dn_keep, dn_send, first_keep, first_send = call(
        functools.partial(normed_back_body, count, block),
        [half_keep, half_send, pair_shape, pair_shape],
        [pltpu.VMEM((seq_rows, 3 * HG), BF)],
        2 * seq_rows * D * 3 * HG,
        d_query,
        d_pair,
        qkv_w,
    )
    dn_c = swap(dn_send, "c", 1)
    dn_x = swap((dn_keep[1] + dn_c[1].astype(F32)).astype(BF), "x", 1)
    p_shape = shape((2, count, part_q, rw, 3 * HG))
    p_keep, p_send, sums_qv = call(
        functools.partial(project_grad_body, count, part_q, rw),
        [p_shape, p_shape, shape((2, D), F32)],
        [pltpu.VMEM((D, 3 * HG), F32), pltpu.VMEM((seq_rows, 3 * HG), BF)],
        2 * seq_rows * D * 3 * HG,
        normed,
        d_query,
        d_pair,
    )
    r_part = after(scatter_slots(r_low, None, "y", r_got), dn_x)
    r_got = direct([r_part[0]] + [r_part[k].astype(BF) for k in range(1, count)], "s")
    *gt, sums_one = call(
        tokens_back_body,
        [shape((block, D))] * count + [shape((2, D), F32)],
        [],
        own_rows * D * 40,
        dn_keep,
        dn_c,
        dn_x,
        tok_a,
        tok_b,
        gain_one,
        d_middle,
    )
    gt = direct(after(gt, *r_got[1:]), "s")
    grad_tokens = in_place(gt, "s")[None]

    mixed = middle + mx_keep[0] + mx_c[0].astype(F32) + mx_x.astype(F32) + r_bias
    mixed = mixed.astype(BF)
    first_x = swap(after(first_send, dn_x), "x", 1)
    first_ck, first_cx = swap(first_keep, "c", 1), swap(first_x, "c", 1)
    from_own = jnp.where(ci == 1, first_keep[:, :HG], first_ck[:, HG:])
    from_other = jnp.where(ci == 1, first_x[:, :HG], first_cx[:, HG:])
    first_back = jnp.where(
        xi == 0,
        jnp.concatenate([from_own, from_other], -1),
        jnp.concatenate([from_other, from_own], -1),
    )
    back = jnp.concatenate([mixed, first_back], -1).reshape(count, block, D + DV)
    back = direct(after(list(back), *gt[1:]), "s")
    home_tie = back[1:]
    back = in_place(back, "s")[None]
    mixed_out, grad_first = back[..., :D], back[..., D:]

    def sum_q(value):
        return scatter_sum(value, "q")

    e_home = sum_q(sum(part.astype(F32) for part in after(tuple(e_got), dn_x)))
    r_home = sum_q(sum(part.astype(F32) for part in r_got)).reshape(GROUP * rw, cw)

    def to_group(part):
        part = part.astype(BF)
        keep = lax.dynamic_index_in_dim(part, ci, 1, keepdims=False)
        got = swap(lax.dynamic_index_in_dim(part, ci ^ 1, 1, keepdims=False), "c", 1)
        both = jnp.stack([keep, got], 1)
        return pick(both, xi), swap(pick(both, xi ^ 1), "x", 1)

    e_home = call(
        functools.partial(units_home_body, blocks_y),
        [shape((rw, FF // nb), F32)],
        [],
        0,
        *to_group(e_home.reshape(2, 2, rw, cw)),
    )[0]

    p_from_c = swap(p_send, "c", 1)
    p_from_x = swap(after(jnp.stack([p_keep[1], p_from_c[1]]), dn_x), "x", 1)
    flat = [v.reshape(-1, rw, 3 * HG) for v in (p_keep[0], p_from_c[0], p_from_x[0], p_from_x[1])]
    home_cols = 2 * cw + DV // nb
    n_rows = count * part_q
    y_low, y_high = call(
        functools.partial(columns_home_body, nb, n_rows),
        [shape((nb // 2, n_rows, rw, home_cols), F32), shape((nb // 2, n_rows, rw, home_cols))],
        [pltpu.VMEM((nb, rw, home_cols), F32)],
        0,
        *flat,
    )
    qkv_part = scatter_slots(y_low, y_high, "y").reshape(count, part_q, rw, home_cols)
    o_part = jnp.moveaxis(o_part, 2, 0)
    o_part = scatter_slots(o_part[:1], after(o_part[1:], dn_x), "x")
    home = after(jnp.concatenate([qkv_part, o_part], -1), *home_tie)
    home = sum_q(direct_sum(home, "s"))
    q_home, k_home, v_home = home[:, :cw], home[:, cw : 2 * cw], home[:, 2 * cw : home_cols]
    o_home = home[:, home_cols:]

    sums = jnp.concatenate([sums_one, sums_qv, sums_two], 0)
    for axis in ("c", "x", "y", "q", "s"):
        sums = whole_sum(sums, axis)
    place = ((si * part_q + qi) * 2 + xi) * 2 + ci
    part = lax.dynamic_slice_in_dim(sums[:8], place * rw, rw, 1)
    vb_home = lax.dynamic_slice_in_dim(sums[3], place * (DV // cycle), DV // cycle, 0)
    eb_home = pick(sums[8:].reshape(cycle, -1), place)
    return (
        mixed_out,
        grad_tokens,
        grad_first,
        part[0],
        part[1],
        q_home,
        part[2],
        k_home,
        v_home,
        vb_home,
        o_home,
        part[4],
        part[5],
        part[6],
        e_home,
        eb_home,
        r_home,
        part[7],
    )


def solution(mesh):
    cycle, nb = mesh.devices.shape
    sequences = 4
    fine = Mesh(
        mesh.devices.reshape(sequences, cycle // (sequences * GROUP), 2, 2, nb),
        ("s", "q", "x", "c", "y"),
    )
    seq = ("s", "q", "x", "c")
    rows = P("y", None, seq, None)
    matrix = P(seq, "y")
    vector = P(seq)
    in_specs = (
        rows,
        rows,
        P("y", None),
        rows,
        vector,
        vector,
        matrix,
        vector,
        matrix,
        matrix,
        vector,
        matrix,
        vector,
        vector,
        vector,
        matrix,
        vector,
        matrix,
        vector,
    )
    out_specs = (
        rows,
        rows,
        rows,
        vector,
        vector,
        matrix,
        vector,
        matrix,
        matrix,
        vector,
        matrix,
        vector,
        vector,
        vector,
        matrix,
        vector,
        matrix,
        vector,
    )
    return jax.shard_map(
        on_device, mesh=fine, in_specs=in_specs, out_specs=out_specs, check_vma=False
    )
```

```python
import enum
import functools

import jax
import jax.numpy as jnp
from jax import lax
from jax.experimental import pallas as pl
from jax.experimental.pallas import tpu as pltpu
from jax.sharding import Mesh, PartitionSpec as P

D = 768
H = 12
HD = 64
FF = 3072
DV = 384
GROUP = 4
HG = D // GROUP
HEADS = HG // HD
UG = FF // GROUP
WIDE = 1024

EPS = 1e-05
NEG = -1e30
SCALE = HD**-0.5
BF = jnp.bfloat16
F32 = jnp.float32
VMEM = pl.BlockSpec(memory_space=pltpu.VMEM)
SMEM = pl.BlockSpec(memory_space=pltpu.SMEM)


def gray(k):
    return k ^ (k >> 1)


def swap(value, axis, mask):
    return lax.ppermute(value, axis, [(i, i ^ mask) for i in range(lax.axis_size(axis))])


def pick(blocks, index):
    return lax.dynamic_index_in_dim(blocks, index, 0, keepdims=False)


def after(value, *others):
    return lax.optimization_barrier((value, *others))[0]


class Step(enum.IntEnum):
    attend = enum.auto()
    attend_back = enum.auto()
    attend_x = enum.auto()
    columns_grad_x = enum.auto()
    columns_home = enum.auto()
    columns_part = enum.auto()
    columns_sent = enum.auto()
    columns_x = enum.auto()
    cores = enum.auto()
    cotangent = enum.auto()
    cotangent_part = enum.auto()
    d_attended_c = enum.auto()
    d_attended_x = enum.auto()
    d_normed_c = enum.auto()
    d_normed_x = enum.auto()
    d_second_c = enum.auto()
    d_second_x = enum.auto()
    expand_home = enum.auto()
    expand_part = enum.auto()
    expand_y = enum.auto()
    expand_z = enum.auto()
    feed = enum.auto()
    feed_far = enum.auto()
    feed_most_y = enum.auto()
    feed_part = enum.auto()
    feed_piece = enum.auto()
    feed_three = enum.auto()
    feed_three_y = enum.auto()
    feed_two = enum.auto()
    home = enum.auto()
    mask = enum.auto()
    middle = enum.auto()
    mixed_c = enum.auto()
    mixed_out = enum.auto()
    mixed_part = enum.auto()
    mixed_rows = enum.auto()
    mixed_x = enum.auto()
    mixed_z = enum.auto()
    normed_back = enum.auto()
    output = enum.auto()
    output_c = enum.auto()
    output_grad = enum.auto()
    output_wide = enum.auto()
    output_x = enum.auto()
    output_y = enum.auto()
    project = enum.auto()
    project_grad = enum.auto()
    reduce = enum.auto()
    reduce_home = enum.auto()
    reduce_part = enum.auto()
    reduce_y = enum.auto()
    reduce_z = enum.auto()
    second_x = enum.auto()
    sums = enum.auto()
    tokens = enum.auto()
    tokens_back = enum.auto()
    tokens_c = enum.auto()
    tokens_near = enum.auto()
    tokens_x = enum.auto()
    tokens_z = enum.auto()
    upstream = enum.auto()
    upstream_x = enum.auto()


PLAN = {
    Step.feed_two: ((), None),
    Step.output_x: ((Step.tokens_x,), Step.attend),
    Step.output_c: ((Step.output_wide,), None),
    Step.tokens_c: ((Step.columns_x,), None),
    Step.feed_three: ((Step.attend_x,), Step.attend),
    Step.cotangent: ((Step.project,), None),
    Step.feed_most_y: ((Step.attend_x,), None),
    Step.feed_three_y: ((), None),
    Step.mask: ((), None),
    Step.upstream_x: ((), None),
    Step.expand_y: ((), None),
    Step.mixed_c: ((Step.d_second_c,), Step.middle),
    Step.expand_z: ((Step.middle,), Step.normed_back),
    Step.reduce_y: ((Step.middle,), None),
    Step.mixed_x: ((Step.d_attended_x,), Step.normed_back),
    Step.output_grad: ((Step.d_normed_c,), None),
    Step.reduce_z: ((Step.attend_back,), Step.tokens_back),
    Step.mixed_z: ((Step.attend_back,), None),
    Step.columns_grad_x: ((), None),
    Step.tokens_z: ((), None),
    Step.output_y: ((), None),
    Step.mixed_out: ((Step.home,), None),
    Step.expand_home: ((Step.tokens_z,), None),
    Step.reduce_home: ((Step.tokens_z,), None),
    Step.sums: ((Step.home,), None),
    Step.output_wide: ((Step.output_x,), None),
}
EARLY = {
    Step.upstream: Step.output,
    Step.reduce: Step.middle,
    Step.expand_part: None,
    Step.mixed_part: Step.attend_back,
    Step.reduce_part: Step.normed_back,
    Step.mixed_rows: Step.normed_back,
    Step.columns_part: None,
    Step.feed_part: Step.attend,
    Step.cotangent_part: Step.attend,
    Step.columns_sent: None,
    Step.feed_piece: Step.cores,
    Step.tokens_near: None,
}


class Tie:
    def __init__(self, values):
        self.values = values

    def __call__(self, value):
        return after(value, *self.values) if self.values else value


class Steps:
    def __init__(self):
        self.reached, self.waiting, self.due = {}, {}, {}

    def reach(self, name, value):
        self.reached[name] = value
        for name, start in list(self.waiting.items()):
            self.begin(name, start)

    def at(self, name):
        return [self.reached[step] for step in PLAN[name][0]]

    def begin(self, name, start):
        if all(step in self.reached for step in PLAN[name][0]):
            self.waiting.pop(name, None)
            self.reached[name] = None
            result = start(Tie(self.at(name)))
            self.reached[name] = jax.tree.leaves(result)[-1]
            self.due.setdefault(PLAN[name][1], []).extend(jax.tree.leaves(result))
            self.results[name] = result
            for other, begin in list(self.waiting.items()):
                self.begin(other, begin)

    results = None

    def move(self, name, start):
        if self.results is None:
            self.results = {}
        self.waiting[name] = start
        self.begin(name, start)
        return lambda: self.results[name]

    def need(self, name, value):
        self.due.setdefault(EARLY.get(name), []).extend(jax.tree.leaves(value))

    def before(self, name, value):
        due = self.due.pop(name, [])
        return after(value, *due) if due else value


def relative(blocks, axis):
    n = lax.axis_size(axis)
    if n == 1:
        return blocks
    me = lax.axis_index(axis)
    return jnp.stack([pick(blocks, gray(r) ^ me) for r in range(n)], 0)


def absolute(rel, axis):
    n = lax.axis_size(axis)
    if n == 1:
        return rel
    me = lax.axis_index(axis)
    return jnp.stack([pick(rel, gray(a ^ me)) for a in range(n)], 0)


def gather_list(value, axis):
    pieces = [(value[None], [0])]
    size = 1
    while size < lax.axis_size(axis):
        held = pieces[0][0] if size == 1 else jnp.concatenate([p for p, unused in pieces], 0)
        pieces.append((swap(held, axis, gray(size)), list(range(size, 2 * size))))
        size *= 2
    return pieces


def gather(value, axis):
    return absolute(jnp.concatenate([p for p, unused in gather_list(value, axis)], 0), axis)


def direct(parts, axis):
    return [parts[0]] + [swap(parts[k], axis, k) for k in range(1, len(parts))]


def in_place(parts, axis):
    held = jnp.stack(parts)
    me = lax.axis_index(axis)
    return jnp.stack([pick(held, a ^ me) for a in range(len(parts))])


def direct_sum(rel, axis):
    got = direct([rel[0].astype(F32)] + [rel[k].astype(BF) for k in range(1, rel.shape[0])], axis)
    return sum(part.astype(F32) for part in got)


def scatter_slots(low, high, axis, got=None):
    while True:
        half = low.shape[0]
        if got is None:
            got = swap(high.astype(BF), axis, gray(half))
        total = low.astype(F32) + got.astype(F32)
        got = None
        if half == 1:
            return total[0]
        low, high = total[: half // 2], total[half // 2 :]


def scatter_sum(rel, axis):
    half = rel.shape[0] // 2
    return rel[0] if half == 0 else scatter_slots(rel[:half], rel[half:], axis)


def exchange(blocks, axis):
    n = lax.axis_size(axis)
    rel = relative(blocks, axis)
    bit = 1
    while bit < n:
        shape = rel.shape
        pairs = rel.reshape((n // (2 * bit), 2, bit) + shape[1:])
        got = swap(pairs[:, 1], axis, gray(bit))
        rel = jnp.stack([pairs[:, 0], got], 1).reshape(shape)
        bit *= 2
    return absolute(rel, axis)


def whole_sum(value, axis):
    n = lax.axis_size(axis)
    bit = 1
    while bit < n:
        value = value + swap(value, axis, bit)
        bit *= 2
    return value


def norm_parts(values):
    centre = values - jnp.mean(values, -1, keepdims=True)
    spread = lax.rsqrt(jnp.mean(centre * centre, -1, keepdims=True) + EPS)
    return centre * spread, spread


def norm_back(d_out, gain, xhat, spread):
    e = d_out * gain
    return spread * (
        e - jnp.mean(e, -1, keepdims=True) - xhat * jnp.mean(e * xhat, -1, keepdims=True)
    )


def dot(a, b):
    return jnp.dot(a, b, preferred_element_type=F32)


def dot_nt(a, b):
    return lax.dot_general(a, b, (((1,), (1,)), ((), ())), preferred_element_type=F32)


def dot_tn(a, b):
    return lax.dot_general(a, b, (((0,), (0,)), ((), ())), preferred_element_type=F32)


def places():
    return tuple(lax.axis_index(a) for a in ("s", "q", "x", "c", "y"))


def merged(blocks):
    n, rows, cols = blocks.shape
    if rows % 16 == 0:
        return blocks.reshape(n * rows, cols)
    return blocks.astype(F32).reshape(n * rows, cols).astype(BF)


def split_rows(rows, n):
    size = rows.shape[0] // n
    if size % 16 == 0:
        return [rows[i * size : (i + 1) * size] for i in range(n)]
    wide = rows.astype(F32)
    return [wide[i * size : (i + 1) * size].astype(BF) for i in range(n)]


def shape(dims, kind=BF):
    return jax.ShapeDtypeStruct(tuple(dims), kind)


def call(body, outs, scratch, *operands, smem=0, mib=24):
    arrays = operands[smem:]
    n, n_out = len(arrays), len(outs)
    def copied(*refs):
        scalars, sources = refs[:smem], refs[smem : smem + n]
        results = refs[smem + n : smem + n + n_out]
        own = refs[smem + n + n_out : len(refs) - n - 1]
        held, sems = refs[len(refs) - n - 1 : -1], refs[-1]
        copies = [
            pltpu.make_async_copy(sources[i], held[i], sems.at[i]) for i in range(n)
        ]
        for copy in copies:
            copy.start()
        for copy in copies:
            copy.wait()
        body(*scalars, *held, *results, *own)

    return pl.pallas_call(
        copied,
        out_shape=tuple(outs),
        in_specs=[SMEM] * smem + [pl.BlockSpec(memory_space=pl.ANY)] * n,
        out_specs=tuple(VMEM for unused in outs),
        scratch_shapes=[*scratch]
        + [pltpu.VMEM(v.shape, v.dtype) for v in arrays]
        + [pltpu.SemaphoreType.DMA((n,))],
        cost_estimate=pl.CostEstimate(flops=1, bytes_accessed=1, transcendentals=0),
        compiler_params=pltpu.CompilerParams(vmem_limit_bytes=mib * 1024 * 1024),
    )(*operands)


def pack_rows_body(nb, query, keys, values, output, *refs):
    vectors = refs[:9]
    out, rows = refs[9:]
    cw, vw = D // nb, DV // nb
    out[:, :cw] = query[...]
    out[:, cw : 2 * cw] = keys[...]
    out[:, 2 * cw : 3 * cw] = output[...]
    out[:, 3 * cw : 3 * cw + vw] = values[...]
    rows[...] = jnp.zeros_like(rows)
    for j, vector in enumerate(vectors):
        size = vector.shape[0]
        rows[j : j + 1, :size] = vector[...].astype(F32).reshape(1, size)
    out[:, 3 * cw + vw :] = rows[...].astype(BF)


def own_columns_body(nb, n_own, *refs):
    owns = refs[:n_own]
    keep, send, out, rows = refs[n_own:]
    si, qi, xi, ci, yi = places()
    cw, vw = D // nb, DV // nb
    per = owns[0].shape[0]
    kept, sent = [], []
    rows[...] = jnp.zeros_like(rows)
    for j in range(n_own):
        for q in range(per):
            held = owns[j][q].astype(F32)
            out[j * per + q] = owns[j][q, :, 2 * cw : 3 * cw]
            values = held[:, 3 * cw : 3 * cw + vw]
            parts = [
                jnp.concatenate([held[:, x * HG : (x + 1) * HG], held[:, cw + x * HG : cw + (x + 1) * HG]], 1)
                for x in range(2)
            ]
            kept.append(jnp.concatenate([jnp.where(xi == 0, *parts), values], 1))
            sent.append(jnp.concatenate([jnp.where(xi == 0, *parts[::-1]), values], 1))
            for v in range(9):
                at = 3 * (j * per + q) + v // 3
                start = 3 * cw + vw
                rows[at : at + 1, (v % 3) * HG : (v % 3 + 1) * HG] = held[v : v + 1, start : start + HG]
    keep[...] = jnp.concatenate(kept + [rows[...]], 0).astype(BF)
    send[...] = jnp.concatenate(sent + [rows[...]], 0).astype(BF)


def both_rows_body(mine, from_x, out):
    out[0] = mine[: out.shape[1], :]
    out[1] = from_x[: out.shape[1], :]


def own_cores_body(mine, from_x, both, from_y, keep, send):
    si, qi, xi, ci, yi = places()
    size = both.shape[1]
    kept, sent = [], []
    for rx in range(2):
        own, other = both[rx].astype(F32), from_y[rx].astype(F32)
        halves = [jnp.where(yi == y, own, other) for y in range(2)]
        values = jnp.where(xi == 0, halves[0][:, 2 * HG :], halves[1][:, 2 * HG :])
        columns = [half[:, : 2 * HG] for half in halves]
        kept.append(jnp.concatenate([jnp.where(ci == 0, *columns), values], 1))
        sent.append(jnp.concatenate([jnp.where(ci == 0, *columns[::-1]), values], 1))
    vectors = [ref[size:, :].astype(F32) for ref in (mine, from_x)]
    keep[...] = jnp.concatenate(kept + vectors, 0).astype(BF)
    send[...] = jnp.concatenate(sent + vectors, 0).astype(BF)


def pack_columns_body(nb, rw, n_own, y_slots, *refs):
    owns = refs[:n_own]
    pieces = refs[n_own : n_own + len(y_slots)]
    keep, send, out, scr, rows = refs[n_own + len(y_slots) :]
    si, qi, xi, ci, yi = places()
    cw, vw = D // nb, DV // nb
    per = owns[0].shape[0]
    n2 = n_own * per
    width = 3 * cw + vw
    rows[...] = jnp.zeros_like(rows)
    for j in range(n_own):
        scr[yi, j * per : (j + 1) * per] = owns[j][:, :, :width]
        out[0, j * per : (j + 1) * per] = owns[j][:, :, 2 * cw : 3 * cw]
        for q in range(per):
            held = owns[j][q, :, width:].astype(F32)
            for v in range(9):
                at = 3 * (j * per + q) + v // 3
                rows[at : at + 1, (v % 3) * HG : (v % 3 + 1) * HG] = held[v : v + 1]
    for ref, slots in zip(pieces, y_slots):
        for at, ry in enumerate(slots):
            scr[yi ^ gray(ry)] = ref[at]
            out[ry] = ref[at, :, :, 2 * cw : 3 * cw]
    both = ([], [])
    for n in range(n2):
        full = [
            jnp.concatenate([scr[y, n][:, a : a + w].astype(F32) for y in range(nb)], 1)
            for a, w in ((0, cw), (cw, cw), (3 * cw, vw))
        ]

        def part(x, c):
            cols = [v[:, (2 * c + x) * HG : (2 * c + x + 1) * HG] for v in full[:2]]
            return jnp.concatenate(cols + [full[2][:, x * HG : (x + 1) * HG]], 1)

        for c in range(2):
            one, two = part(0, c), part(1, c)
            both[c].append((jnp.where(xi == 0, one, two), jnp.where(xi == 0, two, one)))
    for which, ref in ((0, keep), (1, send)):
        parts = [pair[which] for c in range(2) for pair in both[c]] + [rows[...]]
        ref[...] = jnp.concatenate(parts, 0).astype(BF)


def pack_cores_body(vec_rows, mine, from_x, keep, send):
    si, qi, xi, ci, yi = places()
    half = (mine.shape[0] - vec_rows) // 2
    parts = [], []
    for ref in (mine, from_x):
        a, b = ref[:half].astype(F32), ref[half : 2 * half].astype(F32)
        parts[0].append(jnp.where(ci == 0, a, b))
        parts[1].append(jnp.where(ci == 0, b, a))
    vectors = [ref[2 * half :].astype(F32) for ref in (mine, from_x)]
    keep[...] = jnp.concatenate(parts[0] + vectors, 0).astype(BF)
    send[...] = jnp.concatenate(parts[1] + vectors, 0).astype(BF)


def vectors_body(slots, part_q, rw, cycle, *refs):
    pieces = refs[: 2 * len(slots)]
    gain_one, shift_one, q_bias, v_bias, o_bias, gain_two, shift_two, r_bias, e_bias, scr = refs[
        2 * len(slots) :
    ]
    si, qi, xi, ci, yi = places()
    for stage, marks in enumerate(slots):
        for rc in range(2):
            for rx in range(2):
                ref = pieces[2 * stage + rc]
                size = (3 * len(marks) + 15) // 16 * 16
                at = ref.shape[0] - (2 - rx) * size
                rows = ref[at : at + size].astype(F32)
                for at, (rs, rq) in enumerate(marks):
                    place = ((si ^ rs) * part_q + (qi ^ gray(rq))) * GROUP
                    place = place + 2 * (xi ^ rx) + (ci ^ rc)
                    scr[pl.ds(place, 1), 0:3] = rows[3 * at : 3 * at + 3][None]

    def whole(j, size):
        held = scr[:, j // 3, (j % 3) * HG : (j % 3) * HG + size]
        wide = cycle * size
        lane = lax.broadcasted_iota(jnp.int32, (size, wide), 1)
        row = lax.broadcasted_iota(jnp.int32, (size, wide), 0)
        spread = jnp.where(lane % size == row, 1.0, 0.0).astype(BF)
        out = dot(held.astype(BF), spread)
        mark = lax.broadcasted_iota(jnp.int32, (cycle, wide), 1) // size
        row = lax.broadcasted_iota(jnp.int32, (cycle, wide), 0)
        return jnp.sum(jnp.where(mark == row, out, 0.0), 0, keepdims=True)

    for j, ref in ((0, gain_one), (1, shift_one), (4, o_bias), (5, gain_two), (6, shift_two), (7, r_bias)):
        ref[...] = whole(j, rw)
    query = whole(2, rw)
    group = 2 * ci + xi
    total = jnp.zeros((1, HG), F32)
    for g in range(GROUP):
        total = total + jnp.where(group == g, query[:, g * HG : (g + 1) * HG], 0.0)
    q_bias[...] = total
    value = whole(3, DV // cycle)
    v_bias[...] = jnp.where(xi == 0, value[:, :HG], value[:, HG:])
    unit = FF // cycle
    parts = []
    for j in range(cycle // GROUP):
        held = scr[j * GROUP + 2 * xi + ci]
        parts.append(held[2:3, 2 * HG : 2 * HG + unit])
    e_bias[...] = jnp.concatenate(parts, 1)


def pack_units_body(nb, blocks_y, expand, keep, send):
    si, qi, xi, ci, yi = places()
    unit = FF // (blocks_y * GROUP * nb)

    def part(x, c):
        cols = [expand[:, (GROUP * b + 2 * x + c) * unit : (GROUP * b + 2 * x + c + 1) * unit] for b in range(blocks_y)]
        return jnp.concatenate([v.astype(F32) for v in cols], 1)

    for c in range(2):
        one, two = part(0, c), part(1, c)
        keep[c] = jnp.where(xi == 0, one, two).astype(BF)
        send[c] = jnp.where(xi == 0, two, one).astype(BF)


def units_home_body(blocks_y, mine, other, out):
    si, qi, xi, ci, yi = places()
    unit = mine.shape[2] // blocks_y
    for b in range(blocks_y):
        for g in range(GROUP):
            total = jnp.zeros((mine.shape[1], unit), F32)
            for rx, ref in ((0, mine), (1, other)):
                for rc in range(2):
                    here = 2 * (xi ^ rx) + (ci ^ rc) == g
                    part = ref[rc, :, b * unit : (b + 1) * unit].astype(F32)
                    total = total + jnp.where(here, part, 0.0)
            at = (GROUP * b + g) * unit
            out[:, at : at + unit] = total


def columns_home_body(nb, n, keep, from_c, x_keep, x_from_c, low, high, scr):
    si, qi, xi, ci, yi = places()
    cw, vw = D // nb, DV // nb
    sources = ((0, 0, keep), (0, 1, from_c), (1, 0, x_keep), (1, 1, x_from_c))
    for s in range(n):
        full = []
        for kind in range(3):
            groups = []
            for g in range(GROUP if kind < 2 else 2):
                total = jnp.zeros((keep.shape[1], HG), F32)
                for rx, rc, ref in sources:
                    here = 2 * (ci ^ rc) + (xi ^ rx) == g
                    part = ref[s, :, kind * HG : (kind + 1) * HG].astype(F32)
                    total = total + jnp.where(here, part, 0.0)
                groups.append(total)
            full.append(jnp.concatenate(groups, 1))
        for y in range(nb):
            scr[y] = jnp.concatenate(
                [
                    full[0][:, y * cw : (y + 1) * cw],
                    full[1][:, y * cw : (y + 1) * cw],
                    full[2][:, y * vw : (y + 1) * vw],
                ],
                1,
            )
        for ry in range(nb):
            to = low if ry < nb // 2 else high
            to[ry % (nb // 2), s] = scr[yi ^ gray(ry)].astype(to.dtype)


def project_body(slots, count, part_q, block, rw, *refs):
    n_pieces = 2 * len(slots)
    sources = refs[:6]
    pieces = refs[6 : 6 + n_pieces]
    gain, shift, q_bias, v_bias = refs[6 + n_pieces : 10 + n_pieces]
    query, keys, values, normed, weight, scr_w, scr_f = refs[10 + n_pieces :]
    si, qi, xi, ci, unused = places()
    for stage, marks in enumerate(slots):
        for at, (rs, rq) in enumerate(marks):
            base = ((si ^ rs) * part_q + (qi ^ gray(rq))) * GROUP
            for rc in range(2):
                ref = pieces[2 * stage + rc]
                n2 = len(marks)
                held = split_rows(ref[: 2 * n2 * rw], 2 * n2)
                for rx in range(2):
                    place = base + 2 * (xi ^ rx) + (ci ^ rc)
                    scr_w[pl.ds(place, 1)] = held[rx * n2 + at][None]
    weight[...] = merged(scr_w[...])
    for pair in range(4):
        rx, rc = pair % 2, pair // 2
        for r in range(count):
            held = sources[3 * rc : 3 * rc + 3]
            here = held[0][r] if rx == 0 else held[1 + r // 2][r % 2]
            at = (((si ^ r) * 2 + (xi ^ rx)) * 2 + (ci ^ rc)) * block
            at = pl.multiple_of(at, block)
            xhat, unused = norm_parts(here[:, :D].astype(F32))
            normed[pl.ds(at, block), :] = (xhat * gain[...] + shift[...]).astype(BF)
            scr_f[pl.ds(at, block), :] = here[:, D : D + HG]
    rows = GROUP * block
    for i in range(count):
        span = slice(i * rows, (i + 1) * rows)
        out = dot(normed[span, :], weight[...])
        q_low = (out[:, :HG] + q_bias[...]).astype(BF) * SCALE
        k_low = out[:, HG : 2 * HG].astype(BF)
        v_low = (out[:, 2 * HG :] + v_bias[...]).astype(BF)
        v_low = jnp.where(ci == 0, v_low, scr_f[span, :])
        for h in range(HEADS):
            cols = slice(h * HD, (h + 1) * HD)
            query[h, span, :] = q_low[:, cols].astype(BF)
            keys[h, span, :] = k_low[:, cols]
            values[h, span, :] = v_low[:, cols]


def allowed_at(i, rows, width, part_q, length):
    unused, qi, *unused = places()
    row_pos = (i * part_q + qi) * rows + lax.broadcasted_iota(jnp.int32, (1, rows), 1)
    last = jnp.minimum(row_pos, length - 1)
    return lax.broadcasted_iota(jnp.int32, (width, rows), 0) <= last


def attend_body(count, part_q, block, lengths, query, keys, values, att, lse, keep, send, scr):
    si, qi, xi, ci, unused = places()
    length = lengths[0, si]
    rows = GROUP * block
    for i in range(count):
        span = slice(i * rows, (i + 1) * rows)
        width = (i + 1) * part_q * rows
        allowed = allowed_at(i, rows, width, part_q, length)
        outs = []
        for h in range(HEADS):
            scores = dot_nt(keys[h, :width, :], query[h, span, :])
            scores = jnp.where(allowed, scores, NEG)
            peak = jnp.max(scores, 0, keepdims=True)
            weights = jnp.exp(scores - peak)
            total = jnp.sum(weights, 0, keepdims=True)
            out = dot_tn(values[h, :width, :], weights.astype(BF)) * (1.0 / total)
            att[h, :, span] = out
            lse[i * HEADS + h : i * HEADS + h + 1, :] = peak + jnp.log(total)
            outs.append(out)
        scr[span, :] = jnp.concatenate(outs, 0).T.astype(BF)
    for rx, to in ((0, keep), (1, send)):
        for rc in range(2):
            for r in range(count):
                at = (((si ^ r) * 2 + (xi ^ rx)) * 2 + (ci ^ rc)) * block
                to[r * block : (r + 1) * block, rc * HG : (rc + 1) * HG] = scr[
                    pl.ds(pl.multiple_of(at, block), block), :
                ]


def mask_body(part_q, block, lengths, *refs):
    parts, out = refs[:-1], refs[-1]
    si, qi, xi, ci, unused = places()
    for r, part in enumerate(parts):
        start = (((si ^ r) * part_q + qi) * GROUP + 2 * xi + ci) * block
        row = start + lax.broadcasted_iota(jnp.int32, (block, 1), 0)
        here = jnp.where(row < lengths[0, si], part[...].astype(F32), 0.0)
        out[r * block : (r + 1) * block, :] = here.astype(BF)


def output_body(
    slots, count, part_q, block, nb, rw, tok, keep, from_x, from_ck, from_cx, *refs
):
    pieces = refs[:2]
    bias, gain, shift, middle, second, weight, scr = refs[2:]
    si, qi, xi, ci, yi = places()
    for stage, marks in enumerate(slots):
        for rc in range(2):
            for rx in range(2):
                for at, (rs, rq) in enumerate(marks):
                    place = ((si ^ rs) * part_q + (qi ^ gray(rq))) * GROUP
                    place = place + 2 * (xi ^ rx) + (ci ^ rc)
                    for ry in range(nb):
                        scr[yi ^ gray(ry), pl.ds(place, 1)] = pieces[rc][rx, ry, at][None]
    for y in range(nb):
        cw = D // nb
        weight[:, y * cw : (y + 1) * cw] = merged(scr[y])
    tokens = [tok[r][:, :D].astype(F32) for r in range(count)]
    total = jnp.concatenate(tokens, 0) + bias[...]
    for ref, lanes, rx, rc in ((keep, 0, 0, 0), (from_x, 0, 1, 0), (from_ck, 1, 0, 1), (from_cx, 1, 1, 1)):
        group = 2 * (ci ^ rc) + (xi ^ rx)
        rows = weight[pl.ds(pl.multiple_of(group * HG, HG), HG), :]
        total = total + dot(ref[:, lanes * HG : (lanes + 1) * HG], rows)
    middle[...] = total
    xhat, unused = norm_parts(total)
    second[...] = (xhat * gain[...] + shift[...]).astype(BF)


def feed_weights(slots, part_q, nb, pieces, scr_e, scr_r, e_w, r_w):
    si, qi, xi, ci, yi = places()
    for ref, marks in zip(pieces, slots):
        for at, (ry, rs, rq) in enumerate(marks):
            base = ((si ^ rs) * part_q + (qi ^ gray(rq))) * GROUP
            y = yi ^ gray(ry)
            for inner in range(GROUP):
                place = base + 2 * (xi ^ (inner % 2)) + (ci ^ (inner // 2))
                scr_e[y, pl.ds(place, 1)] = ref[at, inner][None]
            scr_r[y, pl.ds(base, GROUP)] = ref[at, GROUP : 2 * GROUP]
    cw = D // nb
    for y in range(nb):
        e_w[:, y * cw : (y + 1) * cw] = merged(scr_e[y])
        r_w[:, y * cw : (y + 1) * cw] = merged(scr_r[y])


def feed_rows(here, up, bias, e_w, r_w):
    hidden = dot(here, e_w[...]) + bias[...]
    k0 = 0.7978845608028654
    square = hidden * hidden
    tanh = jnp.tanh(k0 * hidden * (1.0 + 0.044715 * square))
    half = 0.5 * (1.0 + tanh)
    active = (hidden * half).astype(BF)
    slope = half + 0.5 * k0 * hidden * (1.0 - tanh * tanh) * (1.0 + 3 * 0.044715 * square)
    d_hidden = (dot_nt(up, r_w[...]) * slope).astype(BF)
    return active, d_hidden, dot(active, r_w[...]), dot_nt(d_hidden, e_w[...])


def feed_blocks(own, from_c, up, up_c, bias, e_w, r_w, start, outs):
    mx_keep, mx_send, ds_keep, ds_send, acts, dhs, eb = outs
    rows = own.shape[0]
    total = start
    for b, (here, upper) in enumerate(((own, up), (from_c, up_c))):
        active, d_hidden, mixed, d_second = feed_rows(here[...], upper[...], bias, e_w, r_w)
        acts[b * rows : (b + 1) * rows, :] = active
        dhs[b * rows : (b + 1) * rows, :] = d_hidden
        total = total + jnp.sum(d_hidden.astype(F32), 0, keepdims=True)
        if b == 0:
            mx_keep[...] = mixed
            ds_keep[...] = d_second
        else:
            mx_send[...] = mixed.astype(BF)
            ds_send[...] = d_second.astype(BF)
    eb[...] = total


def feed_near_body(slots, part_q, nb, own, from_c, up, up_c, *refs):
    n = len(slots)
    pieces, bias = refs[:n], refs[n]
    outs, (e_w, r_w, scr_e, scr_r) = refs[n + 1 : n + 8], refs[n + 8 :]
    feed_weights(slots, part_q, nb, pieces, scr_e, scr_r, e_w, r_w)
    start = jnp.zeros((1, UG), F32)
    feed_blocks(own, from_c, up, up_c, bias, e_w, r_w, start, outs)


def feed_far_body(own, from_c, up, up_c, bias, e_w, r_w, near_eb, *outs):
    feed_blocks(own, from_c, up, up_c, bias, e_w, r_w, near_eb[...], outs)


def feed_grad_body(count, part_q, nb, rw, n_left, n_right, *refs):
    left, right = refs[:n_left], refs[n_left : n_left + n_right]
    low, high, all_left, all_right, scr = refs[n_left + n_right :]
    si, qi, xi, ci, yi = places()
    cw = D // nb
    for parts, held in ((left, all_left), (right, all_right)):
        at = 0
        for part in parts:
            held[at : at + part.shape[0], :] = part[...]
            at += part.shape[0]
    for y in range(nb):
        scr[y] = dot_tn(all_left[...], all_right[:, y * cw : (y + 1) * cw])
    for ry in range(nb):
        to = low if ry < nb // 2 else high
        for rs in range(count):
            for rq in range(part_q):
                at = ((si ^ rs) * part_q + (qi ^ gray(rq))) * GROUP * rw
                part = scr[yi ^ gray(ry), pl.ds(pl.multiple_of(at, GROUP * rw), GROUP * rw), :]
                to[ry % (nb // 2), rs, rq] = part.reshape(GROUP, rw, cw).astype(BF)


def middle_back_body(
    cycle, ds_keep, from_c, from_x, upstream, middle, gain, weight, eb, d_middle, d_branch, keep, send, sums
):
    si, qi, xi, ci, yi = places()
    unit = FF // cycle
    parts = []
    for j in range(cycle // GROUP):
        part = eb[:, j * unit : (j + 1) * unit]
        for g in range(GROUP):
            parts.append(jnp.where(2 * xi + ci == g, part, jnp.zeros_like(part)))
    for j in range(FF // D):
        per = len(parts) * D // FF
        sums[4 + j : 5 + j, :] = jnp.concatenate(parts[j * per : (j + 1) * per], 1)
    d_second = ds_keep[...] + from_c[0].astype(F32) + from_x[...].astype(F32)
    xhat, spread = norm_parts(middle[...])
    up = upstream[...].astype(F32)
    total = up + norm_back(d_second, gain[...], xhat, spread)
    d_middle[...] = total
    low = total.astype(BF)
    d_branch[...] = low
    sums[0:1, :] = jnp.sum(low.astype(F32), 0, keepdims=True)
    sums[1:2, :] = jnp.sum(d_second * xhat, 0, keepdims=True)
    sums[2:3, :] = jnp.sum(d_second, 0, keepdims=True)
    sums[3:4, :] = jnp.sum(up, 0, keepdims=True)
    for rx, to in ((0, keep), (1, send)):
        for rc in range(2):
            group = 2 * (ci ^ rc) + (xi ^ rx)
            rows = weight[pl.ds(pl.multiple_of(group * HG, HG), HG), :]
            to[:, rc * HG : (rc + 1) * HG] = dot_nt(low, rows).astype(BF)


def output_grad_body(count, part_q, nb, rw, keep, from_x, from_ck, from_cx, d_branch, low, high, scr):
    si, qi, xi, ci, yi = places()
    cw = D // nb
    for ref, lanes, rx, rc in ((keep, 0, 0, 0), (from_x, 0, 1, 0), (from_ck, 1, 0, 1), (from_cx, 1, 1, 1)):
        group = 2 * (ci ^ rc) + (xi ^ rx)
        grad = dot_tn(ref[:, lanes * HG : (lanes + 1) * HG], d_branch[...])
        for y in range(nb):
            part = grad[:, y * cw : (y + 1) * cw].reshape(HG // rw, rw, cw)
            scr[y, pl.ds(group * (HG // rw), HG // rw)] = part
    for rc, to in ((0, low), (1, high)):
        for ry in range(nb):
            for rs in range(count):
                for rq in range(part_q):
                    base = ((si ^ rs) * part_q + (qi ^ gray(rq))) * GROUP
                    for rx in range(2):
                        place = base + 2 * (xi ^ rx) + (ci ^ rc)
                        to[ry, rs, rq, rx] = scr[yi ^ gray(ry), place].astype(BF)


def attend_back_body(
    count, part_q, block, lengths, keep, from_x, from_ck, from_cx, query, keys, values, att, lse,
    d_query, d_pair, scr_o, acc_k, acc_v,
):
    si, qi, xi, ci, unused = places()
    length = lengths[0, si]
    rows = GROUP * block
    for ref, lanes, rx, rc in ((keep, 0, 0, 0), (from_x, 0, 1, 0), (from_ck, 1, 0, 1), (from_cx, 1, 1, 1)):
        for r in range(count):
            at = (((si ^ r) * 2 + (xi ^ rx)) * 2 + (ci ^ rc)) * block
            at = pl.multiple_of(at, block)
            scr_o[pl.ds(at, block), :] = ref[
                r * block : (r + 1) * block, lanes * HG : (lanes + 1) * HG
            ]
    acc_k[...] = jnp.zeros_like(acc_k)
    acc_v[...] = jnp.zeros_like(acc_v)
    for i in range(count):
        span = slice(i * rows, (i + 1) * rows)
        width = (i + 1) * part_q * rows
        allowed = allowed_at(i, rows, width, part_q, length)
        d_out_all = scr_o[span, :]
        d_out_t = d_out_all.astype(F32).T
        d_queries = []
        for h in range(HEADS):
            q_here = query[h, span, :]
            k_here = keys[h, :width, :]
            d_out = d_out_all[:, h * HD : (h + 1) * HD]
            scores = dot_nt(k_here, q_here)
            logs = lse[i * HEADS + h : i * HEADS + h + 1, :]
            probs = jnp.where(allowed, jnp.exp(scores - logs), 0.0)
            d_probs = dot_nt(values[h, :width, :], d_out)
            delta = jnp.sum(
                d_out_t[h * HD : (h + 1) * HD, :] * att[h, :, span], 0, keepdims=True
            )
            d_scores = (probs * (d_probs - delta)).astype(BF)
            acc_v[h, :width, :] += dot(probs.astype(BF), d_out)
            acc_k[h, :width, :] += dot(d_scores, q_here)
            d_queries.append(dot_tn(k_here, d_scores) * SCALE)
        d_query[span, :] = jnp.concatenate(d_queries, 0).T.astype(BF)
    kind = d_pair.dtype
    for h in range(HEADS):
        d_pair[:, h * HD : (h + 1) * HD] = acc_k[h].astype(kind)
        d_pair[:, HG + h * HD : HG + (h + 1) * HD] = acc_v[h].astype(kind)


def normed_back_body(count, block, d_query, d_pair, weight, keep, send, first, scr):
    si, qi, xi, ci, yi = places()
    scr[:, :HG] = d_query[...]
    scr[:, HG : 2 * HG] = d_pair[:, :HG]
    scr[:, 2 * HG :] = jnp.where(ci == 0, d_pair[:, HG:], jnp.zeros_like(d_pair[:, HG:]))
    for rc in (1, 0):
        for rx in (1, 0):
            starts = [
                pl.multiple_of((((si ^ r) * 2 + (xi ^ rx)) * 2 + (ci ^ rc)) * block, block)
                for r in range(count)
            ]
            here = jnp.concatenate([scr[pl.ds(at, block), :] for at in starts], 0)
            out = dot_nt(here, weight[...])
            part = [d_pair[pl.ds(at, block), HG : 2 * HG] for at in starts]
            part = jnp.concatenate(part, 0)
            if rc == 1:
                send[rx, :, :D] = out.astype(BF)
                send[rx, :, D : D + HG] = part
                send[rx, :, D + HG :] = jnp.zeros((part.shape[0], WIDE - D - HG), BF)
            else:
                keep[rx] = out
                first[rx] = part


def normed_sum_body(keep, first, from_c, send, own):
    si, qi, xi, ci, yi = places()
    send[:, :D] = (keep[1] + from_c[1, :, :D].astype(F32)).astype(BF)
    send[:, D : D + HG] = jnp.where(ci == 1, first[1], from_c[1, :, D : D + HG])
    send[:, D + HG :] = from_c[1, :, D + HG :]
    own[...] = jnp.where(ci == 1, first[0], from_c[0, :, D : D + HG])


def mixed_body(count, block, middle, mx_keep, from_c, from_x, bias, *outs):
    for r in range(count):
        span = slice(r * block, (r + 1) * block)
        mixed = middle[span, :] + mx_keep[span, :] + from_c[0, span, :].astype(F32)
        mixed = mixed + from_x[span, :].astype(F32) + bias[...]
        outs[r][...] = mixed.astype(BF)


def stack_body(keep, from_c, out):
    out[0] = keep[1]
    out[1] = from_c[1]


def project_grad_body(count, part_q, rw, normed, d_query, d_pair, keep, send, sums, scr, scr_d):
    si, qi, xi, ci, yi = places()
    scr_d[:, :HG] = d_query[...]
    scr_d[:, HG : 2 * HG] = d_pair[:, :HG]
    scr_d[:, 2 * HG :] = jnp.where(ci == 0, d_pair[:, HG:], jnp.zeros_like(d_pair[:, HG:]))
    scr[...] = dot_tn(normed[...], scr_d[...])
    total = jnp.sum(scr_d[...].astype(F32), 0, keepdims=True)
    group = 2 * ci + xi
    q_sum = total[:, :HG]
    v_sum = total[:, 2 * HG :]
    zero = jnp.zeros_like(q_sum)
    sums[0:1, :] = jnp.concatenate([jnp.where(group == g, q_sum, zero) for g in range(GROUP)], 1)
    sums[1:2, :] = jnp.concatenate(
        [jnp.where(group == g, v_sum, zero) for g in range(2)] + [zero, zero], 1
    )
    for rc, to in ((0, keep), (1, send)):
        for rx in range(2):
            for rs in range(count):
                for rq in range(part_q):
                    at = ((si ^ rs) * part_q + (qi ^ gray(rq))) * GROUP + 2 * (xi ^ rx) + (ci ^ rc)
                    at = pl.multiple_of(at * rw, rw)
                    to[rx, rs, rq] = scr[pl.ds(at, rw), :].astype(BF)


def tokens_back_body(keep, from_c, from_x, tok, gain, d_middle, own, *refs):
    outs, sums = refs[:4], refs[4]
    si, qi, xi, ci, yi = places()
    block = tok.shape[1]
    g_sum = jnp.zeros((1, D), F32)
    s_sum = jnp.zeros((1, D), F32)
    for r in range(4):
        span = slice(r * block, (r + 1) * block)
        xhat, spread = norm_parts(tok[r][:, :D].astype(F32))
        d_normed = keep[0, span, :] + from_c[0, span, :D].astype(F32)
        d_normed = d_normed + from_x[span, :D].astype(F32)
        g_sum = g_sum + jnp.sum(d_normed * xhat, 0, keepdims=True)
        s_sum = s_sum + jnp.sum(d_normed, 0, keepdims=True)
        out = d_middle[span, :] + norm_back(d_normed, gain[...], xhat, spread)
        outs[r][:, :D] = out.astype(BF)
        mine, theirs = own[span, :], from_x[span, D : D + HG]
        outs[r][:, D : D + HG] = jnp.where(xi == 0, mine, theirs)
        outs[r][:, D + HG :] = jnp.where(xi == 0, theirs, mine)
    sums[0:1, :] = g_sum
    sums[1:2, :] = s_sum


def on_device(
    tokens,
    first_values,
    lengths,
    cotangent,
    first_gain,
    first_shift,
    query_weight,
    query_bias,
    key_weight,
    value_weight,
    value_bias,
    output_weight,
    output_bias,
    second_gain,
    second_shift,
    expand_weight,
    expand_bias,
    reduce_weight,
    reduce_bias,
):
    count = tokens.shape[1]
    block = tokens.shape[2]
    part_q = lax.axis_size("q")
    nb = lax.axis_size("y")
    cycle = count * part_q * GROUP
    own_rows = count * block
    seq_rows = GROUP * own_rows
    rw = D // cycle
    cw = D // nb
    si, qi, xi, ci, yi = places()

    steps = Steps()

    vectors = [
        first_gain,
        first_shift,
        query_bias,
        value_bias,
        output_bias,
        second_gain,
        second_shift,
        reduce_bias,
        expand_bias,
    ]
    width = 3 * cw + DV // nb
    payload = call(
        functools.partial(pack_rows_body, nb),
        [shape((rw, width + HG))],
        [pltpu.VMEM((rw, HG), F32)],
        query_weight,
        key_weight,
        value_weight,
        output_weight,
        *vectors,
        mib=60,
    )[0]
    by_q = jnp.concatenate([p for p, unused in gather_list(payload, "q")], 0)
    by_s = direct([by_q] * count, "s")

    blocks_y = cycle // nb // GROUP
    keep, send = call(
        functools.partial(pack_units_body, nb, blocks_y),
        [shape((2, rw, cw)), shape((2, rw, cw))],
        [],
        expand_weight,
        mib=60,
    )
    from_x = swap(send, "x", 1)
    from_c = swap(jnp.stack([pick(keep, ci ^ 1), pick(from_x, ci ^ 1)]), "c", 1)
    f_parts = [jnp.stack([pick(keep, ci), pick(from_x, ci)]), from_c, reduce_weight.reshape(GROUP, rw, cw)]

    marks = [(rs, rq) for rs in range(count) for rq in range(part_q)]
    n2 = len(marks)
    vec_rows = (3 * n2 + 15) // 16 * 16
    pack_shape = shape((2 * n2 * rw + vec_rows, 3 * HG))
    core_shape = shape((2 * n2 * rw + 2 * vec_rows, 3 * HG))
    both = jnp.concatenate([tokens[0], first_values[0]], -1)
    if nb == 2:
        half_shape = shape((n2 * rw + vec_rows, 3 * HG))
        keep, send, o_own = call(
            functools.partial(own_columns_body, nb, count),
            [half_shape, half_shape, shape((n2, rw, cw))],
            [pltpu.VMEM((vec_rows, 3 * HG), F32)],
            *by_s,
        )
        both = after(both, send, from_c)
    else:
        held = jnp.concatenate(by_s, 0)[:, :, :width]
        both = after(both, held, from_c)
    got = direct([pick(both, si ^ k) for k in range(count)], "s")
    if nb == 2:
        columns_x = swap(send, "x", 1)
        own = keep
        rows = call(both_rows_body, [shape((2, n2 * rw, 3 * HG))], [], own, columns_x)[0]
        ready = rows
    else:
        by_y = gather_list(held, "y")[1:]
        keep, send, o_both = call(
            functools.partial(pack_columns_body, nb, rw, count, [slots for unused, slots in by_y]),
            [pack_shape, pack_shape, shape((nb, n2, rw, cw))],
            [pltpu.VMEM((nb, n2, rw, width), BF), pltpu.VMEM((vec_rows, 3 * HG), F32)],
            *by_s,
            *[part for part, unused in by_y],
        )
        columns_x = swap(send, "x", 1)
        ready = send

    def with_first(parts, x):
        parts = jnp.stack(parts)
        first = parts[..., D:].reshape(parts.shape[:2] + (2, HG))
        first = lax.dynamic_index_in_dim(first, x, 2, False)
        blank = jnp.zeros(first.shape[:2] + (WIDE - D - HG,), BF)
        return jnp.concatenate([parts[..., :D], first, blank], -1)

    near = with_first(got[:2], xi ^ 1)
    steps.need(Step.tokens_near, near)
    tok_x_near = swap(near, "x", 1)
    got = list(after(tuple(got), ready, near))
    far = with_first(got[2:], xi ^ 1)
    tok = with_first(got, xi)
    tok_x_far = swap(far, "x", 1)
    tok_other = far
    if nb == 2:
        columns_y = swap(rows, "y", 1)
    steps.reach(Step.tokens, far)
    steps.reach(Step.columns_x, columns_x)
    steps.reach(Step.tokens_x, tok_x_far)

    f_piece = jnp.concatenate(after(tuple(f_parts), tok_other), 0)
    f_by_q = jnp.concatenate([p for p, unused in gather_list(f_piece, "q")], 0)
    f_by_q = f_by_q.reshape((part_q,) + f_piece.shape)
    steps.need(Step.feed_piece, f_by_q)
    f_both = steps.move(
        Step.feed_two, lambda tie: (swap(tie(f_by_q), "s", 2), swap(tie(f_by_q), "s", 1))
    )
    if nb == 2:
        columns_y = steps.before(Step.cores, columns_y)
        keep, send = call(own_cores_body, [core_shape, core_shape], [], own, columns_x, rows, columns_y)
    else:
        keep, send = call(
            functools.partial(pack_cores_body, vec_rows),
            [core_shape, core_shape],
            [],
            keep,
            steps.before(Step.cores, columns_x),
        )
    steps.reach(Step.cores, keep)

    def output_x(tie):
        if nb != 2:
            return jnp.stack([o_both, swap(tie(o_both), "x", 1)])
        return jnp.stack([o_own, swap(tie(o_own), "x", 1)])

    def output_y(tie):
        held = tie(o_x())
        return held if nb != 2 else jnp.stack([held, swap(held, "y", 1)], 1)

    o_x = steps.move(Step.output_x, output_x)
    o_all = steps.move(Step.output_wide, output_y)
    o_c = steps.move(Step.output_c, lambda tie: swap(tie(o_all()), "c", 1))
    qkv_pieces = [keep, swap(send, "c", 1)]
    qkv_slots = [marks]
    tok_c = steps.move(Step.tokens_c, lambda tie: swap(tie(tok), "c", 1))
    row = shape((1, D), F32)
    gain_one, shift_one, my_qbias, my_vbias, o_bias, gain_two, shift_two, r_bias, my_ebias = call(
        functools.partial(vectors_body, qkv_slots, part_q, rw, cycle),
        [row, row, shape((1, HG), F32), shape((1, HG), F32), row, row, row, row, shape((1, UG), F32)],
        [pltpu.VMEM((cycle, 8, 3 * HG), F32)],
        *qkv_pieces,
    )
    tok_x = [tok_x_near, tok_x_far]
    sources = [tok, *tok_x, tok_c(), *[swap(after(part, keep), "c", 1) for part in tok_x]]
    o_slots = qkv_slots
    f_three = steps.move(Step.feed_three, lambda tie: swap(tie(f_by_q), "s", 3))

    def cotangent_z(tie):
        parts = [pick(tie(cotangent[0]), si ^ k) for k in range(count)]
        steps.need(Step.cotangent_part, parts[1:])
        return direct(parts, "s")

    cot = steps.move(Step.cotangent, cotangent_z)

    heads = [shape((HEADS, seq_rows, HD))] * 3
    query, keys, values, normed, qkv_w = call(
        functools.partial(project_body, qkv_slots, count, part_q, block, rw),
        heads + [shape((seq_rows, D)), shape((D, 3 * HG))],
        [pltpu.VMEM((cycle, rw, 3 * HG), BF), pltpu.VMEM((seq_rows, HG), BF)],
        *sources,
        *qkv_pieces,
        steps.before(Step.project, gain_one),
        shift_one,
        my_qbias,
        my_vbias,
    )
    steps.reach(Step.project, query)

    def whole_keys(value):
        if part_q == 1:
            return value
        parts = gather(value.reshape(HEADS, count, GROUP * block, HD), "q")
        return jnp.moveaxis(parts, 0, 2).reshape(HEADS, part_q * seq_rows, HD)

    keys, values = whole_keys(keys), whole_keys(values)
    key_rows = keys.shape[1]
    pair_shape = shape((own_rows, 2 * HG))
    pieces, piece_slots = [], []

    def most_y(tie):
        held = tie(jnp.concatenate([f_by_q, *f_both()], 0))
        steps.need(Step.feed_part, held)
        return gather_list(held, "y")

    y_most = steps.move(Step.feed_most_y, most_y)
    att, lse, att_keep, att_send = call(
        functools.partial(attend_body, count, part_q, block),
        [
            shape((HEADS, HD, seq_rows), F32),
            shape((count * HEADS, GROUP * block), F32),
            pair_shape,
            pair_shape,
        ],
        [pltpu.VMEM((seq_rows, HG), BF)],
        lengths,
        steps.before(Step.attend, query),
        keys,
        values,
        smem=1,
    )
    steps.reach(Step.attend, att_send)
    att_x = swap(att_send, "x", 1)
    steps.reach(Step.attend_x, att_x)
    y_last = steps.move(Step.feed_three_y, lambda tie: gather_list(tie(f_three()), "y"))
    mask_tie = steps.at(Step.mask)
    upstream = call(
        functools.partial(mask_body, part_q, block),
        [shape((own_rows, D))],
        [],
        lengths,
        *after(tuple(cot()), *mask_tie),
        smem=1,
    )[0]
    up_x = steps.move(Step.upstream_x, lambda tie: swap(tie(upstream), "x", 1))
    steps.need(Step.upstream, upstream)
    att_rows = [att_keep, att_x, swap(att_keep, "c", 1), swap(att_x, "c", 1)]
    middle, second, o_w = call(
        functools.partial(output_body, o_slots, count, part_q, block, nb, rw),
        [shape((own_rows, D), F32), shape((own_rows, D)), shape((D, D))],
        [pltpu.VMEM((nb, cycle, rw, cw), BF)],
        tok,
        *att_rows,
        o_all(),
        o_c(),
        steps.before(Step.output, o_bias),
        gain_two,
        shift_two,
    )
    steps.reach(Step.output, second)

    second_x = swap(second, "x", 1)
    steps.reach(Step.second_x, second_x)
    second_c = swap(second, "c", 1)
    up_c = swap(upstream, "c", 1)
    for held, order in ((y_most(), (0, 2, 1)), (y_last(), (3,))):
        for part, ys in held:
            pieces.append(part.reshape((-1,) + f_piece.shape))
            piece_slots.append([(ry, rs, rq) for ry in ys for rs in order for rq in range(part_q)])
    half_keep = shape((2, own_rows, D), F32)
    one_keep, one_send = shape((own_rows, D), F32), shape((own_rows, D))
    outs = [one_keep, one_send, one_keep, one_send] + [shape((2 * own_rows, D))] * 2 + [shape((1, UG), F32)]
    weight_shape = (nb, cycle, rw, cw)
    mx_near, mx_send_near, ds_near, ds_send_near, acts_near, dhs_near, eb_near, e_w, r_w = call(
        functools.partial(feed_near_body, piece_slots, part_q, nb),
        outs + [shape((D, UG)), shape((UG, D))],
        [pltpu.VMEM(weight_shape, BF)] * 2,
        second,
        second_c,
        upstream,
        up_c,
        *pieces,
        steps.before(Step.feed, my_ebias),
    )
    steps.reach(Step.feed, eb_near)
    far = [second_x, swap(second_x, "c", 1), up_x(), swap(up_x(), "c", 1)]
    mx_far, mx_send_far, ds_far, ds_send_far, acts_far, dhs_far, eb_sum = call(
        feed_far_body,
        outs,
        [],
        *far,
        steps.before(Step.feed_far, my_ebias),
        e_w,
        r_w,
        eb_near,
    )
    ds_c = swap(jnp.stack([ds_send_near, ds_send_far]), "c", 1)
    xs, acts, dhs = [second, second_c] + far[:2], [acts_near, acts_far], [dhs_near, dhs_far]
    us = [upstream, up_c] + far[2:]
    grad_shape = shape((nb // 2, count, part_q, GROUP, rw, cw))

    def feed_grad(left, right):
        return call(
            functools.partial(feed_grad_body, count, part_q, nb, rw, len(left), len(right)),
            [grad_shape, grad_shape],
            [pltpu.VMEM((seq_rows, D), BF)] * 2 + [pltpu.VMEM((nb, D, cw), F32)],
            *left,
            *right,
        )

    e_low, e_high = feed_grad(xs, dhs)
    ds_c = after(ds_c, e_low)
    ds_pay = (ds_far + ds_c[1].astype(F32)).astype(BF)
    ds_x = swap(ds_pay, "x", 1)
    steps.reach(Step.d_second_c, ds_pay)
    steps.reach(Step.d_second_x, ds_x)
    e_y = steps.move(Step.expand_y, lambda tie: swap(tie(e_high), "y", gray(nb // 2)))
    r_low, r_high = feed_grad(after(acts, ds_pay), us)
    mx_send = jnp.stack([mx_send_near, mx_send_far])
    steps.need(Step.reduce, r_low)
    mx_c = steps.move(Step.mixed_c, lambda tie: swap(tie(mx_send), "c", 1))
    d_middle, d_branch, d_keep, d_send, sums_two = call(
        functools.partial(middle_back_body, cycle),
        [shape((own_rows, D), F32), shape((own_rows, D)), pair_shape, pair_shape, shape((8, D), F32)],
        [],
        ds_near,
        ds_c,
        ds_x,
        upstream,
        middle,
        steps.before(Step.middle, gain_two),
        o_w,
        eb_sum,
    )
    steps.reach(Step.middle, d_send)
    d_x = swap(d_send, "x", 1)
    steps.reach(Step.d_attended_x, d_x)
    d_c = [swap(d_keep, "c", 1), swap(d_x, "c", 1)]
    steps.reach(Step.d_attended_c, d_c[1])
    d_rows = [d_keep, d_x] + d_c

    def expand_z(tie):
        low, got = after((e_low, e_y()), *tie.values)
        part = scatter_slots(low, None, "y", got)
        part = [part[0]] + [part[k].astype(BF) for k in range(1, count)]
        steps.need(Step.expand_part, part[1:])
        return direct(part, "s")

    e_z = steps.move(Step.expand_z, expand_z)
    r_y = steps.move(Step.reduce_y, lambda tie: swap(tie(r_high), "y", gray(nb // 2)))

    def mixed_step(tie):
        pay = tie((mx_far + mx_c()[1].astype(F32)).astype(BF))
        steps.need(Step.mixed_part, pay)
        return swap(pay, "x", 1)

    mx_x = steps.move(Step.mixed_x, mixed_step)
    o_shape = shape((nb, count, part_q, 2, rw, cw))

    def output_grad(tie):
        low, high = call(
            functools.partial(output_grad_body, count, part_q, nb, rw),
            [o_shape, o_shape],
            [pltpu.VMEM((nb, cycle, rw, cw), F32)],
            *att_rows,
            tie(d_branch),
        )
        return low, high, swap(high[None], "c", 1)

    o_c_sum = steps.move(Step.output_grad, output_grad)

    d_query, d_pair = call(
        functools.partial(attend_back_body, count, part_q, block),
        [shape((seq_rows, HG)), shape((key_rows, 2 * HG), BF if part_q == 1 else F32)],
        [pltpu.VMEM((seq_rows, HG), BF)] + [pltpu.VMEM((HEADS, key_rows, HD), F32)] * 2,
        lengths,
        *d_rows,
        query,
        keys,
        values,
        steps.before(Step.attend_back, att),
        lse,
        smem=1,
    )
    steps.reach(Step.attend_back, d_query)

    def reduce_z(tie):
        low, got = after((r_low, r_y()), *tie.values)
        part = scatter_slots(low, None, "y", got)
        part = [part[0]] + [part[k].astype(BF) for k in range(1, count)]
        steps.need(Step.reduce_part, part[1:])
        return direct(part, "s")

    r_z = steps.move(Step.reduce_z, reduce_z)

    def mixed_z(tie):
        parts = call(
            functools.partial(mixed_body, count, block),
            [shape((block, D))] * count,
            [],
            middle,
            mx_near,
            mx_c(),
            mx_x(),
            tie(r_bias),
        )
        steps.need(Step.mixed_rows, parts[1:])
        return direct(parts, "s")

    mixed = steps.move(Step.mixed_z, mixed_z)
    qkv_w = steps.before(Step.normed_back, qkv_w)
    if part_q > 1:
        parts = d_pair.reshape(count, part_q, GROUP * block, 2 * HG).swapaxes(0, 1)
        d_pair = scatter_sum(relative(parts, "q"), "q").reshape(seq_rows, 2 * HG).astype(BF)
    dn_keep, dn_send, first_keep = call(
        functools.partial(normed_back_body, count, block),
        [half_keep, shape((2, own_rows, WIDE)), shape((2, own_rows, HG))],
        [pltpu.VMEM((seq_rows, 3 * HG), BF)],
        d_query,
        d_pair,
        qkv_w,
    )
    steps.reach(Step.normed_back, dn_keep)
    dn_c = swap(dn_send, "c", 1)
    dn_pay, first_own = call(
        normed_sum_body,
        [shape((own_rows, WIDE)), shape((own_rows, HG))],
        [],
        dn_keep,
        first_keep,
        dn_c,
    )
    steps.reach(Step.d_normed_c, dn_pay)
    dn_x = swap(dn_pay, "x", 1)
    normed = after(normed, dn_pay)
    p_shape = shape((2, count, part_q, rw, 3 * HG))
    p_keep, p_send, sums_qv = call(
        functools.partial(project_grad_body, count, part_q, rw),
        [p_shape, p_shape, shape((2, D), F32)],
        [pltpu.VMEM((D, 3 * HG), F32), pltpu.VMEM((seq_rows, 3 * HG), BF)],
        steps.before(Step.project_grad, normed),
        d_query,
        d_pair,
    )
    steps.reach(Step.project_grad, p_keep)
    steps.reach(Step.d_normed_x, dn_x)
    p_from_c = swap(p_send, "c", 1)
    p_pay = call(stack_body, [shape((2, count, part_q, rw, 3 * HG))], [], p_keep, p_from_c)[0]
    steps.need(Step.columns_part, p_pay)
    p_from_x = steps.move(Step.columns_grad_x, lambda tie: swap(tie(p_pay), "x", 1))
    *gt, sums_one = call(
        tokens_back_body,
        [shape((block, D + DV))] * count + [shape((2, D), F32)],
        [],
        dn_keep,
        dn_c,
        dn_x,
        tok,
        steps.before(Step.tokens_back, gain_one),
        d_middle,
        first_own,
    )
    steps.reach(Step.tokens_back, gt[0])
    home_cols = 2 * cw + DV // nb
    n_rows = count * part_q
    flat = (steps.before(Step.columns_home, p_keep[0]), p_from_c[0], p_from_x()[0], p_from_x()[1])
    y_low, y_high = call(
        functools.partial(columns_home_body, nb, n_rows),
        [shape((nb // 2, n_rows, rw, home_cols), F32), shape((nb // 2, n_rows, rw, home_cols))],
        [pltpu.VMEM((nb, rw, home_cols), F32)],
        *[v.reshape(-1, rw, 3 * HG) for v in flat],
    )
    steps.reach(Step.columns_home, y_high)
    steps.need(Step.columns_sent, y_high)
    gt = steps.move(Step.tokens_z, lambda tie: direct(tie(gt), "s"))()
    steps.reach(Step.tokens_z, gt[1])
    back = in_place(gt, "s")[None]
    grad_tokens, grad_first = back[..., :D], back[..., D:]

    def sum_q(value):
        return scatter_sum(value, "q")

    o_low, o_high, o_got = o_c_sum()
    o_part = steps.move(
        Step.output_y, lambda tie: scatter_sum(scatter_slots(tie(o_low)[None], None, "c", o_got), "y")
    )()
    o_part = jnp.moveaxis(o_part, 2, 0)
    o_part = scatter_slots(o_part[:1], o_part[1:], "x")
    qkv_part = scatter_slots(y_low, y_high, "y").reshape(count, part_q, rw, home_cols)
    home_pay = jnp.concatenate([steps.before(Step.home, qkv_part), o_part], -1)
    steps.reach(Step.home, home_pay)
    home = sum_q(direct_sum(home_pay, "s"))
    q_home, k_home, v_home = home[:, :cw], home[:, cw : 2 * cw], home[:, 2 * cw : home_cols]
    o_home = home[:, home_cols:]
    mixed_out = in_place(after(tuple(mixed()), *steps.at(Step.mixed_out)), "s")[None]

    def to_group(part):
        part = part.astype(BF)
        keep = lax.dynamic_index_in_dim(part, ci, 1, keepdims=False)
        got = swap(lax.dynamic_index_in_dim(part, ci ^ 1, 1, keepdims=False), "c", 1)
        both = jnp.stack([keep, got], 1)
        return pick(both, xi), swap(pick(both, xi ^ 1), "x", 1)

    e_z = after(tuple(e_z()), *steps.at(Step.expand_home))
    e_home = sum_q(sum(part.astype(F32) for part in e_z))
    e_home = call(
        functools.partial(units_home_body, blocks_y),
        [shape((rw, FF // nb), F32)],
        [],
        *to_group(e_home.reshape(2, 2, rw, cw)),
    )[0]
    r_z = after(tuple(r_z()), *steps.at(Step.reduce_home))
    r_home = sum_q(sum(part.astype(F32) for part in r_z)).reshape(GROUP * rw, cw)

    sums = after(jnp.concatenate([sums_one, sums_qv, sums_two], 0), *steps.at(Step.sums))
    for axis in ("c", "x", "y", "q"):
        sums = whole_sum(sums, axis)
    sums = sum(direct([sums] * count, "s"))
    place = ((si * part_q + qi) * 2 + xi) * 2 + ci
    part = lax.dynamic_slice_in_dim(sums[:8], place * rw, rw, 1)
    vb_home = lax.dynamic_slice_in_dim(sums[3], place * (DV // cycle), DV // cycle, 0)
    eb_home = pick(sums[8:].reshape(cycle, -1), place)
    return (
        mixed_out,
        grad_tokens,
        grad_first,
        part[0],
        part[1],
        q_home,
        part[2],
        k_home,
        v_home,
        vb_home,
        o_home,
        part[4],
        part[5],
        part[6],
        e_home,
        eb_home,
        r_home,
        part[7],
    )


def solution(mesh):
    cycle, nb = mesh.devices.shape
    sequences = 4
    fine = Mesh(
        mesh.devices.reshape(sequences, cycle // (sequences * GROUP), 2, 2, nb),
        ("s", "q", "x", "c", "y"),
    )
    seq = ("s", "q", "x", "c")
    rows = P("y", None, seq, None)
    matrix = P(seq, "y")
    vector = P(seq)
    in_specs = (
        rows,
        rows,
        P("y", None),
        rows,
        vector,
        vector,
        matrix,
        vector,
        matrix,
        matrix,
        vector,
        matrix,
        vector,
        vector,
        vector,
        matrix,
        vector,
        matrix,
        vector,
    )
    out_specs = (
        rows,
        rows,
        rows,
        vector,
        vector,
        matrix,
        vector,
        matrix,
        matrix,
        vector,
        matrix,
        vector,
        vector,
        vector,
        matrix,
        vector,
        matrix,
        vector,
    )
    return jax.shard_map(
        on_device, mesh=fine, in_specs=in_specs, out_specs=out_specs, check_vma=False
    )
```

```python
import enum
import functools

import jax
import jax.numpy as jnp
from jax import lax
from jax.experimental import pallas as pl
from jax.experimental.pallas import tpu as pltpu
from jax.sharding import Mesh, PartitionSpec as P

D = 768
H = 12
HD = 64
FF = 3072
DV = 384
GROUP = 4
HG = D // GROUP
HEADS = HG // HD
UG = FF // GROUP
WIDE = 1024

EPS = 1e-05
NEG = -1e30
SCALE = HD**-0.5
BF = jnp.bfloat16
F32 = jnp.float32
VMEM = pl.BlockSpec(memory_space=pltpu.VMEM)
SMEM = pl.BlockSpec(memory_space=pltpu.SMEM)


def gray(k):
    return k ^ (k >> 1)


def swap(value, axis, mask):
    return lax.ppermute(value, axis, [(i, i ^ mask) for i in range(lax.axis_size(axis))])


def pick(blocks, index):
    return lax.dynamic_index_in_dim(blocks, index, 0, keepdims=False)


def after(value, *others):
    return lax.optimization_barrier((value, *others))[0]


class Step(enum.IntEnum):
    attend = enum.auto()
    attend_back = enum.auto()
    attend_x = enum.auto()
    columns_grad_x = enum.auto()
    columns_home = enum.auto()
    columns_part = enum.auto()
    columns_sent = enum.auto()
    columns_x = enum.auto()
    cores = enum.auto()
    cotangent = enum.auto()
    cotangent_part = enum.auto()
    d_attended_c = enum.auto()
    d_attended_x = enum.auto()
    d_normed_c = enum.auto()
    d_normed_x = enum.auto()
    d_second_c = enum.auto()
    d_second_x = enum.auto()
    expand_home = enum.auto()
    expand_part = enum.auto()
    expand_y = enum.auto()
    expand_z = enum.auto()
    feed = enum.auto()
    feed_far = enum.auto()
    feed_most_y = enum.auto()
    feed_part = enum.auto()
    feed_piece = enum.auto()
    feed_three = enum.auto()
    feed_three_y = enum.auto()
    feed_two = enum.auto()
    home = enum.auto()
    mask = enum.auto()
    middle = enum.auto()
    mixed_c = enum.auto()
    mixed_out = enum.auto()
    mixed_part = enum.auto()
    mixed_rows = enum.auto()
    mixed_x = enum.auto()
    mixed_z = enum.auto()
    normed_back = enum.auto()
    output = enum.auto()
    output_c = enum.auto()
    output_grad = enum.auto()
    output_wide = enum.auto()
    output_x = enum.auto()
    output_y = enum.auto()
    project = enum.auto()
    project_grad = enum.auto()
    reduce = enum.auto()
    reduce_home = enum.auto()
    reduce_part = enum.auto()
    reduce_y = enum.auto()
    reduce_z = enum.auto()
    second_x = enum.auto()
    sums = enum.auto()
    tokens = enum.auto()
    tokens_back = enum.auto()
    tokens_c = enum.auto()
    tokens_near = enum.auto()
    tokens_x = enum.auto()
    tokens_z = enum.auto()
    upstream = enum.auto()
    upstream_x = enum.auto()


PLAN = {
    Step.feed_two: ((), None),
    Step.output_x: ((), None),
    Step.output_c: ((Step.output_wide,), Step.project),
    Step.tokens_c: ((Step.columns_x,), None),
    Step.feed_three: ((Step.attend_x,), Step.attend),
    Step.cotangent: ((Step.project,), None),
    Step.feed_most_y: ((Step.attend_x,), None),
    Step.feed_three_y: ((), None),
    Step.mask: ((), None),
    Step.upstream_x: ((), None),
    Step.expand_y: ((), None),
    Step.mixed_c: ((Step.d_second_c,), Step.middle),
    Step.expand_z: ((Step.middle,), Step.normed_back),
    Step.reduce_y: ((Step.middle,), None),
    Step.mixed_x: ((Step.d_attended_x,), Step.normed_back),
    Step.output_grad: ((Step.d_normed_c,), None),
    Step.reduce_z: ((Step.attend_back,), Step.tokens_back),
    Step.mixed_z: ((Step.attend_back,), None),
    Step.columns_grad_x: ((), None),
    Step.tokens_z: ((), None),
    Step.output_y: ((), None),
    Step.mixed_out: ((Step.home,), None),
    Step.expand_home: ((Step.tokens_z,), None),
    Step.reduce_home: ((Step.tokens_z,), None),
    Step.sums: ((Step.home,), None),
    Step.output_wide: ((Step.output_x,), None),
}
EARLY = {
    Step.upstream: Step.output,
    Step.reduce: Step.middle,
    Step.expand_part: None,
    Step.mixed_part: Step.attend_back,
    Step.reduce_part: Step.normed_back,
    Step.mixed_rows: Step.normed_back,
    Step.columns_part: None,
    Step.feed_part: Step.attend,
    Step.cotangent_part: Step.attend,
    Step.columns_sent: None,
    Step.feed_piece: None,
    Step.tokens_near: Step.cores,
}


class Tie:
    def __init__(self, values):
        self.values = values

    def __call__(self, value):
        return after(value, *self.values) if self.values else value


class Steps:
    def __init__(self):
        self.reached, self.waiting, self.due = {}, {}, {}

    def reach(self, name, value):
        self.reached[name] = value
        for name, start in list(self.waiting.items()):
            self.begin(name, start)

    def at(self, name):
        return [self.reached[step] for step in PLAN[name][0]]

    def begin(self, name, start):
        if all(step in self.reached for step in PLAN[name][0]):
            self.waiting.pop(name, None)
            self.reached[name] = None
            result = start(Tie(self.at(name)))
            self.reached[name] = jax.tree.leaves(result)[-1]
            self.due.setdefault(PLAN[name][1], []).extend(jax.tree.leaves(result))
            self.results[name] = result
            for other, begin in list(self.waiting.items()):
                self.begin(other, begin)

    results = None

    def move(self, name, start):
        if self.results is None:
            self.results = {}
        self.waiting[name] = start
        self.begin(name, start)
        return lambda: self.results[name]

    def need(self, name, value):
        self.due.setdefault(EARLY.get(name), []).extend(jax.tree.leaves(value))

    def before(self, name, value):
        due = self.due.pop(name, [])
        return after(value, *due) if due else value


def relative(blocks, axis):
    n = lax.axis_size(axis)
    if n == 1:
        return blocks
    me = lax.axis_index(axis)
    return jnp.stack([pick(blocks, gray(r) ^ me) for r in range(n)], 0)


def absolute(rel, axis):
    n = lax.axis_size(axis)
    if n == 1:
        return rel
    me = lax.axis_index(axis)
    return jnp.stack([pick(rel, gray(a ^ me)) for a in range(n)], 0)


def gather_list(value, axis):
    pieces = [(value[None], [0])]
    size = 1
    while size < lax.axis_size(axis):
        held = pieces[0][0] if size == 1 else jnp.concatenate([p for p, unused in pieces], 0)
        pieces.append((swap(held, axis, gray(size)), list(range(size, 2 * size))))
        size *= 2
    return pieces


def gather(value, axis):
    return absolute(jnp.concatenate([p for p, unused in gather_list(value, axis)], 0), axis)


def direct(parts, axis):
    return [parts[0]] + [swap(parts[k], axis, k) for k in range(1, len(parts))]


def in_place(parts, axis):
    held = jnp.stack(parts)
    me = lax.axis_index(axis)
    return jnp.stack([pick(held, a ^ me) for a in range(len(parts))])


def direct_sum(rel, axis):
    got = direct([rel[0].astype(F32)] + [rel[k].astype(BF) for k in range(1, rel.shape[0])], axis)
    return sum(part.astype(F32) for part in got)


def scatter_slots(low, high, axis, got=None):
    while True:
        half = low.shape[0]
        if got is None:
            got = swap(high.astype(BF), axis, gray(half))
        total = low.astype(F32) + got.astype(F32)
        got = None
        if half == 1:
            return total[0]
        low, high = total[: half // 2], total[half // 2 :]


def scatter_sum(rel, axis):
    half = rel.shape[0] // 2
    return rel[0] if half == 0 else scatter_slots(rel[:half], rel[half:], axis)


def exchange(blocks, axis):
    n = lax.axis_size(axis)
    rel = relative(blocks, axis)
    bit = 1
    while bit < n:
        shape = rel.shape
        pairs = rel.reshape((n // (2 * bit), 2, bit) + shape[1:])
        got = swap(pairs[:, 1], axis, gray(bit))
        rel = jnp.stack([pairs[:, 0], got], 1).reshape(shape)
        bit *= 2
    return absolute(rel, axis)


def whole_sum(value, axis):
    n = lax.axis_size(axis)
    bit = 1
    while bit < n:
        value = value + swap(value, axis, bit)
        bit *= 2
    return value


def norm_parts(values):
    centre = values - jnp.mean(values, -1, keepdims=True)
    spread = lax.rsqrt(jnp.mean(centre * centre, -1, keepdims=True) + EPS)
    return centre * spread, spread


def norm_back(d_out, gain, xhat, spread):
    e = d_out * gain
    return spread * (
        e - jnp.mean(e, -1, keepdims=True) - xhat * jnp.mean(e * xhat, -1, keepdims=True)
    )


def dot(a, b):
    return jnp.dot(a, b, preferred_element_type=F32)


def dot_nt(a, b):
    return lax.dot_general(a, b, (((1,), (1,)), ((), ())), preferred_element_type=F32)


def dot_tn(a, b):
    return lax.dot_general(a, b, (((0,), (0,)), ((), ())), preferred_element_type=F32)


def places():
    return tuple(lax.axis_index(a) for a in ("s", "q", "x", "c", "y"))


def merged(blocks):
    n, rows, cols = blocks.shape
    if rows % 16 == 0:
        return blocks.reshape(n * rows, cols)
    return blocks.astype(F32).reshape(n * rows, cols).astype(BF)


def split_rows(rows, n):
    size = rows.shape[0] // n
    if size % 16 == 0:
        return [rows[i * size : (i + 1) * size] for i in range(n)]
    wide = rows.astype(F32)
    return [wide[i * size : (i + 1) * size].astype(BF) for i in range(n)]


def shape(dims, kind=BF):
    return jax.ShapeDtypeStruct(tuple(dims), kind)


def call(body, outs, scratch, *operands, smem=0, mib=24):
    arrays = operands[smem:]
    n, n_out = len(arrays), len(outs)
    def copied(*refs):
        scalars, sources = refs[:smem], refs[smem : smem + n]
        results = refs[smem + n : smem + n + n_out]
        own = refs[smem + n + n_out : len(refs) - n - 1]
        held, sems = refs[len(refs) - n - 1 : -1], refs[-1]
        copies = [
            pltpu.make_async_copy(sources[i], held[i], sems.at[i]) for i in range(n)
        ]
        for copy in copies:
            copy.start()
        for copy in copies:
            copy.wait()
        body(*scalars, *held, *results, *own)

    return pl.pallas_call(
        copied,
        out_shape=tuple(outs),
        in_specs=[SMEM] * smem + [pl.BlockSpec(memory_space=pl.ANY)] * n,
        out_specs=tuple(VMEM for unused in outs),
        scratch_shapes=[*scratch]
        + [pltpu.VMEM(v.shape, v.dtype) for v in arrays]
        + [pltpu.SemaphoreType.DMA((n,))],
        cost_estimate=pl.CostEstimate(flops=1, bytes_accessed=1, transcendentals=0),
        compiler_params=pltpu.CompilerParams(vmem_limit_bytes=mib * 1024 * 1024),
    )(*operands)


def pack_rows_body(nb, query, keys, values, output, *refs):
    vectors = refs[:9]
    out, rows = refs[9:]
    cw, vw = D // nb, DV // nb
    out[:, :cw] = query[...]
    out[:, cw : 2 * cw] = keys[...]
    out[:, 2 * cw : 3 * cw] = output[...]
    out[:, 3 * cw : 3 * cw + vw] = values[...]
    rows[...] = jnp.zeros_like(rows)
    for j, vector in enumerate(vectors):
        size = vector.shape[0]
        rows[j : j + 1, :size] = vector[...].astype(F32).reshape(1, size)
    out[:, 3 * cw + vw :] = rows[...].astype(BF)


def own_columns_body(nb, n_own, *refs):
    owns = refs[:n_own]
    keep, send, out, rows = refs[n_own:]
    si, qi, xi, ci, yi = places()
    cw, vw = D // nb, DV // nb
    per = owns[0].shape[0]
    kept, sent = [], []
    rows[...] = jnp.zeros_like(rows)
    for j in range(n_own):
        for q in range(per):
            held = owns[j][q].astype(F32)
            out[j * per + q] = owns[j][q, :, 2 * cw : 3 * cw]
            values = held[:, 3 * cw : 3 * cw + vw]
            parts = [
                jnp.concatenate([held[:, x * HG : (x + 1) * HG], held[:, cw + x * HG : cw + (x + 1) * HG]], 1)
                for x in range(2)
            ]
            kept.append(jnp.concatenate([jnp.where(xi == 0, *parts), values], 1))
            sent.append(jnp.concatenate([jnp.where(xi == 0, *parts[::-1]), values], 1))
            for v in range(9):
                at = 3 * (j * per + q) + v // 3
                start = 3 * cw + vw
                rows[at : at + 1, (v % 3) * HG : (v % 3 + 1) * HG] = held[v : v + 1, start : start + HG]
    keep[...] = jnp.concatenate(kept + [rows[...]], 0).astype(BF)
    send[...] = jnp.concatenate(sent + [rows[...]], 0).astype(BF)


def both_rows_body(mine, from_x, out):
    out[0] = mine[: out.shape[1], :]
    out[1] = from_x[: out.shape[1], :]


def own_cores_body(mine, from_x, both, from_y, keep, send):
    si, qi, xi, ci, yi = places()
    size = both.shape[1]
    kept, sent = [], []
    for rx in range(2):
        own, other = both[rx].astype(F32), from_y[rx].astype(F32)
        halves = [jnp.where(yi == y, own, other) for y in range(2)]
        values = jnp.where(xi == 0, halves[0][:, 2 * HG :], halves[1][:, 2 * HG :])
        columns = [half[:, : 2 * HG] for half in halves]
        kept.append(jnp.concatenate([jnp.where(ci == 0, *columns), values], 1))
        sent.append(jnp.concatenate([jnp.where(ci == 0, *columns[::-1]), values], 1))
    vectors = [ref[size:, :].astype(F32) for ref in (mine, from_x)]
    keep[...] = jnp.concatenate(kept + vectors, 0).astype(BF)
    send[...] = jnp.concatenate(sent + vectors, 0).astype(BF)


def pack_columns_body(nb, rw, n_own, y_slots, *refs):
    owns = refs[:n_own]
    pieces = refs[n_own : n_own + len(y_slots)]
    keep, send, out, scr, rows = refs[n_own + len(y_slots) :]
    si, qi, xi, ci, yi = places()
    cw, vw = D // nb, DV // nb
    per = owns[0].shape[0]
    n2 = n_own * per
    width = 3 * cw + vw
    rows[...] = jnp.zeros_like(rows)
    for j in range(n_own):
        scr[yi, j * per : (j + 1) * per] = owns[j][:, :, :width]
        out[0, j * per : (j + 1) * per] = owns[j][:, :, 2 * cw : 3 * cw]
        for q in range(per):
            held = owns[j][q, :, width:].astype(F32)
            for v in range(9):
                at = 3 * (j * per + q) + v // 3
                rows[at : at + 1, (v % 3) * HG : (v % 3 + 1) * HG] = held[v : v + 1]
    for ref, slots in zip(pieces, y_slots):
        for at, ry in enumerate(slots):
            scr[yi ^ gray(ry)] = ref[at]
            out[ry] = ref[at, :, :, 2 * cw : 3 * cw]
    both = ([], [])
    for n in range(n2):
        full = [
            jnp.concatenate([scr[y, n][:, a : a + w].astype(F32) for y in range(nb)], 1)
            for a, w in ((0, cw), (cw, cw), (3 * cw, vw))
        ]

        def part(x, c):
            cols = [v[:, (2 * c + x) * HG : (2 * c + x + 1) * HG] for v in full[:2]]
            return jnp.concatenate(cols + [full[2][:, x * HG : (x + 1) * HG]], 1)

        for c in range(2):
            one, two = part(0, c), part(1, c)
            both[c].append((jnp.where(xi == 0, one, two), jnp.where(xi == 0, two, one)))
    for which, ref in ((0, keep), (1, send)):
        parts = [pair[which] for c in range(2) for pair in both[c]] + [rows[...]]
        ref[...] = jnp.concatenate(parts, 0).astype(BF)


def pack_cores_body(vec_rows, mine, from_x, keep, send):
    si, qi, xi, ci, yi = places()
    half = (mine.shape[0] - vec_rows) // 2
    parts = [], []
    for ref in (mine, from_x):
        a, b = ref[:half].astype(F32), ref[half : 2 * half].astype(F32)
        parts[0].append(jnp.where(ci == 0, a, b))
        parts[1].append(jnp.where(ci == 0, b, a))
    vectors = [ref[2 * half :].astype(F32) for ref in (mine, from_x)]
    keep[...] = jnp.concatenate(parts[0] + vectors, 0).astype(BF)
    send[...] = jnp.concatenate(parts[1] + vectors, 0).astype(BF)


def vectors_body(slots, part_q, rw, cycle, *refs):
    pieces = refs[: 2 * len(slots)]
    gain_one, shift_one, q_bias, v_bias, o_bias, gain_two, shift_two, r_bias, e_bias, scr = refs[
        2 * len(slots) :
    ]
    si, qi, xi, ci, yi = places()
    for stage, marks in enumerate(slots):
        for rc in range(2):
            for rx in range(2):
                ref = pieces[2 * stage + rc]
                size = (3 * len(marks) + 15) // 16 * 16
                at = ref.shape[0] - (2 - rx) * size
                rows = ref[at : at + size].astype(F32)
                for at, (rs, rq) in enumerate(marks):
                    place = ((si ^ rs) * part_q + (qi ^ gray(rq))) * GROUP
                    place = place + 2 * (xi ^ rx) + (ci ^ rc)
                    scr[pl.ds(place, 1), 0:3] = rows[3 * at : 3 * at + 3][None]

    def whole(j, size):
        held = scr[:, j // 3, (j % 3) * HG : (j % 3) * HG + size]
        wide = cycle * size
        lane = lax.broadcasted_iota(jnp.int32, (size, wide), 1)
        row = lax.broadcasted_iota(jnp.int32, (size, wide), 0)
        spread = jnp.where(lane % size == row, 1.0, 0.0).astype(BF)
        out = dot(held.astype(BF), spread)
        mark = lax.broadcasted_iota(jnp.int32, (cycle, wide), 1) // size
        row = lax.broadcasted_iota(jnp.int32, (cycle, wide), 0)
        return jnp.sum(jnp.where(mark == row, out, 0.0), 0, keepdims=True)

    for j, ref in ((0, gain_one), (1, shift_one), (4, o_bias), (5, gain_two), (6, shift_two), (7, r_bias)):
        ref[...] = whole(j, rw)
    query = whole(2, rw)
    group = 2 * ci + xi
    total = jnp.zeros((1, HG), F32)
    for g in range(GROUP):
        total = total + jnp.where(group == g, query[:, g * HG : (g + 1) * HG], 0.0)
    q_bias[...] = total
    value = whole(3, DV // cycle)
    v_bias[...] = jnp.where(xi == 0, value[:, :HG], value[:, HG:])
    unit = FF // cycle
    parts = []
    for j in range(cycle // GROUP):
        held = scr[j * GROUP + 2 * xi + ci]
        parts.append(held[2:3, 2 * HG : 2 * HG + unit])
    e_bias[...] = jnp.concatenate(parts, 1)


def pack_units_body(nb, blocks_y, expand, keep, send):
    si, qi, xi, ci, yi = places()
    unit = FF // (blocks_y * GROUP * nb)

    def part(x, c):
        cols = [expand[:, (GROUP * b + 2 * x + c) * unit : (GROUP * b + 2 * x + c + 1) * unit] for b in range(blocks_y)]
        return jnp.concatenate([v.astype(F32) for v in cols], 1)

    for c in range(2):
        one, two = part(0, c), part(1, c)
        keep[c] = jnp.where(xi == 0, one, two).astype(BF)
        send[c] = jnp.where(xi == 0, two, one).astype(BF)


def units_home_body(blocks_y, mine, other, out):
    si, qi, xi, ci, yi = places()
    unit = mine.shape[2] // blocks_y
    for b in range(blocks_y):
        for g in range(GROUP):
            total = jnp.zeros((mine.shape[1], unit), F32)
            for rx, ref in ((0, mine), (1, other)):
                for rc in range(2):
                    here = 2 * (xi ^ rx) + (ci ^ rc) == g
                    part = ref[rc, :, b * unit : (b + 1) * unit].astype(F32)
                    total = total + jnp.where(here, part, 0.0)
            at = (GROUP * b + g) * unit
            out[:, at : at + unit] = total


def columns_home_body(nb, n, keep, from_c, x_keep, x_from_c, low, high, scr):
    si, qi, xi, ci, yi = places()
    cw, vw = D // nb, DV // nb
    sources = ((0, 0, keep), (0, 1, from_c), (1, 0, x_keep), (1, 1, x_from_c))
    for s in range(n):
        full = []
        for kind in range(3):
            groups = []
            for g in range(GROUP if kind < 2 else 2):
                total = jnp.zeros((keep.shape[1], HG), F32)
                for rx, rc, ref in sources:
                    here = 2 * (ci ^ rc) + (xi ^ rx) == g
                    part = ref[s, :, kind * HG : (kind + 1) * HG].astype(F32)
                    total = total + jnp.where(here, part, 0.0)
                groups.append(total)
            full.append(jnp.concatenate(groups, 1))
        for y in range(nb):
            scr[y] = jnp.concatenate(
                [
                    full[0][:, y * cw : (y + 1) * cw],
                    full[1][:, y * cw : (y + 1) * cw],
                    full[2][:, y * vw : (y + 1) * vw],
                ],
                1,
            )
        for ry in range(nb):
            to = low if ry < nb // 2 else high
            to[ry % (nb // 2), s] = scr[yi ^ gray(ry)].astype(to.dtype)


def project_body(slots, count, part_q, block, rw, *refs):
    n_pieces = 2 * len(slots)
    sources = refs[:6]
    pieces = refs[6 : 6 + n_pieces]
    gain, shift, q_bias, v_bias = refs[6 + n_pieces : 10 + n_pieces]
    query, keys, values, normed, weight, scr_w, scr_f = refs[10 + n_pieces :]
    si, qi, xi, ci, unused = places()
    for stage, marks in enumerate(slots):
        for at, (rs, rq) in enumerate(marks):
            base = ((si ^ rs) * part_q + (qi ^ gray(rq))) * GROUP
            for rc in range(2):
                ref = pieces[2 * stage + rc]
                n2 = len(marks)
                held = split_rows(ref[: 2 * n2 * rw], 2 * n2)
                for rx in range(2):
                    place = base + 2 * (xi ^ rx) + (ci ^ rc)
                    scr_w[pl.ds(place, 1)] = held[rx * n2 + at][None]
    weight[...] = merged(scr_w[...])
    for pair in range(4):
        rx, rc = pair % 2, pair // 2
        for r in range(count):
            held = sources[3 * rc : 3 * rc + 3]
            here = held[0][r] if rx == 0 else held[1 + r // 2][r % 2]
            at = (((si ^ r) * 2 + (xi ^ rx)) * 2 + (ci ^ rc)) * block
            at = pl.multiple_of(at, block)
            xhat, unused = norm_parts(here[:, :D].astype(F32))
            normed[pl.ds(at, block), :] = (xhat * gain[...] + shift[...]).astype(BF)
            scr_f[pl.ds(at, block), :] = here[:, D : D + HG]
    rows = GROUP * block
    for i in range(count):
        span = slice(i * rows, (i + 1) * rows)
        out = dot(normed[span, :], weight[...])
        q_low = (out[:, :HG] + q_bias[...]).astype(BF) * SCALE
        k_low = out[:, HG : 2 * HG].astype(BF)
        v_low = (out[:, 2 * HG :] + v_bias[...]).astype(BF)
        v_low = jnp.where(ci == 0, v_low, scr_f[span, :])
        for h in range(HEADS):
            cols = slice(h * HD, (h + 1) * HD)
            query[h, span, :] = q_low[:, cols].astype(BF)
            keys[h, span, :] = k_low[:, cols]
            values[h, span, :] = v_low[:, cols]


def allowed_at(i, rows, width, part_q, length):
    unused, qi, *unused = places()
    row_pos = (i * part_q + qi) * rows + lax.broadcasted_iota(jnp.int32, (1, rows), 1)
    last = jnp.minimum(row_pos, length - 1)
    return lax.broadcasted_iota(jnp.int32, (width, rows), 0) <= last


def attend_body(count, part_q, block, lengths, query, keys, values, att, lse, keep, send, scr):
    si, qi, xi, ci, unused = places()
    length = lengths[0, si]
    rows = GROUP * block
    for i in range(count):
        span = slice(i * rows, (i + 1) * rows)
        width = (i + 1) * part_q * rows
        allowed = allowed_at(i, rows, width, part_q, length)
        outs = []
        for h in range(HEADS):
            scores = dot_nt(keys[h, :width, :], query[h, span, :])
            scores = jnp.where(allowed, scores, NEG)
            peak = jnp.max(scores, 0, keepdims=True)
            weights = jnp.exp(scores - peak)
            total = jnp.sum(weights, 0, keepdims=True)
            out = dot_tn(values[h, :width, :], weights.astype(BF)) * (1.0 / total)
            att[h, :, span] = out
            lse[i * HEADS + h : i * HEADS + h + 1, :] = peak + jnp.log(total)
            outs.append(out)
        scr[span, :] = jnp.concatenate(outs, 0).T.astype(BF)
    for rx, to in ((0, keep), (1, send)):
        for rc in range(2):
            for r in range(count):
                at = (((si ^ r) * 2 + (xi ^ rx)) * 2 + (ci ^ rc)) * block
                to[r * block : (r + 1) * block, rc * HG : (rc + 1) * HG] = scr[
                    pl.ds(pl.multiple_of(at, block), block), :
                ]


def mask_body(part_q, block, lengths, *refs):
    parts, out = refs[:-1], refs[-1]
    si, qi, xi, ci, unused = places()
    for r, part in enumerate(parts):
        start = (((si ^ r) * part_q + qi) * GROUP + 2 * xi + ci) * block
        row = start + lax.broadcasted_iota(jnp.int32, (block, 1), 0)
        here = jnp.where(row < lengths[0, si], part[...].astype(F32), 0.0)
        out[r * block : (r + 1) * block, :] = here.astype(BF)


def output_body(
    slots, count, part_q, block, nb, rw, tok, keep, from_x, from_ck, from_cx, *refs
):
    pieces = refs[:2]
    bias, gain, shift, middle, second, weight, scr = refs[2:]
    si, qi, xi, ci, yi = places()
    for stage, marks in enumerate(slots):
        for rc in range(2):
            for rx in range(2):
                for at, (rs, rq) in enumerate(marks):
                    place = ((si ^ rs) * part_q + (qi ^ gray(rq))) * GROUP
                    place = place + 2 * (xi ^ rx) + (ci ^ rc)
                    for ry in range(nb):
                        scr[yi ^ gray(ry), pl.ds(place, 1)] = pieces[rc][rx, ry, at][None]
    for y in range(nb):
        cw = D // nb
        weight[:, y * cw : (y + 1) * cw] = merged(scr[y])
    tokens = [tok[r][:, :D].astype(F32) for r in range(count)]
    total = jnp.concatenate(tokens, 0) + bias[...]
    for ref, lanes, rx, rc in ((keep, 0, 0, 0), (from_x, 0, 1, 0), (from_ck, 1, 0, 1), (from_cx, 1, 1, 1)):
        group = 2 * (ci ^ rc) + (xi ^ rx)
        rows = weight[pl.ds(pl.multiple_of(group * HG, HG), HG), :]
        total = total + dot(ref[:, lanes * HG : (lanes + 1) * HG], rows)
    middle[...] = total
    xhat, unused = norm_parts(total)
    second[...] = (xhat * gain[...] + shift[...]).astype(BF)


def feed_weights(slots, part_q, nb, pieces, scr_e, scr_r, e_w, r_w):
    si, qi, xi, ci, yi = places()
    for ref, marks in zip(pieces, slots):
        for at, (ry, rs, rq) in enumerate(marks):
            base = ((si ^ rs) * part_q + (qi ^ gray(rq))) * GROUP
            y = yi ^ gray(ry)
            for inner in range(GROUP):
                place = base + 2 * (xi ^ (inner % 2)) + (ci ^ (inner // 2))
                scr_e[y, pl.ds(place, 1)] = ref[at, inner][None]
            scr_r[y, pl.ds(base, GROUP)] = ref[at, GROUP : 2 * GROUP]
    cw = D // nb
    for y in range(nb):
        e_w[:, y * cw : (y + 1) * cw] = merged(scr_e[y])
        r_w[:, y * cw : (y + 1) * cw] = merged(scr_r[y])


def feed_rows(here, up, bias, e_w, r_w):
    hidden = dot(here, e_w[...]) + bias[...]
    k0 = 0.7978845608028654
    square = hidden * hidden
    tanh = jnp.tanh(k0 * hidden * (1.0 + 0.044715 * square))
    half = 0.5 * (1.0 + tanh)
    active = (hidden * half).astype(BF)
    slope = half + 0.5 * k0 * hidden * (1.0 - tanh * tanh) * (1.0 + 3 * 0.044715 * square)
    d_hidden = (dot_nt(up, r_w[...]) * slope).astype(BF)
    return active, d_hidden, dot(active, r_w[...]), dot_nt(d_hidden, e_w[...])


def feed_blocks(own, from_c, up, up_c, bias, e_w, r_w, start, outs):
    mx_keep, mx_send, ds_keep, ds_send, acts, dhs, eb = outs
    rows = own.shape[0]
    total = start
    for b, (here, upper) in enumerate(((own, up), (from_c, up_c))):
        active, d_hidden, mixed, d_second = feed_rows(here[...], upper[...], bias, e_w, r_w)
        acts[b * rows : (b + 1) * rows, :] = active
        dhs[b * rows : (b + 1) * rows, :] = d_hidden
        total = total + jnp.sum(d_hidden.astype(F32), 0, keepdims=True)
        if b == 0:
            mx_keep[...] = mixed
            ds_keep[...] = d_second
        else:
            mx_send[...] = mixed.astype(BF)
            ds_send[...] = d_second.astype(BF)
    eb[...] = total


def feed_near_body(slots, part_q, nb, own, from_c, up, up_c, *refs):
    n = len(slots)
    pieces, bias = refs[:n], refs[n]
    outs, (e_w, r_w, scr_e, scr_r) = refs[n + 1 : n + 8], refs[n + 8 :]
    feed_weights(slots, part_q, nb, pieces, scr_e, scr_r, e_w, r_w)
    start = jnp.zeros((1, UG), F32)
    feed_blocks(own, from_c, up, up_c, bias, e_w, r_w, start, outs)


def feed_far_body(own, from_c, up, up_c, bias, e_w, r_w, near_eb, *outs):
    feed_blocks(own, from_c, up, up_c, bias, e_w, r_w, near_eb[...], outs)


def feed_grad_body(count, part_q, nb, rw, n_left, n_right, *refs):
    left, right = refs[:n_left], refs[n_left : n_left + n_right]
    low, high, all_left, all_right, scr = refs[n_left + n_right :]
    si, qi, xi, ci, yi = places()
    cw = D // nb
    for parts, held in ((left, all_left), (right, all_right)):
        at = 0
        for part in parts:
            held[at : at + part.shape[0], :] = part[...]
            at += part.shape[0]
    for y in range(nb):
        scr[y] = dot_tn(all_left[...], all_right[:, y * cw : (y + 1) * cw])
    for ry in range(nb):
        to = low if ry < nb // 2 else high
        for rs in range(count):
            for rq in range(part_q):
                at = ((si ^ rs) * part_q + (qi ^ gray(rq))) * GROUP * rw
                part = scr[yi ^ gray(ry), pl.ds(pl.multiple_of(at, GROUP * rw), GROUP * rw), :]
                to[ry % (nb // 2), rs, rq] = part.reshape(GROUP, rw, cw).astype(BF)


def middle_back_body(
    cycle, ds_keep, from_c, from_x, upstream, middle, gain, weight, eb, d_middle, d_branch, keep, send, sums
):
    si, qi, xi, ci, yi = places()
    unit = FF // cycle
    parts = []
    for j in range(cycle // GROUP):
        part = eb[:, j * unit : (j + 1) * unit]
        for g in range(GROUP):
            parts.append(jnp.where(2 * xi + ci == g, part, jnp.zeros_like(part)))
    for j in range(FF // D):
        per = len(parts) * D // FF
        sums[4 + j : 5 + j, :] = jnp.concatenate(parts[j * per : (j + 1) * per], 1)
    d_second = ds_keep[...] + from_c[0].astype(F32) + from_x[...].astype(F32)
    xhat, spread = norm_parts(middle[...])
    up = upstream[...].astype(F32)
    total = up + norm_back(d_second, gain[...], xhat, spread)
    d_middle[...] = total
    low = total.astype(BF)
    d_branch[...] = low
    sums[0:1, :] = jnp.sum(low.astype(F32), 0, keepdims=True)
    sums[1:2, :] = jnp.sum(d_second * xhat, 0, keepdims=True)
    sums[2:3, :] = jnp.sum(d_second, 0, keepdims=True)
    sums[3:4, :] = jnp.sum(up, 0, keepdims=True)
    for rx, to in ((0, keep), (1, send)):
        for rc in range(2):
            group = 2 * (ci ^ rc) + (xi ^ rx)
            rows = weight[pl.ds(pl.multiple_of(group * HG, HG), HG), :]
            to[:, rc * HG : (rc + 1) * HG] = dot_nt(low, rows).astype(BF)


def output_grad_body(count, part_q, nb, rw, keep, from_x, from_ck, from_cx, d_branch, low, high, scr):
    si, qi, xi, ci, yi = places()
    cw = D // nb
    for ref, lanes, rx, rc in ((keep, 0, 0, 0), (from_x, 0, 1, 0), (from_ck, 1, 0, 1), (from_cx, 1, 1, 1)):
        group = 2 * (ci ^ rc) + (xi ^ rx)
        grad = dot_tn(ref[:, lanes * HG : (lanes + 1) * HG], d_branch[...])
        for y in range(nb):
            part = grad[:, y * cw : (y + 1) * cw].reshape(HG // rw, rw, cw)
            scr[y, pl.ds(group * (HG // rw), HG // rw)] = part
    for rc, to in ((0, low), (1, high)):
        for ry in range(nb):
            for rs in range(count):
                for rq in range(part_q):
                    base = ((si ^ rs) * part_q + (qi ^ gray(rq))) * GROUP
                    for rx in range(2):
                        place = base + 2 * (xi ^ rx) + (ci ^ rc)
                        to[ry, rs, rq, rx] = scr[yi ^ gray(ry), place].astype(BF)


def attend_back_body(
    count, part_q, block, lengths, keep, from_x, from_ck, from_cx, query, keys, values, att, lse,
    d_query, d_pair, scr_o, acc_k, acc_v,
):
    si, qi, xi, ci, unused = places()
    length = lengths[0, si]
    rows = GROUP * block
    for ref, lanes, rx, rc in ((keep, 0, 0, 0), (from_x, 0, 1, 0), (from_ck, 1, 0, 1), (from_cx, 1, 1, 1)):
        for r in range(count):
            at = (((si ^ r) * 2 + (xi ^ rx)) * 2 + (ci ^ rc)) * block
            at = pl.multiple_of(at, block)
            scr_o[pl.ds(at, block), :] = ref[
                r * block : (r + 1) * block, lanes * HG : (lanes + 1) * HG
            ]
    acc_k[...] = jnp.zeros_like(acc_k)
    acc_v[...] = jnp.zeros_like(acc_v)
    for i in range(count):
        span = slice(i * rows, (i + 1) * rows)
        width = (i + 1) * part_q * rows
        allowed = allowed_at(i, rows, width, part_q, length)
        d_out_all = scr_o[span, :]
        d_out_t = d_out_all.astype(F32).T
        d_queries = []
        for h in range(HEADS):
            q_here = query[h, span, :]
            k_here = keys[h, :width, :]
            d_out = d_out_all[:, h * HD : (h + 1) * HD]
            scores = dot_nt(k_here, q_here)
            logs = lse[i * HEADS + h : i * HEADS + h + 1, :]
            probs = jnp.where(allowed, jnp.exp(scores - logs), 0.0)
            d_probs = dot_nt(values[h, :width, :], d_out)
            delta = jnp.sum(
                d_out_t[h * HD : (h + 1) * HD, :] * att[h, :, span], 0, keepdims=True
            )
            d_scores = (probs * (d_probs - delta)).astype(BF)
            acc_v[h, :width, :] += dot(probs.astype(BF), d_out)
            acc_k[h, :width, :] += dot(d_scores, q_here)
            d_queries.append(dot_tn(k_here, d_scores) * SCALE)
        d_query[span, :] = jnp.concatenate(d_queries, 0).T.astype(BF)
    kind = d_pair.dtype
    for h in range(HEADS):
        d_pair[:, h * HD : (h + 1) * HD] = acc_k[h].astype(kind)
        d_pair[:, HG + h * HD : HG + (h + 1) * HD] = acc_v[h].astype(kind)


def normed_back_body(count, block, d_query, d_pair, weight, keep, send, first, scr):
    si, qi, xi, ci, yi = places()
    scr[:, :HG] = d_query[...]
    scr[:, HG : 2 * HG] = d_pair[:, :HG]
    scr[:, 2 * HG :] = jnp.where(ci == 0, d_pair[:, HG:], jnp.zeros_like(d_pair[:, HG:]))
    for rc in (1, 0):
        for rx in (1, 0):
            starts = [
                pl.multiple_of((((si ^ r) * 2 + (xi ^ rx)) * 2 + (ci ^ rc)) * block, block)
                for r in range(count)
            ]
            here = jnp.concatenate([scr[pl.ds(at, block), :] for at in starts], 0)
            out = dot_nt(here, weight[...])
            part = [d_pair[pl.ds(at, block), HG : 2 * HG] for at in starts]
            part = jnp.concatenate(part, 0)
            if rc == 1:
                send[rx, :, :D] = out.astype(BF)
                send[rx, :, D : D + HG] = part
                send[rx, :, D + HG :] = jnp.zeros((part.shape[0], WIDE - D - HG), BF)
            else:
                keep[rx] = out
                first[rx] = part


def normed_sum_body(keep, first, from_c, send, own):
    si, qi, xi, ci, yi = places()
    send[:, :D] = (keep[1] + from_c[1, :, :D].astype(F32)).astype(BF)
    send[:, D : D + HG] = jnp.where(ci == 1, first[1], from_c[1, :, D : D + HG])
    send[:, D + HG :] = from_c[1, :, D + HG :]
    own[...] = jnp.where(ci == 1, first[0], from_c[0, :, D : D + HG])


def mixed_body(count, block, middle, mx_keep, from_c, from_x, bias, *outs):
    for r in range(count):
        span = slice(r * block, (r + 1) * block)
        mixed = middle[span, :] + mx_keep[span, :] + from_c[0, span, :].astype(F32)
        mixed = mixed + from_x[span, :].astype(F32) + bias[...]
        outs[r][...] = mixed.astype(BF)


def stack_body(keep, from_c, out):
    out[0] = keep[1]
    out[1] = from_c[1]


def project_grad_body(count, part_q, rw, normed, d_query, d_pair, keep, send, sums, scr, scr_d):
    si, qi, xi, ci, yi = places()
    scr_d[:, :HG] = d_query[...]
    scr_d[:, HG : 2 * HG] = d_pair[:, :HG]
    scr_d[:, 2 * HG :] = jnp.where(ci == 0, d_pair[:, HG:], jnp.zeros_like(d_pair[:, HG:]))
    scr[...] = dot_tn(normed[...], scr_d[...])
    total = jnp.sum(scr_d[...].astype(F32), 0, keepdims=True)
    group = 2 * ci + xi
    q_sum = total[:, :HG]
    v_sum = total[:, 2 * HG :]
    zero = jnp.zeros_like(q_sum)
    sums[0:1, :] = jnp.concatenate([jnp.where(group == g, q_sum, zero) for g in range(GROUP)], 1)
    sums[1:2, :] = jnp.concatenate(
        [jnp.where(group == g, v_sum, zero) for g in range(2)] + [zero, zero], 1
    )
    for rc, to in ((0, keep), (1, send)):
        for rx in range(2):
            for rs in range(count):
                for rq in range(part_q):
                    at = ((si ^ rs) * part_q + (qi ^ gray(rq))) * GROUP + 2 * (xi ^ rx) + (ci ^ rc)
                    at = pl.multiple_of(at * rw, rw)
                    to[rx, rs, rq] = scr[pl.ds(at, rw), :].astype(BF)


def tokens_back_body(keep, from_c, from_x, tok, gain, d_middle, own, *refs):
    outs, sums = refs[:4], refs[4]
    si, qi, xi, ci, yi = places()
    block = tok.shape[1]
    g_sum = jnp.zeros((1, D), F32)
    s_sum = jnp.zeros((1, D), F32)
    for r in range(4):
        span = slice(r * block, (r + 1) * block)
        xhat, spread = norm_parts(tok[r][:, :D].astype(F32))
        d_normed = keep[0, span, :] + from_c[0, span, :D].astype(F32)
        d_normed = d_normed + from_x[span, :D].astype(F32)
        g_sum = g_sum + jnp.sum(d_normed * xhat, 0, keepdims=True)
        s_sum = s_sum + jnp.sum(d_normed, 0, keepdims=True)
        out = d_middle[span, :] + norm_back(d_normed, gain[...], xhat, spread)
        outs[r][:, :D] = out.astype(BF)
        mine, theirs = own[span, :], from_x[span, D : D + HG]
        outs[r][:, D : D + HG] = jnp.where(xi == 0, mine, theirs)
        outs[r][:, D + HG :] = jnp.where(xi == 0, theirs, mine)
    sums[0:1, :] = g_sum
    sums[1:2, :] = s_sum


def on_device(
    tokens,
    first_values,
    lengths,
    cotangent,
    first_gain,
    first_shift,
    query_weight,
    query_bias,
    key_weight,
    value_weight,
    value_bias,
    output_weight,
    output_bias,
    second_gain,
    second_shift,
    expand_weight,
    expand_bias,
    reduce_weight,
    reduce_bias,
):
    count = tokens.shape[1]
    block = tokens.shape[2]
    part_q = lax.axis_size("q")
    nb = lax.axis_size("y")
    cycle = count * part_q * GROUP
    own_rows = count * block
    seq_rows = GROUP * own_rows
    rw = D // cycle
    cw = D // nb
    si, qi, xi, ci, yi = places()

    steps = Steps()

    vectors = [
        first_gain,
        first_shift,
        query_bias,
        value_bias,
        output_bias,
        second_gain,
        second_shift,
        reduce_bias,
        expand_bias,
    ]
    width = 3 * cw + DV // nb
    payload = call(
        functools.partial(pack_rows_body, nb),
        [shape((rw, width + HG))],
        [pltpu.VMEM((rw, HG), F32)],
        query_weight,
        key_weight,
        value_weight,
        output_weight,
        *vectors,
        mib=60,
    )[0]
    by_q = jnp.concatenate([p for p, unused in gather_list(payload, "q")], 0)
    by_s = direct([by_q] * count, "s")

    blocks_y = cycle // nb // GROUP
    keep, send = call(
        functools.partial(pack_units_body, nb, blocks_y),
        [shape((2, rw, cw)), shape((2, rw, cw))],
        [],
        expand_weight,
        mib=60,
    )
    from_x = swap(send, "x", 1)
    from_c = swap(jnp.stack([pick(keep, ci ^ 1), pick(from_x, ci ^ 1)]), "c", 1)
    f_parts = [jnp.stack([pick(keep, ci), pick(from_x, ci)]), from_c, reduce_weight.reshape(GROUP, rw, cw)]

    marks = [(rs, rq) for rs in range(count) for rq in range(part_q)]
    n2 = len(marks)
    vec_rows = (3 * n2 + 15) // 16 * 16
    pack_shape = shape((2 * n2 * rw + vec_rows, 3 * HG))
    core_shape = shape((2 * n2 * rw + 2 * vec_rows, 3 * HG))
    both = jnp.concatenate([tokens[0], first_values[0]], -1)
    if nb == 2:
        half_shape = shape((n2 * rw + vec_rows, 3 * HG))
        keep, send, o_own = call(
            functools.partial(own_columns_body, nb, count),
            [half_shape, half_shape, shape((n2, rw, cw))],
            [pltpu.VMEM((vec_rows, 3 * HG), F32)],
            *by_s,
        )
        both = after(both, send, from_c)
    else:
        held = jnp.concatenate(by_s, 0)[:, :, :width]
        both = after(both, held, from_c)
    got = direct([pick(both, si ^ k) for k in range(count)], "s")
    if nb == 2:
        columns_x = swap(send, "x", 1)
        own = keep
        rows = call(both_rows_body, [shape((2, n2 * rw, 3 * HG))], [], own, columns_x)[0]
        ready = rows
    else:
        by_y = gather_list(held, "y")[1:]
        keep, send, o_both = call(
            functools.partial(pack_columns_body, nb, rw, count, [slots for unused, slots in by_y]),
            [pack_shape, pack_shape, shape((nb, n2, rw, cw))],
            [pltpu.VMEM((nb, n2, rw, width), BF), pltpu.VMEM((vec_rows, 3 * HG), F32)],
            *by_s,
            *[part for part, unused in by_y],
        )
        columns_x = swap(send, "x", 1)
        ready = send

    def with_first(parts, x):
        parts = jnp.stack(parts)
        first = parts[..., D:].reshape(parts.shape[:2] + (2, HG))
        first = lax.dynamic_index_in_dim(first, x, 2, False)
        blank = jnp.zeros(first.shape[:2] + (WIDE - D - HG,), BF)
        return jnp.concatenate([parts[..., :D], first, blank], -1)

    near = with_first(got[:2], xi ^ 1)
    steps.need(Step.tokens_near, near)
    tok_x_near = swap(near, "x", 1)
    got = list(after(tuple(got), ready, near))
    far = with_first(got[2:], xi ^ 1)
    tok = with_first(got, xi)
    tok_x_far = swap(far, "x", 1)
    tok_other = far
    if nb == 2:
        columns_y = swap(rows, "y", 1)
    steps.reach(Step.tokens, far)
    steps.reach(Step.columns_x, columns_x)
    steps.reach(Step.tokens_x, tok_x_far)

    f_piece = jnp.concatenate(after(tuple(f_parts), tok_other), 0)
    f_by_q = jnp.concatenate([p for p, unused in gather_list(f_piece, "q")], 0)
    f_by_q = f_by_q.reshape((part_q,) + f_piece.shape)
    steps.need(Step.feed_piece, f_by_q)
    f_both = steps.move(
        Step.feed_two, lambda tie: (swap(tie(f_by_q), "s", 2), swap(tie(f_by_q), "s", 1))
    )
    if nb == 2:
        columns_y = steps.before(Step.cores, columns_y)
        keep, send = call(own_cores_body, [core_shape, core_shape], [], own, columns_x, rows, columns_y)
    else:
        keep, send = call(
            functools.partial(pack_cores_body, vec_rows),
            [core_shape, core_shape],
            [],
            keep,
            steps.before(Step.cores, columns_x),
        )
    steps.reach(Step.cores, keep)

    def output_x(tie):
        if nb != 2:
            return jnp.stack([o_both, swap(tie(o_both), "x", 1)])
        return jnp.stack([o_own, swap(tie(o_own), "x", 1)])

    def output_y(tie):
        held = tie(o_x())
        return held if nb != 2 else jnp.stack([held, swap(held, "y", 1)], 1)

    o_x = steps.move(Step.output_x, output_x)
    o_all = steps.move(Step.output_wide, output_y)
    o_c = steps.move(Step.output_c, lambda tie: swap(tie(o_all()), "c", 1))
    qkv_pieces = [keep, swap(send, "c", 1)]
    qkv_slots = [marks]
    tok_c = steps.move(Step.tokens_c, lambda tie: swap(tie(tok), "c", 1))
    row = shape((1, D), F32)
    gain_one, shift_one, my_qbias, my_vbias, o_bias, gain_two, shift_two, r_bias, my_ebias = call(
        functools.partial(vectors_body, qkv_slots, part_q, rw, cycle),
        [row, row, shape((1, HG), F32), shape((1, HG), F32), row, row, row, row, shape((1, UG), F32)],
        [pltpu.VMEM((cycle, 8, 3 * HG), F32)],
        *qkv_pieces,
    )
    tok_x = [tok_x_near, tok_x_far]
    sources = [tok, *tok_x, tok_c(), *[swap(after(part, keep), "c", 1) for part in tok_x]]
    o_slots = qkv_slots
    f_three = steps.move(Step.feed_three, lambda tie: swap(tie(f_by_q), "s", 3))

    def cotangent_z(tie):
        parts = [pick(tie(cotangent[0]), si ^ k) for k in range(count)]
        steps.need(Step.cotangent_part, parts[1:])
        return direct(parts, "s")

    cot = steps.move(Step.cotangent, cotangent_z)

    heads = [shape((HEADS, seq_rows, HD))] * 3
    query, keys, values, normed, qkv_w = call(
        functools.partial(project_body, qkv_slots, count, part_q, block, rw),
        heads + [shape((seq_rows, D)), shape((D, 3 * HG))],
        [pltpu.VMEM((cycle, rw, 3 * HG), BF), pltpu.VMEM((seq_rows, HG), BF)],
        *sources,
        *qkv_pieces,
        steps.before(Step.project, gain_one),
        shift_one,
        my_qbias,
        my_vbias,
    )
    steps.reach(Step.project, query)

    def whole_keys(value):
        if part_q == 1:
            return value
        parts = gather(value.reshape(HEADS, count, GROUP * block, HD), "q")
        return jnp.moveaxis(parts, 0, 2).reshape(HEADS, part_q * seq_rows, HD)

    keys, values = whole_keys(keys), whole_keys(values)
    key_rows = keys.shape[1]
    pair_shape = shape((own_rows, 2 * HG))
    pieces, piece_slots = [], []

    def most_y(tie):
        held = tie(jnp.concatenate([f_by_q, *f_both()], 0))
        steps.need(Step.feed_part, held)
        return gather_list(held, "y")

    y_most = steps.move(Step.feed_most_y, most_y)
    att, lse, att_keep, att_send = call(
        functools.partial(attend_body, count, part_q, block),
        [
            shape((HEADS, HD, seq_rows), F32),
            shape((count * HEADS, GROUP * block), F32),
            pair_shape,
            pair_shape,
        ],
        [pltpu.VMEM((seq_rows, HG), BF)],
        lengths,
        steps.before(Step.attend, query),
        keys,
        values,
        smem=1,
    )
    steps.reach(Step.attend, att_send)
    att_x = swap(att_send, "x", 1)
    steps.reach(Step.attend_x, att_x)
    y_last = steps.move(Step.feed_three_y, lambda tie: gather_list(tie(f_three()), "y"))
    mask_tie = steps.at(Step.mask)
    upstream = call(
        functools.partial(mask_body, part_q, block),
        [shape((own_rows, D))],
        [],
        lengths,
        *after(tuple(cot()), *mask_tie),
        smem=1,
    )[0]
    up_x = steps.move(Step.upstream_x, lambda tie: swap(tie(upstream), "x", 1))
    steps.need(Step.upstream, upstream)
    att_rows = [att_keep, att_x, swap(att_keep, "c", 1), swap(att_x, "c", 1)]
    middle, second, o_w = call(
        functools.partial(output_body, o_slots, count, part_q, block, nb, rw),
        [shape((own_rows, D), F32), shape((own_rows, D)), shape((D, D))],
        [pltpu.VMEM((nb, cycle, rw, cw), BF)],
        tok,
        *att_rows,
        o_all(),
        o_c(),
        steps.before(Step.output, o_bias),
        gain_two,
        shift_two,
    )
    steps.reach(Step.output, second)

    second_x = swap(second, "x", 1)
    steps.reach(Step.second_x, second_x)
    second_c = swap(second, "c", 1)
    up_c = swap(upstream, "c", 1)
    for held, order in ((y_most(), (0, 2, 1)), (y_last(), (3,))):
        for part, ys in held:
            pieces.append(part.reshape((-1,) + f_piece.shape))
            piece_slots.append([(ry, rs, rq) for ry in ys for rs in order for rq in range(part_q)])
    half_keep = shape((2, own_rows, D), F32)
    one_keep, one_send = shape((own_rows, D), F32), shape((own_rows, D))
    outs = [one_keep, one_send, one_keep, one_send] + [shape((2 * own_rows, D))] * 2 + [shape((1, UG), F32)]
    weight_shape = (nb, cycle, rw, cw)
    mx_near, mx_send_near, ds_near, ds_send_near, acts_near, dhs_near, eb_near, e_w, r_w = call(
        functools.partial(feed_near_body, piece_slots, part_q, nb),
        outs + [shape((D, UG)), shape((UG, D))],
        [pltpu.VMEM(weight_shape, BF)] * 2,
        second,
        second_c,
        upstream,
        up_c,
        *pieces,
        steps.before(Step.feed, my_ebias),
    )
    steps.reach(Step.feed, eb_near)
    far = [second_x, swap(second_x, "c", 1), up_x(), swap(up_x(), "c", 1)]
    mx_far, mx_send_far, ds_far, ds_send_far, acts_far, dhs_far, eb_sum = call(
        feed_far_body,
        outs,
        [],
        *far,
        steps.before(Step.feed_far, my_ebias),
        e_w,
        r_w,
        eb_near,
    )
    ds_c = swap(jnp.stack([ds_send_near, ds_send_far]), "c", 1)
    xs, acts, dhs = [second, second_c] + far[:2], [acts_near, acts_far], [dhs_near, dhs_far]
    us = [upstream, up_c] + far[2:]
    grad_shape = shape((nb // 2, count, part_q, GROUP, rw, cw))

    def feed_grad(left, right):
        return call(
            functools.partial(feed_grad_body, count, part_q, nb, rw, len(left), len(right)),
            [grad_shape, grad_shape],
            [pltpu.VMEM((seq_rows, D), BF)] * 2 + [pltpu.VMEM((nb, D, cw), F32)],
            *left,
            *right,
        )

    e_low, e_high = feed_grad(xs, dhs)
    ds_c = after(ds_c, e_low)
    ds_pay = (ds_far + ds_c[1].astype(F32)).astype(BF)
    ds_x = swap(ds_pay, "x", 1)
    steps.reach(Step.d_second_c, ds_pay)
    steps.reach(Step.d_second_x, ds_x)
    e_y = steps.move(Step.expand_y, lambda tie: swap(tie(e_high), "y", gray(nb // 2)))
    r_low, r_high = feed_grad(after(acts, ds_pay), us)
    mx_send = jnp.stack([mx_send_near, mx_send_far])
    steps.need(Step.reduce, r_low)
    mx_c = steps.move(Step.mixed_c, lambda tie: swap(tie(mx_send), "c", 1))
    d_middle, d_branch, d_keep, d_send, sums_two = call(
        functools.partial(middle_back_body, cycle),
        [shape((own_rows, D), F32), shape((own_rows, D)), pair_shape, pair_shape, shape((8, D), F32)],
        [],
        ds_near,
        ds_c,
        ds_x,
        upstream,
        middle,
        steps.before(Step.middle, gain_two),
        o_w,
        eb_sum,
    )
    steps.reach(Step.middle, d_send)
    d_x = swap(d_send, "x", 1)
    steps.reach(Step.d_attended_x, d_x)
    d_c = [swap(d_keep, "c", 1), swap(d_x, "c", 1)]
    steps.reach(Step.d_attended_c, d_c[1])
    d_rows = [d_keep, d_x] + d_c

    def expand_z(tie):
        low, got = after((e_low, e_y()), *tie.values)
        part = scatter_slots(low, None, "y", got)
        part = [part[0]] + [part[k].astype(BF) for k in range(1, count)]
        steps.need(Step.expand_part, part[1:])
        return direct(part, "s")

    e_z = steps.move(Step.expand_z, expand_z)
    r_y = steps.move(Step.reduce_y, lambda tie: swap(tie(r_high), "y", gray(nb // 2)))

    def mixed_step(tie):
        pay = tie((mx_far + mx_c()[1].astype(F32)).astype(BF))
        steps.need(Step.mixed_part, pay)
        return swap(pay, "x", 1)

    mx_x = steps.move(Step.mixed_x, mixed_step)
    o_shape = shape((nb, count, part_q, 2, rw, cw))

    def output_grad(tie):
        low, high = call(
            functools.partial(output_grad_body, count, part_q, nb, rw),
            [o_shape, o_shape],
            [pltpu.VMEM((nb, cycle, rw, cw), F32)],
            *att_rows,
            tie(d_branch),
        )
        return low, high, swap(high[None], "c", 1)

    o_c_sum = steps.move(Step.output_grad, output_grad)

    d_query, d_pair = call(
        functools.partial(attend_back_body, count, part_q, block),
        [shape((seq_rows, HG)), shape((key_rows, 2 * HG), BF if part_q == 1 else F32)],
        [pltpu.VMEM((seq_rows, HG), BF)] + [pltpu.VMEM((HEADS, key_rows, HD), F32)] * 2,
        lengths,
        *d_rows,
        query,
        keys,
        values,
        steps.before(Step.attend_back, att),
        lse,
        smem=1,
    )
    steps.reach(Step.attend_back, d_query)

    def reduce_z(tie):
        low, got = after((r_low, r_y()), *tie.values)
        part = scatter_slots(low, None, "y", got)
        part = [part[0]] + [part[k].astype(BF) for k in range(1, count)]
        steps.need(Step.reduce_part, part[1:])
        return direct(part, "s")

    r_z = steps.move(Step.reduce_z, reduce_z)

    def mixed_z(tie):
        parts = call(
            functools.partial(mixed_body, count, block),
            [shape((block, D))] * count,
            [],
            middle,
            mx_near,
            mx_c(),
            mx_x(),
            tie(r_bias),
        )
        steps.need(Step.mixed_rows, parts[1:])
        return direct(parts, "s")

    mixed = steps.move(Step.mixed_z, mixed_z)
    qkv_w = steps.before(Step.normed_back, qkv_w)
    if part_q > 1:
        parts = d_pair.reshape(count, part_q, GROUP * block, 2 * HG).swapaxes(0, 1)
        d_pair = scatter_sum(relative(parts, "q"), "q").reshape(seq_rows, 2 * HG).astype(BF)
    dn_keep, dn_send, first_keep = call(
        functools.partial(normed_back_body, count, block),
        [half_keep, shape((2, own_rows, WIDE)), shape((2, own_rows, HG))],
        [pltpu.VMEM((seq_rows, 3 * HG), BF)],
        d_query,
        d_pair,
        qkv_w,
    )
    steps.reach(Step.normed_back, dn_keep)
    dn_c = swap(dn_send, "c", 1)
    dn_pay, first_own = call(
        normed_sum_body,
        [shape((own_rows, WIDE)), shape((own_rows, HG))],
        [],
        dn_keep,
        first_keep,
        dn_c,
    )
    steps.reach(Step.d_normed_c, dn_pay)
    dn_x = swap(dn_pay, "x", 1)
    normed = after(normed, dn_pay)
    p_shape = shape((2, count, part_q, rw, 3 * HG))
    p_keep, p_send, sums_qv = call(
        functools.partial(project_grad_body, count, part_q, rw),
        [p_shape, p_shape, shape((2, D), F32)],
        [pltpu.VMEM((D, 3 * HG), F32), pltpu.VMEM((seq_rows, 3 * HG), BF)],
        steps.before(Step.project_grad, normed),
        d_query,
        d_pair,
    )
    steps.reach(Step.project_grad, p_keep)
    steps.reach(Step.d_normed_x, dn_x)
    p_from_c = swap(p_send, "c", 1)
    p_pay = call(stack_body, [shape((2, count, part_q, rw, 3 * HG))], [], p_keep, p_from_c)[0]
    steps.need(Step.columns_part, p_pay)
    p_from_x = steps.move(Step.columns_grad_x, lambda tie: swap(tie(p_pay), "x", 1))
    *gt, sums_one = call(
        tokens_back_body,
        [shape((block, D + DV))] * count + [shape((2, D), F32)],
        [],
        dn_keep,
        dn_c,
        dn_x,
        tok,
        steps.before(Step.tokens_back, gain_one),
        d_middle,
        first_own,
    )
    steps.reach(Step.tokens_back, gt[0])
    home_cols = 2 * cw + DV // nb
    n_rows = count * part_q
    flat = (steps.before(Step.columns_home, p_keep[0]), p_from_c[0], p_from_x()[0], p_from_x()[1])
    y_low, y_high = call(
        functools.partial(columns_home_body, nb, n_rows),
        [shape((nb // 2, n_rows, rw, home_cols), F32), shape((nb // 2, n_rows, rw, home_cols))],
        [pltpu.VMEM((nb, rw, home_cols), F32)],
        *[v.reshape(-1, rw, 3 * HG) for v in flat],
    )
    steps.reach(Step.columns_home, y_high)
    steps.need(Step.columns_sent, y_high)
    gt = steps.move(Step.tokens_z, lambda tie: direct(tie(gt), "s"))()
    steps.reach(Step.tokens_z, gt[1])
    back = in_place(gt, "s")[None]
    grad_tokens, grad_first = back[..., :D], back[..., D:]

    def sum_q(value):
        return scatter_sum(value, "q")

    o_low, o_high, o_got = o_c_sum()
    o_part = steps.move(
        Step.output_y, lambda tie: scatter_sum(scatter_slots(tie(o_low)[None], None, "c", o_got), "y")
    )()
    o_part = jnp.moveaxis(o_part, 2, 0)
    o_part = scatter_slots(o_part[:1], o_part[1:], "x")
    qkv_part = scatter_slots(y_low, y_high, "y").reshape(count, part_q, rw, home_cols)
    home_pay = jnp.concatenate([steps.before(Step.home, qkv_part), o_part], -1)
    steps.reach(Step.home, home_pay)
    home = sum_q(direct_sum(home_pay, "s"))
    q_home, k_home, v_home = home[:, :cw], home[:, cw : 2 * cw], home[:, 2 * cw : home_cols]
    o_home = home[:, home_cols:]
    mixed_out = in_place(after(tuple(mixed()), *steps.at(Step.mixed_out)), "s")[None]

    def to_group(part):
        part = part.astype(BF)
        keep = lax.dynamic_index_in_dim(part, ci, 1, keepdims=False)
        got = swap(lax.dynamic_index_in_dim(part, ci ^ 1, 1, keepdims=False), "c", 1)
        both = jnp.stack([keep, got], 1)
        return pick(both, xi), swap(pick(both, xi ^ 1), "x", 1)

    e_z = after(tuple(e_z()), *steps.at(Step.expand_home))
    e_home = sum_q(sum(part.astype(F32) for part in e_z))
    e_home = call(
        functools.partial(units_home_body, blocks_y),
        [shape((rw, FF // nb), F32)],
        [],
        *to_group(e_home.reshape(2, 2, rw, cw)),
    )[0]
    r_z = after(tuple(r_z()), *steps.at(Step.reduce_home))
    r_home = sum_q(sum(part.astype(F32) for part in r_z)).reshape(GROUP * rw, cw)

    sums = after(jnp.concatenate([sums_one, sums_qv, sums_two], 0), *steps.at(Step.sums))
    for axis in ("c", "x", "y", "q"):
        sums = whole_sum(sums, axis)
    sums = sum(direct([sums] * count, "s"))
    place = ((si * part_q + qi) * 2 + xi) * 2 + ci
    part = lax.dynamic_slice_in_dim(sums[:8], place * rw, rw, 1)
    vb_home = lax.dynamic_slice_in_dim(sums[3], place * (DV // cycle), DV // cycle, 0)
    eb_home = pick(sums[8:].reshape(cycle, -1), place)
    return (
        mixed_out,
        grad_tokens,
        grad_first,
        part[0],
        part[1],
        q_home,
        part[2],
        k_home,
        v_home,
        vb_home,
        o_home,
        part[4],
        part[5],
        part[6],
        e_home,
        eb_home,
        r_home,
        part[7],
    )


def solution(mesh):
    cycle, nb = mesh.devices.shape
    sequences = 4
    fine = Mesh(
        mesh.devices.reshape(sequences, cycle // (sequences * GROUP), 2, 2, nb),
        ("s", "q", "x", "c", "y"),
    )
    seq = ("s", "q", "x", "c")
    rows = P("y", None, seq, None)
    matrix = P(seq, "y")
    vector = P(seq)
    in_specs = (
        rows,
        rows,
        P("y", None),
        rows,
        vector,
        vector,
        matrix,
        vector,
        matrix,
        matrix,
        vector,
        matrix,
        vector,
        vector,
        vector,
        matrix,
        vector,
        matrix,
        vector,
    )
    out_specs = (
        rows,
        rows,
        rows,
        vector,
        vector,
        matrix,
        vector,
        matrix,
        matrix,
        vector,
        matrix,
        vector,
        vector,
        vector,
        matrix,
        vector,
        matrix,
        vector,
    )
    return jax.shard_map(
        on_device, mesh=fine, in_specs=in_specs, out_specs=out_specs, check_vma=False
    )
```

```python
import enum
import functools

import jax
import jax.numpy as jnp
from jax import lax
from jax.experimental import pallas as pl
from jax.experimental.pallas import tpu as pltpu
from jax.sharding import Mesh, PartitionSpec as P

D = 768
H = 12
HD = 64
FF = 3072
DV = 384
GROUP = 4
HG = D // GROUP
HEADS = HG // HD
UG = FF // GROUP
WIDE = 1024

EPS = 1e-05
NEG = -1e30
SCALE = HD**-0.5
BF = jnp.bfloat16
F32 = jnp.float32
VMEM = pl.BlockSpec(memory_space=pltpu.VMEM)
SMEM = pl.BlockSpec(memory_space=pltpu.SMEM)


def gray(k):
    return k ^ (k >> 1)


def swap(value, axis, mask):
    return lax.ppermute(value, axis, [(i, i ^ mask) for i in range(lax.axis_size(axis))])


def pick(blocks, index):
    return lax.dynamic_index_in_dim(blocks, index, 0, keepdims=False)


def after(value, *others):
    return lax.optimization_barrier((value, *others))[0]


class Step(enum.IntEnum):
    attend = enum.auto()
    attend_back = enum.auto()
    attend_x = enum.auto()
    columns_grad_x = enum.auto()
    columns_home = enum.auto()
    columns_part = enum.auto()
    columns_sent = enum.auto()
    columns_x = enum.auto()
    cores = enum.auto()
    cotangent = enum.auto()
    cotangent_part = enum.auto()
    d_attended_c = enum.auto()
    d_attended_x = enum.auto()
    d_normed_c = enum.auto()
    d_normed_x = enum.auto()
    d_second_c = enum.auto()
    d_second_x = enum.auto()
    expand_home = enum.auto()
    expand_part = enum.auto()
    expand_y = enum.auto()
    expand_z = enum.auto()
    feed = enum.auto()
    feed_far = enum.auto()
    feed_most_y = enum.auto()
    feed_part = enum.auto()
    feed_piece = enum.auto()
    feed_three = enum.auto()
    feed_three_y = enum.auto()
    feed_two = enum.auto()
    home = enum.auto()
    mask = enum.auto()
    middle = enum.auto()
    mixed_c = enum.auto()
    mixed_out = enum.auto()
    mixed_part = enum.auto()
    mixed_rows = enum.auto()
    mixed_x = enum.auto()
    mixed_z = enum.auto()
    normed_back = enum.auto()
    output = enum.auto()
    output_c = enum.auto()
    output_grad = enum.auto()
    output_wide = enum.auto()
    output_x = enum.auto()
    output_y = enum.auto()
    project = enum.auto()
    project_grad = enum.auto()
    reduce = enum.auto()
    reduce_home = enum.auto()
    reduce_part = enum.auto()
    reduce_y = enum.auto()
    reduce_z = enum.auto()
    second_x = enum.auto()
    sums = enum.auto()
    tokens = enum.auto()
    tokens_back = enum.auto()
    tokens_c = enum.auto()
    tokens_near = enum.auto()
    tokens_x = enum.auto()
    tokens_z = enum.auto()
    upstream = enum.auto()
    upstream_x = enum.auto()


PLAN = {
    Step.feed_two: ((), None),
    Step.output_x: ((), None),
    Step.output_c: ((Step.output_wide,), Step.project),
    Step.tokens_c: ((Step.columns_x,), None),
    Step.feed_three: ((Step.attend_x,), Step.attend),
    Step.cotangent: ((Step.project,), None),
    Step.feed_most_y: ((Step.attend_x,), None),
    Step.feed_three_y: ((), None),
    Step.mask: ((), None),
    Step.upstream_x: ((), None),
    Step.expand_y: ((), None),
    Step.mixed_c: ((Step.d_second_c,), Step.middle),
    Step.expand_z: ((Step.middle,), Step.normed_back),
    Step.reduce_y: ((Step.middle,), None),
    Step.mixed_x: ((Step.d_attended_x,), Step.normed_back),
    Step.output_grad: ((Step.d_normed_c,), None),
    Step.reduce_z: ((Step.attend_back,), Step.tokens_back),
    Step.mixed_z: ((Step.attend_back,), None),
    Step.columns_grad_x: ((), None),
    Step.tokens_z: ((), None),
    Step.output_y: ((), None),
    Step.mixed_out: ((Step.home,), None),
    Step.expand_home: ((Step.tokens_z,), None),
    Step.reduce_home: ((Step.tokens_z,), None),
    Step.sums: ((Step.home,), None),
    Step.output_wide: ((Step.output_x,), None),
}
EARLY = {
    Step.upstream: Step.output,
    Step.reduce: Step.middle,
    Step.expand_part: None,
    Step.mixed_part: Step.attend_back,
    Step.reduce_part: Step.normed_back,
    Step.mixed_rows: Step.normed_back,
    Step.columns_part: None,
    Step.feed_part: Step.attend,
    Step.cotangent_part: Step.attend,
    Step.columns_sent: None,
    Step.feed_piece: None,
    Step.tokens_near: Step.cores,
}


class Tie:
    def __init__(self, values):
        self.values = values

    def __call__(self, value):
        return after(value, *self.values) if self.values else value


class Steps:
    def __init__(self):
        self.reached, self.waiting, self.due = {}, {}, {}

    def reach(self, name, value):
        self.reached[name] = value
        for name, start in list(self.waiting.items()):
            self.begin(name, start)

    def at(self, name):
        return [self.reached[step] for step in PLAN[name][0]]

    def begin(self, name, start):
        if all(step in self.reached for step in PLAN[name][0]):
            self.waiting.pop(name, None)
            self.reached[name] = None
            result = start(Tie(self.at(name)))
            self.reached[name] = jax.tree.leaves(result)[-1]
            self.due.setdefault(PLAN[name][1], []).extend(jax.tree.leaves(result))
            self.results[name] = result
            for other, begin in list(self.waiting.items()):
                self.begin(other, begin)

    results = None

    def move(self, name, start):
        if self.results is None:
            self.results = {}
        self.waiting[name] = start
        self.begin(name, start)
        return lambda: self.results[name]

    def need(self, name, value):
        self.due.setdefault(EARLY.get(name), []).extend(jax.tree.leaves(value))

    def before(self, name, value):
        due = self.due.pop(name, [])
        return after(value, *due) if due else value


def relative(blocks, axis):
    n = lax.axis_size(axis)
    if n == 1:
        return blocks
    me = lax.axis_index(axis)
    return jnp.stack([pick(blocks, gray(r) ^ me) for r in range(n)], 0)


def absolute(rel, axis):
    n = lax.axis_size(axis)
    if n == 1:
        return rel
    me = lax.axis_index(axis)
    return jnp.stack([pick(rel, gray(a ^ me)) for a in range(n)], 0)


def gather_list(value, axis):
    pieces = [(value[None], [0])]
    size = 1
    while size < lax.axis_size(axis):
        held = pieces[0][0] if size == 1 else jnp.concatenate([p for p, unused in pieces], 0)
        pieces.append((swap(held, axis, gray(size)), list(range(size, 2 * size))))
        size *= 2
    return pieces


def gather(value, axis):
    return absolute(jnp.concatenate([p for p, unused in gather_list(value, axis)], 0), axis)


def direct(parts, axis):
    return [parts[0]] + [swap(parts[k], axis, k) for k in range(1, len(parts))]


def in_place(parts, axis):
    held = jnp.stack(parts)
    me = lax.axis_index(axis)
    return jnp.stack([pick(held, a ^ me) for a in range(len(parts))])


def direct_sum(rel, axis):
    got = direct([rel[0].astype(F32)] + [rel[k].astype(BF) for k in range(1, rel.shape[0])], axis)
    return sum(part.astype(F32) for part in got)


def scatter_slots(low, high, axis, got=None):
    while True:
        half = low.shape[0]
        if got is None:
            got = swap(high.astype(BF), axis, gray(half))
        total = low.astype(F32) + got.astype(F32)
        got = None
        if half == 1:
            return total[0]
        low, high = total[: half // 2], total[half // 2 :]


def scatter_sum(rel, axis):
    half = rel.shape[0] // 2
    return rel[0] if half == 0 else scatter_slots(rel[:half], rel[half:], axis)


def exchange(blocks, axis):
    n = lax.axis_size(axis)
    rel = relative(blocks, axis)
    bit = 1
    while bit < n:
        shape = rel.shape
        pairs = rel.reshape((n // (2 * bit), 2, bit) + shape[1:])
        got = swap(pairs[:, 1], axis, gray(bit))
        rel = jnp.stack([pairs[:, 0], got], 1).reshape(shape)
        bit *= 2
    return absolute(rel, axis)


def whole_sum(value, axis):
    n = lax.axis_size(axis)
    bit = 1
    while bit < n:
        value = value + swap(value, axis, bit)
        bit *= 2
    return value


def norm_parts(values):
    centre = values - jnp.mean(values, -1, keepdims=True)
    spread = lax.rsqrt(jnp.mean(centre * centre, -1, keepdims=True) + EPS)
    return centre * spread, spread


def norm_back(d_out, gain, xhat, spread):
    e = d_out * gain
    return spread * (
        e - jnp.mean(e, -1, keepdims=True) - xhat * jnp.mean(e * xhat, -1, keepdims=True)
    )


def dot(a, b):
    return jnp.dot(a, b, preferred_element_type=F32)


def dot_nt(a, b):
    return lax.dot_general(a, b, (((1,), (1,)), ((), ())), preferred_element_type=F32)


def dot_tn(a, b):
    return lax.dot_general(a, b, (((0,), (0,)), ((), ())), preferred_element_type=F32)


def places():
    return tuple(lax.axis_index(a) for a in ("s", "q", "x", "c", "y"))


def merged(blocks):
    n, rows, cols = blocks.shape
    if rows % 16 == 0:
        return blocks.reshape(n * rows, cols)
    return blocks.astype(F32).reshape(n * rows, cols).astype(BF)


def split_rows(rows, n):
    size = rows.shape[0] // n
    if size % 16 == 0:
        return [rows[i * size : (i + 1) * size] for i in range(n)]
    wide = rows.astype(F32)
    return [wide[i * size : (i + 1) * size].astype(BF) for i in range(n)]


def shape(dims, kind=BF):
    return jax.ShapeDtypeStruct(tuple(dims), kind)


def call(body, outs, scratch, *operands, smem=0, mib=24, direct_in=False):
    arrays = operands[smem:]
    n, n_out = len(arrays), len(outs)
    if direct_in:
        return pl.pallas_call(
            body,
            out_shape=tuple(outs),
            in_specs=[SMEM] * smem + [VMEM] * n,
            out_specs=tuple(VMEM for unused in outs),
            scratch_shapes=scratch,
            cost_estimate=pl.CostEstimate(flops=1, bytes_accessed=1, transcendentals=0),
            compiler_params=pltpu.CompilerParams(vmem_limit_bytes=mib * 1024 * 1024),
        )(*operands)

    def copied(*refs):
        scalars, sources = refs[:smem], refs[smem : smem + n]
        results = refs[smem + n : smem + n + n_out]
        own = refs[smem + n + n_out : len(refs) - n - 1]
        held, sems = refs[len(refs) - n - 1 : -1], refs[-1]
        copies = [
            pltpu.make_async_copy(sources[i], held[i], sems.at[i]) for i in range(n)
        ]
        for copy in copies:
            copy.start()
        for copy in copies:
            copy.wait()
        body(*scalars, *held, *results, *own)

    return pl.pallas_call(
        copied,
        out_shape=tuple(outs),
        in_specs=[SMEM] * smem + [pl.BlockSpec(memory_space=pl.ANY)] * n,
        out_specs=tuple(VMEM for unused in outs),
        scratch_shapes=[*scratch]
        + [pltpu.VMEM(v.shape, v.dtype) for v in arrays]
        + [pltpu.SemaphoreType.DMA((n,))],
        cost_estimate=pl.CostEstimate(flops=1, bytes_accessed=1, transcendentals=0),
        compiler_params=pltpu.CompilerParams(vmem_limit_bytes=mib * 1024 * 1024),
    )(*operands)


def pack_rows_body(nb, query, keys, values, output, *refs):
    vectors = refs[:9]
    out, rows = refs[9:]
    cw, vw = D // nb, DV // nb
    out[:, :cw] = query[...]
    out[:, cw : 2 * cw] = keys[...]
    out[:, 2 * cw : 3 * cw] = output[...]
    out[:, 3 * cw : 3 * cw + vw] = values[...]
    rows[...] = jnp.zeros_like(rows)
    for j, vector in enumerate(vectors):
        size = vector.shape[0]
        rows[j : j + 1, :size] = vector[...].astype(F32).reshape(1, size)
    out[:, 3 * cw + vw :] = rows[...].astype(BF)


def own_columns_body(nb, n_own, *refs):
    owns = refs[:n_own]
    keep, send, out, rows = refs[n_own:]
    si, qi, xi, ci, yi = places()
    cw, vw = D // nb, DV // nb
    per = owns[0].shape[0]
    kept, sent = [], []
    rows[...] = jnp.zeros_like(rows)
    for j in range(n_own):
        for q in range(per):
            held = owns[j][q].astype(F32)
            out[j * per + q] = owns[j][q, :, 2 * cw : 3 * cw]
            values = held[:, 3 * cw : 3 * cw + vw]
            parts = [
                jnp.concatenate([held[:, x * HG : (x + 1) * HG], held[:, cw + x * HG : cw + (x + 1) * HG]], 1)
                for x in range(2)
            ]
            kept.append(jnp.concatenate([jnp.where(xi == 0, *parts), values], 1))
            sent.append(jnp.concatenate([jnp.where(xi == 0, *parts[::-1]), values], 1))
            for v in range(9):
                at = 3 * (j * per + q) + v // 3
                start = 3 * cw + vw
                rows[at : at + 1, (v % 3) * HG : (v % 3 + 1) * HG] = held[v : v + 1, start : start + HG]
    keep[...] = jnp.concatenate(kept + [rows[...]], 0).astype(BF)
    send[...] = jnp.concatenate(sent + [rows[...]], 0).astype(BF)


def both_rows_body(mine, from_x, out):
    out[0] = mine[: out.shape[1], :]
    out[1] = from_x[: out.shape[1], :]


def own_cores_body(mine, from_x, both, from_y, keep, send):
    si, qi, xi, ci, yi = places()
    size = both.shape[1]
    kept, sent = [], []
    for rx in range(2):
        own, other = both[rx].astype(F32), from_y[rx].astype(F32)
        halves = [jnp.where(yi == y, own, other) for y in range(2)]
        values = jnp.where(xi == 0, halves[0][:, 2 * HG :], halves[1][:, 2 * HG :])
        columns = [half[:, : 2 * HG] for half in halves]
        kept.append(jnp.concatenate([jnp.where(ci == 0, *columns), values], 1))
        sent.append(jnp.concatenate([jnp.where(ci == 0, *columns[::-1]), values], 1))
    vectors = [ref[size:, :].astype(F32) for ref in (mine, from_x)]
    keep[...] = jnp.concatenate(kept + vectors, 0).astype(BF)
    send[...] = jnp.concatenate(sent + vectors, 0).astype(BF)


def pack_columns_body(nb, rw, n_own, y_slots, *refs):
    owns = refs[:n_own]
    pieces = refs[n_own : n_own + len(y_slots)]
    keep, send, out, scr, rows = refs[n_own + len(y_slots) :]
    si, qi, xi, ci, yi = places()
    cw, vw = D // nb, DV // nb
    per = owns[0].shape[0]
    n2 = n_own * per
    width = 3 * cw + vw
    rows[...] = jnp.zeros_like(rows)
    for j in range(n_own):
        scr[yi, j * per : (j + 1) * per] = owns[j][:, :, :width]
        out[0, j * per : (j + 1) * per] = owns[j][:, :, 2 * cw : 3 * cw]
        for q in range(per):
            held = owns[j][q, :, width:].astype(F32)
            for v in range(9):
                at = 3 * (j * per + q) + v // 3
                rows[at : at + 1, (v % 3) * HG : (v % 3 + 1) * HG] = held[v : v + 1]
    for ref, slots in zip(pieces, y_slots):
        for at, ry in enumerate(slots):
            scr[yi ^ gray(ry)] = ref[at]
            out[ry] = ref[at, :, :, 2 * cw : 3 * cw]
    both = ([], [])
    for n in range(n2):
        full = [
            jnp.concatenate([scr[y, n][:, a : a + w].astype(F32) for y in range(nb)], 1)
            for a, w in ((0, cw), (cw, cw), (3 * cw, vw))
        ]

        def part(x, c):
            cols = [v[:, (2 * c + x) * HG : (2 * c + x + 1) * HG] for v in full[:2]]
            return jnp.concatenate(cols + [full[2][:, x * HG : (x + 1) * HG]], 1)

        for c in range(2):
            one, two = part(0, c), part(1, c)
            both[c].append((jnp.where(xi == 0, one, two), jnp.where(xi == 0, two, one)))
    for which, ref in ((0, keep), (1, send)):
        parts = [pair[which] for c in range(2) for pair in both[c]] + [rows[...]]
        ref[...] = jnp.concatenate(parts, 0).astype(BF)


def pack_cores_body(vec_rows, mine, from_x, keep, send):
    si, qi, xi, ci, yi = places()
    half = (mine.shape[0] - vec_rows) // 2
    parts = [], []
    for ref in (mine, from_x):
        a, b = ref[:half].astype(F32), ref[half : 2 * half].astype(F32)
        parts[0].append(jnp.where(ci == 0, a, b))
        parts[1].append(jnp.where(ci == 0, b, a))
    vectors = [ref[2 * half :].astype(F32) for ref in (mine, from_x)]
    keep[...] = jnp.concatenate(parts[0] + vectors, 0).astype(BF)
    send[...] = jnp.concatenate(parts[1] + vectors, 0).astype(BF)


def vectors_body(slots, part_q, rw, cycle, *refs):
    pieces = refs[: 2 * len(slots)]
    gain_one, shift_one, q_bias, v_bias, o_bias, gain_two, shift_two, r_bias, e_bias, scr = refs[
        2 * len(slots) :
    ]
    si, qi, xi, ci, yi = places()
    for stage, marks in enumerate(slots):
        for rc in range(2):
            for rx in range(2):
                ref = pieces[2 * stage + rc]
                size = (3 * len(marks) + 15) // 16 * 16
                at = ref.shape[0] - (2 - rx) * size
                rows = ref[at : at + size].astype(F32)
                for at, (rs, rq) in enumerate(marks):
                    place = ((si ^ rs) * part_q + (qi ^ gray(rq))) * GROUP
                    place = place + 2 * (xi ^ rx) + (ci ^ rc)
                    scr[pl.ds(place, 1), 0:3] = rows[3 * at : 3 * at + 3][None]

    def whole(j, size):
        held = scr[:, j // 3, (j % 3) * HG : (j % 3) * HG + size]
        wide = cycle * size
        lane = lax.broadcasted_iota(jnp.int32, (size, wide), 1)
        row = lax.broadcasted_iota(jnp.int32, (size, wide), 0)
        spread = jnp.where(lane % size == row, 1.0, 0.0).astype(BF)
        out = dot(held.astype(BF), spread)
        mark = lax.broadcasted_iota(jnp.int32, (cycle, wide), 1) // size
        row = lax.broadcasted_iota(jnp.int32, (cycle, wide), 0)
        return jnp.sum(jnp.where(mark == row, out, 0.0), 0, keepdims=True)

    for j, ref in ((0, gain_one), (1, shift_one), (4, o_bias), (5, gain_two), (6, shift_two), (7, r_bias)):
        ref[...] = whole(j, rw)
    query = whole(2, rw)
    group = 2 * ci + xi
    total = jnp.zeros((1, HG), F32)
    for g in range(GROUP):
        total = total + jnp.where(group == g, query[:, g * HG : (g + 1) * HG], 0.0)
    q_bias[...] = total
    value = whole(3, DV // cycle)
    v_bias[...] = jnp.where(xi == 0, value[:, :HG], value[:, HG:])
    unit = FF // cycle
    parts = []
    for j in range(cycle // GROUP):
        held = scr[j * GROUP + 2 * xi + ci]
        parts.append(held[2:3, 2 * HG : 2 * HG + unit])
    e_bias[...] = jnp.concatenate(parts, 1)


def pack_units_body(nb, blocks_y, expand, keep, send):
    si, qi, xi, ci, yi = places()
    unit = FF // (blocks_y * GROUP * nb)

    def part(x, c):
        cols = [expand[:, (GROUP * b + 2 * x + c) * unit : (GROUP * b + 2 * x + c + 1) * unit] for b in range(blocks_y)]
        return jnp.concatenate([v.astype(F32) for v in cols], 1)

    for c in range(2):
        one, two = part(0, c), part(1, c)
        keep[c] = jnp.where(xi == 0, one, two).astype(BF)
        send[c] = jnp.where(xi == 0, two, one).astype(BF)


def units_home_body(blocks_y, mine, other, out):
    si, qi, xi, ci, yi = places()
    unit = mine.shape[2] // blocks_y
    for b in range(blocks_y):
        for g in range(GROUP):
            total = jnp.zeros((mine.shape[1], unit), F32)
            for rx, ref in ((0, mine), (1, other)):
                for rc in range(2):
                    here = 2 * (xi ^ rx) + (ci ^ rc) == g
                    part = ref[rc, :, b * unit : (b + 1) * unit].astype(F32)
                    total = total + jnp.where(here, part, 0.0)
            at = (GROUP * b + g) * unit
            out[:, at : at + unit] = total


def columns_home_body(nb, n, keep, from_c, x_keep, x_from_c, low, high, scr):
    si, qi, xi, ci, yi = places()
    cw, vw = D // nb, DV // nb
    sources = ((0, 0, keep), (0, 1, from_c), (1, 0, x_keep), (1, 1, x_from_c))
    for s in range(n):
        full = []
        for kind in range(3):
            groups = []
            for g in range(GROUP if kind < 2 else 2):
                total = jnp.zeros((keep.shape[1], HG), F32)
                for rx, rc, ref in sources:
                    here = 2 * (ci ^ rc) + (xi ^ rx) == g
                    part = ref[s, :, kind * HG : (kind + 1) * HG].astype(F32)
                    total = total + jnp.where(here, part, 0.0)
                groups.append(total)
            full.append(jnp.concatenate(groups, 1))
        for y in range(nb):
            scr[y] = jnp.concatenate(
                [
                    full[0][:, y * cw : (y + 1) * cw],
                    full[1][:, y * cw : (y + 1) * cw],
                    full[2][:, y * vw : (y + 1) * vw],
                ],
                1,
            )
        for ry in range(nb):
            to = low if ry < nb // 2 else high
            to[ry % (nb // 2), s] = scr[yi ^ gray(ry)].astype(to.dtype)


def project_body(slots, count, part_q, block, rw, *refs):
    n_pieces = 2 * len(slots)
    sources = refs[:6]
    pieces = refs[6 : 6 + n_pieces]
    gain, shift, q_bias, v_bias = refs[6 + n_pieces : 10 + n_pieces]
    query, keys, values, normed, weight, scr_w, scr_f = refs[10 + n_pieces :]
    si, qi, xi, ci, unused = places()
    for stage, marks in enumerate(slots):
        for at, (rs, rq) in enumerate(marks):
            base = ((si ^ rs) * part_q + (qi ^ gray(rq))) * GROUP
            for rc in range(2):
                ref = pieces[2 * stage + rc]
                n2 = len(marks)
                held = split_rows(ref[: 2 * n2 * rw], 2 * n2)
                for rx in range(2):
                    place = base + 2 * (xi ^ rx) + (ci ^ rc)
                    scr_w[pl.ds(place, 1)] = held[rx * n2 + at][None]
    weight[...] = merged(scr_w[...])
    for pair in range(4):
        rx, rc = pair % 2, pair // 2
        for r in range(count):
            held = sources[3 * rc : 3 * rc + 3]
            here = held[0][r] if rx == 0 else held[1 + r // 2][r % 2]
            at = (((si ^ r) * 2 + (xi ^ rx)) * 2 + (ci ^ rc)) * block
            at = pl.multiple_of(at, block)
            xhat, unused = norm_parts(here[:, :D].astype(F32))
            normed[pl.ds(at, block), :] = (xhat * gain[...] + shift[...]).astype(BF)
            scr_f[pl.ds(at, block), :] = here[:, D : D + HG]
    rows = GROUP * block
    for i in range(count):
        span = slice(i * rows, (i + 1) * rows)
        out = dot(normed[span, :], weight[...])
        q_low = (out[:, :HG] + q_bias[...]).astype(BF) * SCALE
        k_low = out[:, HG : 2 * HG].astype(BF)
        v_low = (out[:, 2 * HG :] + v_bias[...]).astype(BF)
        v_low = jnp.where(ci == 0, v_low, scr_f[span, :])
        for h in range(HEADS):
            cols = slice(h * HD, (h + 1) * HD)
            query[h, span, :] = q_low[:, cols].astype(BF)
            keys[h, span, :] = k_low[:, cols]
            values[h, span, :] = v_low[:, cols]


def allowed_at(i, rows, width, part_q, length):
    unused, qi, *unused = places()
    row_pos = (i * part_q + qi) * rows + lax.broadcasted_iota(jnp.int32, (1, rows), 1)
    last = jnp.minimum(row_pos, length - 1)
    return lax.broadcasted_iota(jnp.int32, (width, rows), 0) <= last


def attend_body(count, part_q, block, lengths, query, keys, values, att, lse, keep, send, scr):
    si, qi, xi, ci, unused = places()
    length = lengths[0, si]
    rows = GROUP * block
    for i in range(count):
        span = slice(i * rows, (i + 1) * rows)
        width = (i + 1) * part_q * rows
        allowed = allowed_at(i, rows, width, part_q, length)
        outs = []
        for h in range(HEADS):
            scores = dot_nt(keys[h, :width, :], query[h, span, :])
            scores = jnp.where(allowed, scores, NEG)
            peak = jnp.max(scores, 0, keepdims=True)
            weights = jnp.exp(scores - peak)
            total = jnp.sum(weights, 0, keepdims=True)
            out = dot_tn(values[h, :width, :], weights.astype(BF)) * (1.0 / total)
            att[h, :, span] = out
            lse[i * HEADS + h : i * HEADS + h + 1, :] = peak + jnp.log(total)
            outs.append(out)
        scr[span, :] = jnp.concatenate(outs, 0).T.astype(BF)
    for rx, to in ((0, keep), (1, send)):
        for rc in range(2):
            for r in range(count):
                at = (((si ^ r) * 2 + (xi ^ rx)) * 2 + (ci ^ rc)) * block
                to[r * block : (r + 1) * block, rc * HG : (rc + 1) * HG] = scr[
                    pl.ds(pl.multiple_of(at, block), block), :
                ]


def mask_body(part_q, block, lengths, *refs):
    parts, out = refs[:-1], refs[-1]
    si, qi, xi, ci, unused = places()
    for r, part in enumerate(parts):
        start = (((si ^ r) * part_q + qi) * GROUP + 2 * xi + ci) * block
        row = start + lax.broadcasted_iota(jnp.int32, (block, 1), 0)
        here = jnp.where(row < lengths[0, si], part[...].astype(F32), 0.0)
        out[r * block : (r + 1) * block, :] = here.astype(BF)


def output_body(
    slots, count, part_q, block, nb, rw, tok, keep, from_x, from_ck, from_cx, *refs
):
    pieces = refs[:2]
    bias, gain, shift, middle, second, weight, scr = refs[2:]
    si, qi, xi, ci, yi = places()
    for stage, marks in enumerate(slots):
        for rc in range(2):
            for rx in range(2):
                for at, (rs, rq) in enumerate(marks):
                    place = ((si ^ rs) * part_q + (qi ^ gray(rq))) * GROUP
                    place = place + 2 * (xi ^ rx) + (ci ^ rc)
                    for ry in range(nb):
                        scr[yi ^ gray(ry), pl.ds(place, 1)] = pieces[rc][rx, ry, at][None]
    for y in range(nb):
        cw = D // nb
        weight[:, y * cw : (y + 1) * cw] = merged(scr[y])
    tokens = [tok[r][:, :D].astype(F32) for r in range(count)]
    total = jnp.concatenate(tokens, 0) + bias[...]
    for ref, lanes, rx, rc in ((keep, 0, 0, 0), (from_x, 0, 1, 0), (from_ck, 1, 0, 1), (from_cx, 1, 1, 1)):
        group = 2 * (ci ^ rc) + (xi ^ rx)
        rows = weight[pl.ds(pl.multiple_of(group * HG, HG), HG), :]
        total = total + dot(ref[:, lanes * HG : (lanes + 1) * HG], rows)
    middle[...] = total
    xhat, unused = norm_parts(total)
    second[...] = (xhat * gain[...] + shift[...]).astype(BF)


def feed_weights(slots, part_q, nb, pieces, scr_e, scr_r, e_w, r_w):
    si, qi, xi, ci, yi = places()
    for ref, marks in zip(pieces, slots):
        for at, (ry, rs, rq) in enumerate(marks):
            base = ((si ^ rs) * part_q + (qi ^ gray(rq))) * GROUP
            y = yi ^ gray(ry)
            for inner in range(GROUP):
                place = base + 2 * (xi ^ (inner % 2)) + (ci ^ (inner // 2))
                scr_e[y, pl.ds(place, 1)] = ref[at, inner][None]
            scr_r[y, pl.ds(base, GROUP)] = ref[at, GROUP : 2 * GROUP]
    cw = D // nb
    for y in range(nb):
        e_w[:, y * cw : (y + 1) * cw] = merged(scr_e[y])
        r_w[:, y * cw : (y + 1) * cw] = merged(scr_r[y])


def feed_rows(here, up, bias, e_w, r_w):
    hidden = dot(here, e_w[...]) + bias[...]
    k0 = 0.7978845608028654
    square = hidden * hidden
    tanh = jnp.tanh(k0 * hidden * (1.0 + 0.044715 * square))
    half = 0.5 * (1.0 + tanh)
    active = (hidden * half).astype(BF)
    slope = half + 0.5 * k0 * hidden * (1.0 - tanh * tanh) * (1.0 + 3 * 0.044715 * square)
    d_hidden = (dot_nt(up, r_w[...]) * slope).astype(BF)
    return active, d_hidden, dot(active, r_w[...]), dot_nt(d_hidden, e_w[...])


def feed_blocks(own, from_c, up, up_c, bias, e_w, r_w, start, outs):
    mx_keep, mx_send, ds_keep, ds_send, acts, dhs, eb = outs
    rows = own.shape[0]
    total = start
    for b, (here, upper) in enumerate(((own, up), (from_c, up_c))):
        active, d_hidden, mixed, d_second = feed_rows(here[...], upper[...], bias, e_w, r_w)
        acts[b * rows : (b + 1) * rows, :] = active
        dhs[b * rows : (b + 1) * rows, :] = d_hidden
        total = total + jnp.sum(d_hidden.astype(F32), 0, keepdims=True)
        if b == 0:
            mx_keep[...] = mixed
            ds_keep[...] = d_second
        else:
            mx_send[...] = mixed.astype(BF)
            ds_send[...] = d_second.astype(BF)
    eb[...] = total


def feed_near_body(slots, part_q, nb, own, from_c, up, up_c, *refs):
    n = len(slots)
    pieces, bias = refs[:n], refs[n]
    outs, (e_w, r_w, scr_e, scr_r) = refs[n + 1 : n + 8], refs[n + 8 :]
    feed_weights(slots, part_q, nb, pieces, scr_e, scr_r, e_w, r_w)
    start = jnp.zeros((1, UG), F32)
    feed_blocks(own, from_c, up, up_c, bias, e_w, r_w, start, outs)


def feed_far_body(own, from_c, up, up_c, bias, e_w, r_w, near_eb, *outs):
    feed_blocks(own, from_c, up, up_c, bias, e_w, r_w, near_eb[...], outs)


def feed_grad_body(count, part_q, nb, rw, n_left, n_right, *refs):
    left, right = refs[:n_left], refs[n_left : n_left + n_right]
    low, high, all_left, all_right, scr = refs[n_left + n_right :]
    si, qi, xi, ci, yi = places()
    cw = D // nb
    for parts, held in ((left, all_left), (right, all_right)):
        at = 0
        for part in parts:
            held[at : at + part.shape[0], :] = part[...]
            at += part.shape[0]
    for y in range(nb):
        scr[y] = dot_tn(all_left[...], all_right[:, y * cw : (y + 1) * cw])
    for ry in range(nb):
        to = low if ry < nb // 2 else high
        for rs in range(count):
            for rq in range(part_q):
                at = ((si ^ rs) * part_q + (qi ^ gray(rq))) * GROUP * rw
                part = scr[yi ^ gray(ry), pl.ds(pl.multiple_of(at, GROUP * rw), GROUP * rw), :]
                to[ry % (nb // 2), rs, rq] = part.reshape(GROUP, rw, cw).astype(BF)


def middle_back_body(
    cycle, ds_keep, from_c, from_x, upstream, middle, gain, weight, eb, d_middle, d_branch, keep, send, sums
):
    si, qi, xi, ci, yi = places()
    unit = FF // cycle
    parts = []
    for j in range(cycle // GROUP):
        part = eb[:, j * unit : (j + 1) * unit]
        for g in range(GROUP):
            parts.append(jnp.where(2 * xi + ci == g, part, jnp.zeros_like(part)))
    for j in range(FF // D):
        per = len(parts) * D // FF
        sums[4 + j : 5 + j, :] = jnp.concatenate(parts[j * per : (j + 1) * per], 1)
    d_second = ds_keep[...] + from_c[0].astype(F32) + from_x[...].astype(F32)
    xhat, spread = norm_parts(middle[...])
    up = upstream[...].astype(F32)
    total = up + norm_back(d_second, gain[...], xhat, spread)
    d_middle[...] = total
    low = total.astype(BF)
    d_branch[...] = low
    sums[0:1, :] = jnp.sum(low.astype(F32), 0, keepdims=True)
    sums[1:2, :] = jnp.sum(d_second * xhat, 0, keepdims=True)
    sums[2:3, :] = jnp.sum(d_second, 0, keepdims=True)
    sums[3:4, :] = jnp.sum(up, 0, keepdims=True)
    for rx, to in ((0, keep), (1, send)):
        for rc in range(2):
            group = 2 * (ci ^ rc) + (xi ^ rx)
            rows = weight[pl.ds(pl.multiple_of(group * HG, HG), HG), :]
            to[:, rc * HG : (rc + 1) * HG] = dot_nt(low, rows).astype(BF)


def output_grad_body(count, part_q, nb, rw, keep, from_x, from_ck, from_cx, d_branch, low, high, scr):
    si, qi, xi, ci, yi = places()
    cw = D // nb
    for ref, lanes, rx, rc in ((keep, 0, 0, 0), (from_x, 0, 1, 0), (from_ck, 1, 0, 1), (from_cx, 1, 1, 1)):
        group = 2 * (ci ^ rc) + (xi ^ rx)
        grad = dot_tn(ref[:, lanes * HG : (lanes + 1) * HG], d_branch[...])
        for y in range(nb):
            part = grad[:, y * cw : (y + 1) * cw].reshape(HG // rw, rw, cw)
            scr[y, pl.ds(group * (HG // rw), HG // rw)] = part
    for rc, to in ((0, low), (1, high)):
        for ry in range(nb):
            for rs in range(count):
                for rq in range(part_q):
                    base = ((si ^ rs) * part_q + (qi ^ gray(rq))) * GROUP
                    for rx in range(2):
                        place = base + 2 * (xi ^ rx) + (ci ^ rc)
                        to[ry, rs, rq, rx] = scr[yi ^ gray(ry), place].astype(BF)


def attend_back_body(
    count, part_q, block, lengths, keep, from_x, from_ck, from_cx, query, keys, values, att, lse,
    d_query, d_pair, scr_o, acc_k, acc_v,
):
    si, qi, xi, ci, unused = places()
    length = lengths[0, si]
    rows = GROUP * block
    for ref, lanes, rx, rc in ((keep, 0, 0, 0), (from_x, 0, 1, 0), (from_ck, 1, 0, 1), (from_cx, 1, 1, 1)):
        for r in range(count):
            at = (((si ^ r) * 2 + (xi ^ rx)) * 2 + (ci ^ rc)) * block
            at = pl.multiple_of(at, block)
            scr_o[pl.ds(at, block), :] = ref[
                r * block : (r + 1) * block, lanes * HG : (lanes + 1) * HG
            ]
    acc_k[...] = jnp.zeros_like(acc_k)
    acc_v[...] = jnp.zeros_like(acc_v)
    for i in range(count):
        span = slice(i * rows, (i + 1) * rows)
        width = (i + 1) * part_q * rows
        allowed = allowed_at(i, rows, width, part_q, length)
        d_out_all = scr_o[span, :]
        d_out_t = d_out_all.astype(F32).T
        d_queries = []
        for h in range(HEADS):
            q_here = query[h, span, :]
            k_here = keys[h, :width, :]
            d_out = d_out_all[:, h * HD : (h + 1) * HD]
            scores = dot_nt(k_here, q_here)
            logs = lse[i * HEADS + h : i * HEADS + h + 1, :]
            probs = jnp.where(allowed, jnp.exp(scores - logs), 0.0)
            d_probs = dot_nt(values[h, :width, :], d_out)
            delta = jnp.sum(
                d_out_t[h * HD : (h + 1) * HD, :] * att[h, :, span], 0, keepdims=True
            )
            d_scores = (probs * (d_probs - delta)).astype(BF)
            acc_v[h, :width, :] += dot(probs.astype(BF), d_out)
            acc_k[h, :width, :] += dot(d_scores, q_here)
            d_queries.append(dot_tn(k_here, d_scores) * SCALE)
        d_query[span, :] = jnp.concatenate(d_queries, 0).T.astype(BF)
    kind = d_pair.dtype
    for h in range(HEADS):
        d_pair[:, h * HD : (h + 1) * HD] = acc_k[h].astype(kind)
        d_pair[:, HG + h * HD : HG + (h + 1) * HD] = acc_v[h].astype(kind)


def normed_back_body(count, block, d_query, d_pair, weight, keep, send, first, scr):
    si, qi, xi, ci, yi = places()
    scr[:, :HG] = d_query[...]
    scr[:, HG : 2 * HG] = d_pair[:, :HG]
    scr[:, 2 * HG :] = jnp.where(ci == 0, d_pair[:, HG:], jnp.zeros_like(d_pair[:, HG:]))
    for rc in (1, 0):
        for rx in (1, 0):
            starts = [
                pl.multiple_of((((si ^ r) * 2 + (xi ^ rx)) * 2 + (ci ^ rc)) * block, block)
                for r in range(count)
            ]
            here = jnp.concatenate([scr[pl.ds(at, block), :] for at in starts], 0)
            out = dot_nt(here, weight[...])
            part = [d_pair[pl.ds(at, block), HG : 2 * HG] for at in starts]
            part = jnp.concatenate(part, 0)
            if rc == 1:
                send[rx, :, :D] = out.astype(BF)
                send[rx, :, D : D + HG] = part
                send[rx, :, D + HG :] = jnp.zeros((part.shape[0], WIDE - D - HG), BF)
            else:
                keep[rx] = out
                first[rx] = part


def normed_sum_body(keep, first, from_c, send, own):
    si, qi, xi, ci, yi = places()
    send[:, :D] = (keep[1] + from_c[1, :, :D].astype(F32)).astype(BF)
    send[:, D : D + HG] = jnp.where(ci == 1, first[1], from_c[1, :, D : D + HG])
    send[:, D + HG :] = from_c[1, :, D + HG :]
    own[...] = jnp.where(ci == 1, first[0], from_c[0, :, D : D + HG])


def mixed_body(count, block, middle, mx_keep, from_c, from_x, bias, *outs):
    for r in range(count):
        span = slice(r * block, (r + 1) * block)
        mixed = middle[span, :] + mx_keep[span, :] + from_c[0, span, :].astype(F32)
        mixed = mixed + from_x[span, :].astype(F32) + bias[...]
        outs[r][...] = mixed.astype(BF)


def stack_body(keep, from_c, out):
    out[0] = keep[1]
    out[1] = from_c[1]


def project_grad_body(count, part_q, rw, normed, d_query, d_pair, keep, send, sums, scr, scr_d):
    si, qi, xi, ci, yi = places()
    scr_d[:, :HG] = d_query[...]
    scr_d[:, HG : 2 * HG] = d_pair[:, :HG]
    scr_d[:, 2 * HG :] = jnp.where(ci == 0, d_pair[:, HG:], jnp.zeros_like(d_pair[:, HG:]))
    scr[...] = dot_tn(normed[...], scr_d[...])
    total = jnp.sum(scr_d[...].astype(F32), 0, keepdims=True)
    group = 2 * ci + xi
    q_sum = total[:, :HG]
    v_sum = total[:, 2 * HG :]
    zero = jnp.zeros_like(q_sum)
    sums[0:1, :] = jnp.concatenate([jnp.where(group == g, q_sum, zero) for g in range(GROUP)], 1)
    sums[1:2, :] = jnp.concatenate(
        [jnp.where(group == g, v_sum, zero) for g in range(2)] + [zero, zero], 1
    )
    for rc, to in ((0, keep), (1, send)):
        for rx in range(2):
            for rs in range(count):
                for rq in range(part_q):
                    at = ((si ^ rs) * part_q + (qi ^ gray(rq))) * GROUP + 2 * (xi ^ rx) + (ci ^ rc)
                    at = pl.multiple_of(at * rw, rw)
                    to[rx, rs, rq] = scr[pl.ds(at, rw), :].astype(BF)


def tokens_back_body(keep, from_c, from_x, tok, gain, d_middle, own, *refs):
    outs, sums = refs[:4], refs[4]
    si, qi, xi, ci, yi = places()
    block = tok.shape[1]
    g_sum = jnp.zeros((1, D), F32)
    s_sum = jnp.zeros((1, D), F32)
    for r in range(4):
        span = slice(r * block, (r + 1) * block)
        xhat, spread = norm_parts(tok[r][:, :D].astype(F32))
        d_normed = keep[0, span, :] + from_c[0, span, :D].astype(F32)
        d_normed = d_normed + from_x[span, :D].astype(F32)
        g_sum = g_sum + jnp.sum(d_normed * xhat, 0, keepdims=True)
        s_sum = s_sum + jnp.sum(d_normed, 0, keepdims=True)
        out = d_middle[span, :] + norm_back(d_normed, gain[...], xhat, spread)
        outs[r][:, :D] = out.astype(BF)
        mine, theirs = own[span, :], from_x[span, D : D + HG]
        outs[r][:, D : D + HG] = jnp.where(xi == 0, mine, theirs)
        outs[r][:, D + HG :] = jnp.where(xi == 0, theirs, mine)
    sums[0:1, :] = g_sum
    sums[1:2, :] = s_sum


def on_device(
    tokens,
    first_values,
    lengths,
    cotangent,
    first_gain,
    first_shift,
    query_weight,
    query_bias,
    key_weight,
    value_weight,
    value_bias,
    output_weight,
    output_bias,
    second_gain,
    second_shift,
    expand_weight,
    expand_bias,
    reduce_weight,
    reduce_bias,
):
    count = tokens.shape[1]
    block = tokens.shape[2]
    part_q = lax.axis_size("q")
    nb = lax.axis_size("y")
    cycle = count * part_q * GROUP
    own_rows = count * block
    seq_rows = GROUP * own_rows
    rw = D // cycle
    cw = D // nb
    si, qi, xi, ci, yi = places()

    steps = Steps()

    vectors = [
        first_gain,
        first_shift,
        query_bias,
        value_bias,
        output_bias,
        second_gain,
        second_shift,
        reduce_bias,
        expand_bias,
    ]
    width = 3 * cw + DV // nb
    payload = call(
        functools.partial(pack_rows_body, nb),
        [shape((rw, width + HG))],
        [pltpu.VMEM((rw, HG), F32)],
        query_weight,
        key_weight,
        value_weight,
        output_weight,
        *vectors,
        mib=60,
    )[0]
    by_q = jnp.concatenate([p for p, unused in gather_list(payload, "q")], 0)
    by_s = direct([by_q] * count, "s")

    blocks_y = cycle // nb // GROUP
    keep, send = call(
        functools.partial(pack_units_body, nb, blocks_y),
        [shape((2, rw, cw)), shape((2, rw, cw))],
        [],
        expand_weight,
        mib=60,
    )
    from_x = swap(send, "x", 1)
    from_c = swap(jnp.stack([pick(keep, ci ^ 1), pick(from_x, ci ^ 1)]), "c", 1)
    f_parts = [jnp.stack([pick(keep, ci), pick(from_x, ci)]), from_c, reduce_weight.reshape(GROUP, rw, cw)]

    marks = [(rs, rq) for rs in range(count) for rq in range(part_q)]
    n2 = len(marks)
    vec_rows = (3 * n2 + 15) // 16 * 16
    pack_shape = shape((2 * n2 * rw + vec_rows, 3 * HG))
    core_shape = shape((2 * n2 * rw + 2 * vec_rows, 3 * HG))
    both = jnp.concatenate([tokens[0], first_values[0]], -1)
    if nb == 2:
        half_shape = shape((n2 * rw + vec_rows, 3 * HG))
        keep, send, o_own = call(
            functools.partial(own_columns_body, nb, count),
            [half_shape, half_shape, shape((n2, rw, cw))],
            [pltpu.VMEM((vec_rows, 3 * HG), F32)],
            *by_s,
        )
        both = after(both, send, from_c)
    else:
        held = jnp.concatenate(by_s, 0)[:, :, :width]
        both = after(both, held, from_c)
    got = direct([pick(both, si ^ k) for k in range(count)], "s")
    if nb == 2:
        columns_x = swap(send, "x", 1)
        own = keep
        rows = call(both_rows_body, [shape((2, n2 * rw, 3 * HG))], [], own, columns_x)[0]
        ready = rows
    else:
        by_y = gather_list(held, "y")[1:]
        keep, send, o_both = call(
            functools.partial(pack_columns_body, nb, rw, count, [slots for unused, slots in by_y]),
            [pack_shape, pack_shape, shape((nb, n2, rw, cw))],
            [pltpu.VMEM((nb, n2, rw, width), BF), pltpu.VMEM((vec_rows, 3 * HG), F32)],
            *by_s,
            *[part for part, unused in by_y],
        )
        columns_x = swap(send, "x", 1)
        ready = send

    def with_first(parts, x):
        parts = jnp.stack(parts)
        first = parts[..., D:].reshape(parts.shape[:2] + (2, HG))
        first = lax.dynamic_index_in_dim(first, x, 2, False)
        blank = jnp.zeros(first.shape[:2] + (WIDE - D - HG,), BF)
        return jnp.concatenate([parts[..., :D], first, blank], -1)

    near = with_first(got[:2], xi ^ 1)
    steps.need(Step.tokens_near, near)
    tok_x_near = swap(near, "x", 1)
    got = list(after(tuple(got), ready, near))
    far = with_first(got[2:], xi ^ 1)
    tok = with_first(got, xi)
    tok_x_far = swap(far, "x", 1)
    tok_other = far
    if nb == 2:
        columns_y = swap(rows, "y", 1)
    steps.reach(Step.tokens, far)
    steps.reach(Step.columns_x, columns_x)
    steps.reach(Step.tokens_x, tok_x_far)

    f_piece = jnp.concatenate(after(tuple(f_parts), tok_other), 0)
    f_by_q = jnp.concatenate([p for p, unused in gather_list(f_piece, "q")], 0)
    f_by_q = f_by_q.reshape((part_q,) + f_piece.shape)
    steps.need(Step.feed_piece, f_by_q)
    f_both = steps.move(
        Step.feed_two, lambda tie: (swap(tie(f_by_q), "s", 2), swap(tie(f_by_q), "s", 1))
    )
    if nb == 2:
        columns_y = steps.before(Step.cores, columns_y)
        keep, send = call(own_cores_body, [core_shape, core_shape], [], own, columns_x, rows, columns_y)
    else:
        keep, send = call(
            functools.partial(pack_cores_body, vec_rows),
            [core_shape, core_shape],
            [],
            keep,
            steps.before(Step.cores, columns_x),
        )
    steps.reach(Step.cores, keep)

    def output_x(tie):
        if nb != 2:
            return jnp.stack([o_both, swap(tie(o_both), "x", 1)])
        return jnp.stack([o_own, swap(tie(o_own), "x", 1)])

    def output_y(tie):
        held = tie(o_x())
        return held if nb != 2 else jnp.stack([held, swap(held, "y", 1)], 1)

    o_x = steps.move(Step.output_x, output_x)
    o_all = steps.move(Step.output_wide, output_y)
    o_c = steps.move(Step.output_c, lambda tie: swap(tie(o_all()), "c", 1))
    qkv_pieces = [keep, swap(send, "c", 1)]
    qkv_slots = [marks]
    tok_c = steps.move(Step.tokens_c, lambda tie: swap(tie(tok), "c", 1))
    row = shape((1, D), F32)
    gain_one, shift_one, my_qbias, my_vbias, o_bias, gain_two, shift_two, r_bias, my_ebias = call(
        functools.partial(vectors_body, qkv_slots, part_q, rw, cycle),
        [row, row, shape((1, HG), F32), shape((1, HG), F32), row, row, row, row, shape((1, UG), F32)],
        [pltpu.VMEM((cycle, 8, 3 * HG), F32)],
        *qkv_pieces,
    )
    tok_x = [tok_x_near, tok_x_far]
    sources = [tok, *tok_x, tok_c(), *[swap(after(part, keep), "c", 1) for part in tok_x]]
    o_slots = qkv_slots
    f_three = steps.move(Step.feed_three, lambda tie: swap(tie(f_by_q), "s", 3))

    def cotangent_z(tie):
        parts = [pick(tie(cotangent[0]), si ^ k) for k in range(count)]
        steps.need(Step.cotangent_part, parts[1:])
        return direct(parts, "s")

    cot = steps.move(Step.cotangent, cotangent_z)

    heads = [shape((HEADS, seq_rows, HD))] * 3
    query, keys, values, normed, qkv_w = call(
        functools.partial(project_body, qkv_slots, count, part_q, block, rw),
        heads + [shape((seq_rows, D)), shape((D, 3 * HG))],
        [pltpu.VMEM((cycle, rw, 3 * HG), BF), pltpu.VMEM((seq_rows, HG), BF)],
        *sources,
        *qkv_pieces,
        steps.before(Step.project, gain_one),
        shift_one,
        my_qbias,
        my_vbias,
    )
    steps.reach(Step.project, query)

    def whole_keys(value):
        if part_q == 1:
            return value
        parts = gather(value.reshape(HEADS, count, GROUP * block, HD), "q")
        return jnp.moveaxis(parts, 0, 2).reshape(HEADS, part_q * seq_rows, HD)

    keys, values = whole_keys(keys), whole_keys(values)
    key_rows = keys.shape[1]
    pair_shape = shape((own_rows, 2 * HG))
    pieces, piece_slots = [], []

    def most_y(tie):
        held = tie(jnp.concatenate([f_by_q, *f_both()], 0))
        steps.need(Step.feed_part, held)
        return gather_list(held, "y")

    y_most = steps.move(Step.feed_most_y, most_y)
    att, lse, att_keep, att_send = call(
        functools.partial(attend_body, count, part_q, block),
        [
            shape((HEADS, HD, seq_rows), F32),
            shape((count * HEADS, GROUP * block), F32),
            pair_shape,
            pair_shape,
        ],
        [pltpu.VMEM((seq_rows, HG), BF)],
        lengths,
        steps.before(Step.attend, query),
        keys,
        values,
        smem=1,
    )
    steps.reach(Step.attend, att_send)
    att_x = swap(att_send, "x", 1)
    steps.reach(Step.attend_x, att_x)
    y_last = steps.move(Step.feed_three_y, lambda tie: gather_list(tie(f_three()), "y"))
    mask_tie = steps.at(Step.mask)
    upstream = call(
        functools.partial(mask_body, part_q, block),
        [shape((own_rows, D))],
        [],
        lengths,
        *after(tuple(cot()), *mask_tie),
        smem=1,
    )[0]
    up_x = steps.move(Step.upstream_x, lambda tie: swap(tie(upstream), "x", 1))
    steps.need(Step.upstream, upstream)
    att_rows = [att_keep, att_x, swap(att_keep, "c", 1), swap(att_x, "c", 1)]
    middle, second, o_w = call(
        functools.partial(output_body, o_slots, count, part_q, block, nb, rw),
        [shape((own_rows, D), F32), shape((own_rows, D)), shape((D, D))],
        [pltpu.VMEM((nb, cycle, rw, cw), BF)],
        tok,
        *att_rows,
        o_all(),
        o_c(),
        steps.before(Step.output, o_bias),
        gain_two,
        shift_two,
    )
    steps.reach(Step.output, second)

    second_x = swap(second, "x", 1)
    steps.reach(Step.second_x, second_x)
    second_c = swap(second, "c", 1)
    up_c = swap(upstream, "c", 1)
    for held, order in ((y_most(), (0, 2, 1)), (y_last(), (3,))):
        for part, ys in held:
            pieces.append(part.reshape((-1,) + f_piece.shape))
            piece_slots.append([(ry, rs, rq) for ry in ys for rs in order for rq in range(part_q)])
    half_keep = shape((2, own_rows, D), F32)
    one_keep, one_send = shape((own_rows, D), F32), shape((own_rows, D))
    outs = [one_keep, one_send, one_keep, one_send] + [shape((2 * own_rows, D))] * 2 + [shape((1, UG), F32)]
    weight_shape = (nb, cycle, rw, cw)
    mx_near, mx_send_near, ds_near, ds_send_near, acts_near, dhs_near, eb_near, e_w, r_w = call(
        functools.partial(feed_near_body, piece_slots, part_q, nb),
        outs + [shape((D, UG)), shape((UG, D))],
        [pltpu.VMEM(weight_shape, BF)] * 2,
        second,
        second_c,
        upstream,
        up_c,
        *pieces,
        steps.before(Step.feed, my_ebias),
    )
    steps.reach(Step.feed, eb_near)
    far = [second_x, swap(second_x, "c", 1), up_x(), swap(up_x(), "c", 1)]
    mx_far, mx_send_far, ds_far, ds_send_far, acts_far, dhs_far, eb_sum = call(
        feed_far_body,
        outs,
        [],
        *far,
        steps.before(Step.feed_far, my_ebias),
        e_w,
        r_w,
        eb_near,
    )
    ds_c = swap(jnp.stack([ds_send_near, ds_send_far]), "c", 1)
    xs, acts, dhs = [second, second_c] + far[:2], [acts_near, acts_far], [dhs_near, dhs_far]
    us = [upstream, up_c] + far[2:]
    grad_shape = shape((nb // 2, count, part_q, GROUP, rw, cw))

    def feed_grad(left, right):
        return call(
            functools.partial(feed_grad_body, count, part_q, nb, rw, len(left), len(right)),
            [grad_shape, grad_shape],
            [pltpu.VMEM((seq_rows, D), BF)] * 2 + [pltpu.VMEM((nb, D, cw), F32)],
            *left,
            *right,
            direct_in=True,
        )

    e_low, e_high = feed_grad(xs, dhs)
    ds_c = after(ds_c, e_low)
    ds_pay = (ds_far + ds_c[1].astype(F32)).astype(BF)
    ds_x = swap(ds_pay, "x", 1)
    steps.reach(Step.d_second_c, ds_pay)
    steps.reach(Step.d_second_x, ds_x)
    e_y = steps.move(Step.expand_y, lambda tie: swap(tie(e_high), "y", gray(nb // 2)))
    r_low, r_high = feed_grad(after(acts, ds_pay), us)
    mx_send = jnp.stack([mx_send_near, mx_send_far])
    steps.need(Step.reduce, r_low)
    mx_c = steps.move(Step.mixed_c, lambda tie: swap(tie(mx_send), "c", 1))
    d_middle, d_branch, d_keep, d_send, sums_two = call(
        functools.partial(middle_back_body, cycle),
        [shape((own_rows, D), F32), shape((own_rows, D)), pair_shape, pair_shape, shape((8, D), F32)],
        [],
        ds_near,
        ds_c,
        ds_x,
        upstream,
        middle,
        steps.before(Step.middle, gain_two),
        o_w,
        eb_sum,
    )
    steps.reach(Step.middle, d_send)
    d_x = swap(d_send, "x", 1)
    steps.reach(Step.d_attended_x, d_x)
    d_c = [swap(d_keep, "c", 1), swap(d_x, "c", 1)]
    steps.reach(Step.d_attended_c, d_c[1])
    d_rows = [d_keep, d_x] + d_c

    def expand_z(tie):
        low, got = after((e_low, e_y()), *tie.values)
        part = scatter_slots(low, None, "y", got)
        part = [part[0]] + [part[k].astype(BF) for k in range(1, count)]
        steps.need(Step.expand_part, part[1:])
        return direct(part, "s")

    e_z = steps.move(Step.expand_z, expand_z)
    r_y = steps.move(Step.reduce_y, lambda tie: swap(tie(r_high), "y", gray(nb // 2)))

    def mixed_step(tie):
        pay = tie((mx_far + mx_c()[1].astype(F32)).astype(BF))
        steps.need(Step.mixed_part, pay)
        return swap(pay, "x", 1)

    mx_x = steps.move(Step.mixed_x, mixed_step)
    o_shape = shape((nb, count, part_q, 2, rw, cw))

    def output_grad(tie):
        low, high = call(
            functools.partial(output_grad_body, count, part_q, nb, rw),
            [o_shape, o_shape],
            [pltpu.VMEM((nb, cycle, rw, cw), F32)],
            *att_rows,
            tie(d_branch),
        )
        return low, high, swap(high[None], "c", 1)

    o_c_sum = steps.move(Step.output_grad, output_grad)

    d_query, d_pair = call(
        functools.partial(attend_back_body, count, part_q, block),
        [shape((seq_rows, HG)), shape((key_rows, 2 * HG), BF if part_q == 1 else F32)],
        [pltpu.VMEM((seq_rows, HG), BF)] + [pltpu.VMEM((HEADS, key_rows, HD), F32)] * 2,
        lengths,
        *d_rows,
        query,
        keys,
        values,
        steps.before(Step.attend_back, att),
        lse,
        smem=1,
        direct_in=True,
    )
    steps.reach(Step.attend_back, d_query)

    def reduce_z(tie):
        low, got = after((r_low, r_y()), *tie.values)
        part = scatter_slots(low, None, "y", got)
        part = [part[0]] + [part[k].astype(BF) for k in range(1, count)]
        steps.need(Step.reduce_part, part[1:])
        return direct(part, "s")

    r_z = steps.move(Step.reduce_z, reduce_z)

    def mixed_z(tie):
        parts = call(
            functools.partial(mixed_body, count, block),
            [shape((block, D))] * count,
            [],
            middle,
            mx_near,
            mx_c(),
            mx_x(),
            tie(r_bias),
        )
        steps.need(Step.mixed_rows, parts[1:])
        return direct(parts, "s")

    mixed = steps.move(Step.mixed_z, mixed_z)
    qkv_w = steps.before(Step.normed_back, qkv_w)
    if part_q > 1:
        parts = d_pair.reshape(count, part_q, GROUP * block, 2 * HG).swapaxes(0, 1)
        d_pair = scatter_sum(relative(parts, "q"), "q").reshape(seq_rows, 2 * HG).astype(BF)
    dn_keep, dn_send, first_keep = call(
        functools.partial(normed_back_body, count, block),
        [half_keep, shape((2, own_rows, WIDE)), shape((2, own_rows, HG))],
        [pltpu.VMEM((seq_rows, 3 * HG), BF)],
        d_query,
        d_pair,
        qkv_w,
        direct_in=True,
    )
    steps.reach(Step.normed_back, dn_keep)
    dn_c = swap(dn_send, "c", 1)
    dn_pay, first_own = call(
        normed_sum_body,
        [shape((own_rows, WIDE)), shape((own_rows, HG))],
        [],
        dn_keep,
        first_keep,
        dn_c,
    )
    steps.reach(Step.d_normed_c, dn_pay)
    dn_x = swap(dn_pay, "x", 1)
    normed = after(normed, dn_pay)
    p_shape = shape((2, count, part_q, rw, 3 * HG))
    p_keep, p_send, sums_qv = call(
        functools.partial(project_grad_body, count, part_q, rw),
        [p_shape, p_shape, shape((2, D), F32)],
        [pltpu.VMEM((D, 3 * HG), F32), pltpu.VMEM((seq_rows, 3 * HG), BF)],
        steps.before(Step.project_grad, normed),
        d_query,
        d_pair,
    )
    steps.reach(Step.project_grad, p_keep)
    steps.reach(Step.d_normed_x, dn_x)
    p_from_c = swap(p_send, "c", 1)
    p_pay = call(stack_body, [shape((2, count, part_q, rw, 3 * HG))], [], p_keep, p_from_c)[0]
    steps.need(Step.columns_part, p_pay)
    p_from_x = steps.move(Step.columns_grad_x, lambda tie: swap(tie(p_pay), "x", 1))
    *gt, sums_one = call(
        tokens_back_body,
        [shape((block, D + DV))] * count + [shape((2, D), F32)],
        [],
        dn_keep,
        dn_c,
        dn_x,
        tok,
        steps.before(Step.tokens_back, gain_one),
        d_middle,
        first_own,
    )
    steps.reach(Step.tokens_back, gt[0])
    home_cols = 2 * cw + DV // nb
    n_rows = count * part_q
    flat = (steps.before(Step.columns_home, p_keep[0]), p_from_c[0], p_from_x()[0], p_from_x()[1])
    y_low, y_high = call(
        functools.partial(columns_home_body, nb, n_rows),
        [shape((nb // 2, n_rows, rw, home_cols), F32), shape((nb // 2, n_rows, rw, home_cols))],
        [pltpu.VMEM((nb, rw, home_cols), F32)],
        *[v.reshape(-1, rw, 3 * HG) for v in flat],
    )
    steps.reach(Step.columns_home, y_high)
    steps.need(Step.columns_sent, y_high)
    gt = steps.move(Step.tokens_z, lambda tie: direct(tie(gt), "s"))()
    steps.reach(Step.tokens_z, gt[1])
    back = in_place(gt, "s")[None]
    grad_tokens, grad_first = back[..., :D], back[..., D:]

    def sum_q(value):
        return scatter_sum(value, "q")

    o_low, o_high, o_got = o_c_sum()
    o_part = steps.move(
        Step.output_y, lambda tie: scatter_sum(scatter_slots(tie(o_low)[None], None, "c", o_got), "y")
    )()
    o_part = jnp.moveaxis(o_part, 2, 0)
    o_part = scatter_slots(o_part[:1], o_part[1:], "x")
    qkv_part = scatter_slots(y_low, y_high, "y").reshape(count, part_q, rw, home_cols)
    home_pay = jnp.concatenate([steps.before(Step.home, qkv_part), o_part], -1)
    steps.reach(Step.home, home_pay)
    home = sum_q(direct_sum(home_pay, "s"))
    q_home, k_home, v_home = home[:, :cw], home[:, cw : 2 * cw], home[:, 2 * cw : home_cols]
    o_home = home[:, home_cols:]
    mixed_out = in_place(after(tuple(mixed()), *steps.at(Step.mixed_out)), "s")[None]

    def to_group(part):
        part = part.astype(BF)
        keep = lax.dynamic_index_in_dim(part, ci, 1, keepdims=False)
        got = swap(lax.dynamic_index_in_dim(part, ci ^ 1, 1, keepdims=False), "c", 1)
        both = jnp.stack([keep, got], 1)
        return pick(both, xi), swap(pick(both, xi ^ 1), "x", 1)

    e_z = after(tuple(e_z()), *steps.at(Step.expand_home))
    e_home = sum_q(sum(part.astype(F32) for part in e_z))
    e_home = call(
        functools.partial(units_home_body, blocks_y),
        [shape((rw, FF // nb), F32)],
        [],
        *to_group(e_home.reshape(2, 2, rw, cw)),
    )[0]
    r_z = after(tuple(r_z()), *steps.at(Step.reduce_home))
    r_home = sum_q(sum(part.astype(F32) for part in r_z)).reshape(GROUP * rw, cw)

    sums = after(jnp.concatenate([sums_one, sums_qv, sums_two], 0), *steps.at(Step.sums))
    for axis in ("c", "x", "y", "q"):
        sums = whole_sum(sums, axis)
    sums = sum(direct([sums] * count, "s"))
    place = ((si * part_q + qi) * 2 + xi) * 2 + ci
    part = lax.dynamic_slice_in_dim(sums[:8], place * rw, rw, 1)
    vb_home = lax.dynamic_slice_in_dim(sums[3], place * (DV // cycle), DV // cycle, 0)
    eb_home = pick(sums[8:].reshape(cycle, -1), place)
    return (
        mixed_out,
        grad_tokens,
        grad_first,
        part[0],
        part[1],
        q_home,
        part[2],
        k_home,
        v_home,
        vb_home,
        o_home,
        part[4],
        part[5],
        part[6],
        e_home,
        eb_home,
        r_home,
        part[7],
    )


def solution(mesh):
    cycle, nb = mesh.devices.shape
    sequences = 4
    fine = Mesh(
        mesh.devices.reshape(sequences, cycle // (sequences * GROUP), 2, 2, nb),
        ("s", "q", "x", "c", "y"),
    )
    seq = ("s", "q", "x", "c")
    rows = P("y", None, seq, None)
    matrix = P(seq, "y")
    vector = P(seq)
    in_specs = (
        rows,
        rows,
        P("y", None),
        rows,
        vector,
        vector,
        matrix,
        vector,
        matrix,
        matrix,
        vector,
        matrix,
        vector,
        vector,
        vector,
        matrix,
        vector,
        matrix,
        vector,
    )
    out_specs = (
        rows,
        rows,
        rows,
        vector,
        vector,
        matrix,
        vector,
        matrix,
        matrix,
        vector,
        matrix,
        vector,
        vector,
        vector,
        matrix,
        vector,
        matrix,
        vector,
    )
    return jax.shard_map(
        on_device, mesh=fine, in_specs=in_specs, out_specs=out_specs, check_vma=False
    )
```
